32 devices in a mesh: dp: 8 (over z, x), tensor: 4 (over y, core).
Axes of the slice: x: 2, y: 2, z: 4, core: 2. Of those that a mesh axis runs over, the one named last changes fastest.
Arguments:
- tokens: bfloat16 [2048, 2048], P(('dp', 'tensor')), may hold values from -6 to 6
- grad_out: bfloat16 [2048, 2048], P(('dp', 'tensor')), may hold values from -6 to 6
- lengths: int32 [8, 3], P('dp'), may hold values from 1 to 254, as said below
- gain_attn: bfloat16 [2048], P('dp'), may hold values from 0.5 to 1.5
- gain_ffn: bfloat16 [2048], P('dp'), may hold values from 0.5 to 1.5
- w_query: bfloat16 [2048, 2048], P('dp', 'tensor'), may hold values from -0.125 to 0.125
- w_keyval: bfloat16 [2048, 512], P('dp'), may hold values from -0.125 to 0.125
- w_out: bfloat16 [2048, 2048], P('dp', 'tensor'), may hold values from -1 to 1
- w_gate: bfloat16 [2048, 16384], P('dp', 'tensor'), may hold values from -0.125 to 0.125
- w_up: bfloat16 [2048, 16384], P('dp', 'tensor'), may hold values from -0.125 to 0.125
- w_down: bfloat16 [2048, 16384], P('dp', 'tensor'), may hold values from -0.046875 to 0.046875
Outputs:
- block_out: bfloat16 [2048, 2048], P(('dp', 'tensor'))
- grad_tokens: float32 [2048, 2048], P(('dp', 'tensor'))
- grad_gain_attn: float32 [2048], P('dp')
- grad_gain_ffn: float32 [2048], P('dp')
- grad_w_query: float32 [2048, 2048], P('dp', 'tensor')
- grad_w_keyval: float32 [2048, 512], P('dp')
- grad_w_out: float32 [2048, 2048], P('dp', 'tensor')
- grad_w_gate: float32 [2048, 16384], P('dp', 'tensor')
- grad_w_up: float32 [2048, 16384], P('dp', 'tensor')
- grad_w_down: float32 [2048, 16384], P('dp', 'tensor')
The draws below stay inside these ranges and needn't reach their ends.
Inputs may be any that keep to these rules, and one draw needn't show every extreme that they name: Each row of lengths holds the lengths of the 3 sequences of one group in order and sums to 256; in every group one sequence, at a position drawn from the seed, begins before place 64 - 1 and ends after place 3 * 64.
All inputs are finite; a program needn't handle non-finite values.
Results may differ from the reference program's by a relative error of at most 0.024.
Values may be sent and summed in bfloat16 or wider, within the bound.
A program may use at most 320 MiB of HBM per device.

```python
import jax
import jax.numpy as jnp
from jax import lax

D = 2048
H = 8
HD = 256
FF = 16384
WINDOW = 2048
TOK_GRP = 256
TDEV = 64
GROUPS = 8
TOKENS = 2048


def draw_lengths(key, part):
    key = jax.random.fold_in(key, 7)
    short_key, slot_key, pick_key = jax.random.split(key, 3)
    shorts = jax.random.randint(short_key, (GROUPS, 2), 1, TDEV // 2, dtype=jnp.int32)
    chosen_group = jax.random.randint(pick_key, (), 0, GROUPS, dtype=jnp.int32)
    group_place = jnp.arange(GROUPS, dtype=jnp.int32)
    shorts = jnp.where((group_place == chosen_group)[:, None], jnp.ones_like(shorts), shorts)
    longest = TOK_GRP - shorts[:, 0] - shorts[:, 1]
    slot_pick = jax.random.randint(slot_key, (GROUPS,), 0, 3, dtype=jnp.int32)
    first_len = jnp.where(slot_pick == 0, longest, shorts[:, 0])
    second_len = jnp.where(slot_pick == 0, shorts[:, 0], jnp.where(slot_pick == 1, longest, shorts[:, 1]))
    third_len = jnp.where(slot_pick == 2, longest, shorts[:, 1])
    return jnp.stack([first_len, second_len, third_len], axis=1).astype(jnp.int32)


def block_scale(own_key, dims, shards, least, largest):
    gain, own = 1.0, jax.random.fold_in(own_key, 6)
    for position, shards_of in shards:
        draws = jnp.exp(jax.random.uniform(jax.random.fold_in(own, position), (shards_of,), jnp.float32, least / len(shards), largest / len(shards)))
        gain = gain * jnp.repeat(draws, dims[position] // shards_of).reshape([-1 if axis == position else 1 for axis in range(len(dims))])
    return gain


def centred(own_key, dims, width, limit, pieces=(), kind=jnp.bfloat16):
    array = jax.random.normal(own_key, dims, jnp.float32) * width
    if len(pieces) > 0:
        array = block_scale(own_key, dims, pieces, -0.22, 0.18) * array
    return jnp.clip(array, min=-limit, max=limit).astype(kind)


def setup_inputs(seed: int = 0) -> dict:
    key_of = jax.random.split(jax.random.key(seed), 12)
    return {
        "tokens": centred(key_of[0], (TOKENS, D), 1.0, 6.0, ((0, 32),)),
        "grad_out": centred(key_of[1], (TOKENS, D), 1.0, 6.0, ((0, 32),)),
        "lengths": draw_lengths(jax.random.fold_in(key_of[11], 71), 0),
        "gain_attn": jnp.clip(1.0 + 0.1 * jax.random.normal(key_of[3], (D,), jnp.float32), 0.5, 1.5).astype(jnp.bfloat16),
        "gain_ffn": jnp.clip(1.0 + 0.1 * jax.random.normal(key_of[4], (D,), jnp.float32), 0.5, 1.5).astype(jnp.bfloat16),
        "w_query": centred(key_of[5], (D, H * HD), D ** -0.5, 0.125, ((0, 8), (1, 4))),
        "w_keyval": centred(key_of[6], (D, 2 * HD), D ** -0.5, 0.125, ((0, 8),)),
        "w_out": centred(key_of[7], (D, H * HD), (max(H * HD // 64, 1)) ** -0.5, 1.0, ((0, 8), (1, 4))),
        "w_gate": centred(key_of[8], (D, FF), D ** -0.5, 0.125, ((0, 8), (1, 4))),
        "w_up": centred(key_of[9], (D, FF), D ** -0.5, 0.125, ((0, 8), (1, 4))),
        "w_down": centred(key_of[10], (D, FF), FF ** -0.5, 0.046875, ((0, 8), (1, 4))),
    }


@jax.custom_vjp
def low(v):
    return lax.optimization_barrier(v.astype(jnp.bfloat16)).astype(jnp.float32)

@jax.custom_vjp
def low_back(v):
    return v

def low_keep(v):
    return (low(v), None)

def low_pass(kept, grad):
    return (grad,)

def back_keep(v):
    return (v, None)

def back_low(kept, grad):
    return (low(grad),)
low.defvjp(low_keep, low_pass)
low_back.defvjp(back_keep, back_low)
norm_eps = 1e-06
masked_score = -1e+30
full_precision = lax.Precision.HIGHEST

def norm_rows(values_in, gain_vec):
    inverse_root = lax.rsqrt(lax.optimization_barrier(jnp.mean(values_in * values_in, axis=-1, keepdims=True)) + norm_eps)
    return values_in * inverse_root * gain_vec

def gelu_mix(gate_act, up_act):
    return jax.nn.gelu(gate_act, approximate=True) * up_act

def segment_ids(length_row, row_count):
    seq_ends = jnp.cumsum(length_row)
    positions = jnp.arange(row_count, dtype=jnp.int32)
    return lax.optimization_barrier(jnp.sum((positions[:, None] >= seq_ends[None, :]).astype(jnp.int32), axis=1))

def window_allowed(segment, block_start, block_rows):
    row_count = segment.shape[0]
    query_place = block_start + jnp.arange(block_rows, dtype=jnp.int32)
    key_place = jnp.arange(row_count, dtype=jnp.int32)
    block_segment = lax.dynamic_slice_in_dim(segment, block_start, block_rows, 0)
    distance = query_place[:, None] - key_place[None, :]
    return (block_segment[:, None] == segment[None, :]) & (distance >= 0) & (distance < WINDOW)

def attend(queries, keyval, segment):
    row_count = queries.shape[0]
    query_heads = queries.reshape(row_count, H, HD)
    key_part = keyval[:, :HD]
    value_part = keyval[:, HD:]
    block_rows = 512 if row_count % 512 == 0 else row_count
    factor = HD ** (-0.5)

    def one_block(block_index):
        block_start = (block_index * block_rows).astype(jnp.int32)
        query_block = lax.dynamic_slice_in_dim(query_heads, block_start, block_rows, 0)
        allowed = window_allowed(segment, block_start, block_rows)
        scores = jnp.einsum('qhd,kd->hqk', query_block, key_part, precision=full_precision) * factor
        scores = jnp.where(allowed[None], low_back(scores), masked_score)
        peak_score = lax.optimization_barrier(jnp.max(scores, axis=-1, keepdims=True))
        weights = jnp.exp(scores - peak_score)
        probabilities = low(weights / lax.optimization_barrier(jnp.sum(weights, axis=-1, keepdims=True)))
        return jnp.einsum('hqk,kd->qhd', probabilities, value_part, precision=full_precision)
    contexts = lax.map(jax.checkpoint(one_block), jnp.arange(row_count // block_rows, dtype=jnp.int32))
    return contexts.reshape(row_count, H * HD)

def forward(inputs, gain_attn, gain_ffn, w_query, w_keyval, w_out, w_gate, w_up, w_down, segment):
    normed_attn = low(norm_rows(inputs, gain_attn))
    queries = low(low_back(jnp.dot(normed_attn, w_query, precision=full_precision)))
    keyval = low(low_back(jnp.dot(normed_attn, w_keyval, precision=full_precision)))
    context = low(low_back(attend(queries, keyval, segment)))
    branch = low_back(jnp.dot(context, w_out.T, precision=full_precision))
    middle = inputs + branch
    normed_ffn = low(norm_rows(middle, gain_ffn))
    gate_act = low_back(jnp.dot(normed_ffn, w_gate, precision=full_precision))
    up_act = low_back(jnp.dot(normed_ffn, w_up, precision=full_precision))
    hidden = low(gelu_mix(gate_act, up_act))
    return middle + low_back(jnp.dot(hidden, w_down.T, precision=full_precision))

def reference(tokens, grad_out, lengths, gain_attn, gain_ffn, w_query, w_keyval, w_out, w_gate, w_up, w_down):
    params = tuple((param_arr.astype(jnp.float32) for param_arr in (gain_attn, gain_ffn, w_query, w_keyval, w_out, w_gate, w_up, w_down)))
    token_groups = tokens.astype(jnp.float32).reshape(GROUPS, TOK_GRP, D)
    cot_groups = grad_out.astype(jnp.float32).reshape(GROUPS, TOK_GRP, D)

    def group_step(carried, group_item):
        inputs, cotangent, length_row = group_item
        segment = segment_ids(length_row, TOK_GRP)

        def local_forward(inputs_in, *param_list):
            return forward(inputs_in, *param_list, segment)
        outputs, pullback = jax.vjp(local_forward, inputs, *params)
        gradients = pullback(cotangent)
        carried = tuple((old_sum + new_term for old_sum, new_term in zip(carried, gradients[1:])))
        return (carried, (outputs.astype(jnp.bfloat16), gradients[0]))
    zero_sums = tuple((jnp.zeros(param_arr.shape, jnp.float32) for param_arr in params))
    gradient_sums, (block_out, grad_tokens) = lax.scan(group_step, zero_sums, (token_groups, cot_groups, lengths))
    return (block_out.reshape(TOKENS, D), grad_tokens.reshape(TOKENS, D), gradient_sums[0], gradient_sums[1], gradient_sums[2], gradient_sums[3], gradient_sums[4], gradient_sums[5], gradient_sums[6], gradient_sums[7])
```

```python
import functools

import jax
import jax.numpy as jnp
from jax import lax
from jax.experimental import pallas as pl
from jax.experimental.pallas import tpu as pltpu
from jax.sharding import PartitionSpec as P

HD = 256
WINDOW = 2048
NORM_EPS = 1e-06
MASKED = -1e30
BF16, F32 = jnp.bfloat16, jnp.float32
MESH = pl.DeviceIdType.MESH
ANY = pl.BlockSpec(memory_space=pl.ANY)
VMEM = pl.BlockSpec(memory_space=pltpu.VMEM)
SMEM = pl.BlockSpec(memory_space=pltpu.SMEM)
MIB = 1 << 20


def dot_nn(a, b):
    return lax.dot_general(a, b, (((1,), (0,)), ((), ())), preferred_element_type=F32)


def dot_nt(a, b):
    return lax.dot_general(a, b, (((1,), (1,)), ((), ())), preferred_element_type=F32)


def dot_tn(a, b):
    return lax.dot_general(a, b, (((0,), (0,)), ((), ())), preferred_element_type=F32)


class Net:
    def __init__(self, n, send, recv):
        self.n, self.nz = n, n // 2
        self.send, self.recv, self.used = send, recv, 0
        self.d = lax.axis_index("dp")
        self.t = lax.axis_index("tensor")
        self.z = self.d // 2
        self.x = self.d % 2
        self.dx = self.d + 1 - 2 * self.x
        self.ty = (self.t + 2) % 4
        self.tc = self.t + 1 - 2 * (self.t % 2)
        self.tcy = (self.tc + 2) % 4
        self.ends = []

    def take(self, count):
        first = self.used
        self.used += count
        return first

    def dp(self, other):
        return (other, self.t)

    def tensor(self, other):
        return (self.d, other)

    def make(self, src, dst, k, device):
        return pltpu.make_async_remote_copy(
            src_ref=src,
            dst_ref=dst,
            send_sem=self.send.at[k],
            recv_sem=self.recv.at[k],
            device_id=device,
            device_id_type=MESH,
        )

    def start(self, src, dst, k, device):
        self.make(src, dst, k, device).start()

    def landed(self, ref, k):
        self.make(ref, ref, k, self.tensor(self.tc)).wait_recv()

    def sent(self, ref, k):
        self.make(ref, ref, k, self.tensor(self.tc)).wait_send()

    def greet(self):
        barrier = pltpu.get_barrier_semaphore()

        @pl.loop(1, self.n)
        def _(m):
            pl.semaphore_signal(
                barrier, inc=1, device_id=self.dp((self.d + m) % self.n), device_id_type=MESH
            )

        for other in (self.ty, self.tc):
            pl.semaphore_signal(
                barrier, inc=1, device_id=self.tensor(other), device_id_type=MESH
            )
        pl.semaphore_wait(barrier, self.n + 1)

    def finish(self):
        for end in self.ends:
            end()


class TensorGather:
    def __init__(self, net, at):
        self.net, self.at, self.k = net, at, net.take(3)
        net.ends.append(self.end)

    def begin(self):
        net = self.net
        net.start(self.at(net.t), self.at(net.t), self.k, net.tensor(net.ty))
        net.start(self.at(net.t), self.at(net.t), self.k + 1, net.tensor(net.tc))

    def rest(self):
        net = self.net
        net.landed(self.at(net.ty), self.k)
        net.start(self.at(net.ty), self.at(net.ty), self.k + 2, net.tensor(net.tc))
        net.landed(self.at(net.tc), self.k + 1)
        net.landed(self.at(net.tcy), self.k + 2)

    def end(self):
        for i in range(3):
            self.net.sent(self.at(0), self.k + i)


class TensorScatter:
    def __init__(self, net, part, cl, yl):
        self.net, self.part, self.cl, self.yl, self.k = net, part, cl, yl, net.take(3)
        net.ends.append(self.end)

    def begin(self):
        net = self.net
        net.start(self.part.at[net.tcy], self.cl.at[1], self.k + 1, net.tensor(net.tc))
        net.start(self.part.at[net.tc], self.cl.at[0], self.k, net.tensor(net.tc))

    def rest(self):
        net = self.net
        net.landed(self.cl.at[1], self.k + 1)
        pair = self.part[net.ty].astype(F32) + self.cl[1].astype(F32)
        self.part[net.ty] = pair.astype(self.part.dtype)
        net.start(self.part.at[net.ty], self.yl, self.k + 2, net.tensor(net.ty))
        net.landed(self.cl.at[0], self.k)
        own = self.part[net.t].astype(F32) + self.cl[0].astype(F32)
        net.landed(self.yl, self.k + 2)
        return own + self.yl[...].astype(F32)

    def end(self):
        for i in range(3):
            self.net.sent(self.yl, self.k + i)


class Spread:
    def __init__(self, net, bufs, block, wide=False):
        self.net, self.bufs, self.block, self.wide = net, bufs, block, wide
        nz, n = net.nz, net.n
        self.zk = [net.take(2 * nz) for _ in bufs]
        self.xk = [net.take(nz) for _ in bufs]
        if wide:
            self.yk = [net.take(n) for _ in bufs]
            self.ck = [net.take(n) for _ in bufs]
        net.ends.append(self.end)

    def line(self, j, src, zb, right):
        net = self.net
        where = self.block(self.bufs[j], 2 * zb + net.x)
        if right:
            net.start(src, where, self.zk[j] + zb, net.dp(net.d + 2))
        else:
            net.start(src, where, self.zk[j] + net.nz + zb, net.dp(net.d - 2))

    def over_x(self, j, src, zb):
        net = self.net
        where = self.block(self.bufs[j], 2 * zb + net.x)
        net.start(src, where, self.xk[j] + zb, net.dp(net.dx))

    def over_y(self, j, src, idx):
        net = self.net
        net.start(src, self.bufs[j].at[1, idx], self.yk[j] + idx, net.tensor(net.ty))

    def begin(self, own=None):
        net = self.net
        own = own or [self.block(b, net.d) for b in self.bufs]
        for j, src in enumerate(own):

            @pl.when(net.z < net.nz - 1)
            def _():
                self.line(j, src, net.z, True)

            @pl.when(net.z > 0)
            def _():
                self.line(j, src, net.z, False)

            self.over_x(j, src, net.z)
            if self.wide:
                self.over_y(j, src, net.d)

    def hop(self, h):
        net = self.net
        nz = net.nz
        for j, buf in enumerate(self.bufs):

            @pl.when(net.z - h >= 0)
            def _():
                zb = net.z - h
                here = self.block(buf, 2 * zb + net.x)
                net.landed(here, self.zk[j] + zb)

                @pl.when(net.z < nz - 1)
                def _():
                    self.line(j, here, zb, True)

                self.over_x(j, here, zb)
                if self.wide:
                    self.over_y(j, here, 2 * zb + net.x)

            @pl.when(net.z + h <= nz - 1)
            def _():
                zb = net.z + h
                here = self.block(buf, 2 * zb + net.x)
                net.landed(here, self.zk[j] + nz + zb)

                @pl.when(net.z > 0)
                def _():
                    self.line(j, here, zb, False)

                self.over_x(j, here, zb)
                if self.wide:
                    self.over_y(j, here, 2 * zb + net.x)

    def hops(self):
        @pl.loop(1, self.net.nz)
        def _(h):
            self.hop(h)

    def cross(self):
        net = self.net

        @pl.loop(0, net.nz)
        def _(k):
            zb = (net.z + k) % net.nz
            idx = 2 * zb + 1 - net.x
            for j, buf in enumerate(self.bufs):
                net.landed(self.block(buf, idx), self.xk[j] + zb)
                if self.wide:
                    self.over_y(j, self.block(buf, idx), idx)

    def over(self):
        net = self.net

        @pl.loop(0, net.n)
        def _(k):
            idx = (2 * net.z + net.x + k) % net.n
            for j, buf in enumerate(self.bufs):
                net.landed(buf.at[1, idx], self.yk[j] + idx)
                net.start(
                    buf.at[pl.ds(0, 2), idx],
                    buf.at[pl.ds(2, 2), idx],
                    self.ck[j] + idx,
                    net.tensor(net.tc),
                )

    def done(self):
        net = self.net

        @pl.loop(0, net.n)
        def _(k):
            idx = (2 * net.z + net.x + k) % net.n
            for j, buf in enumerate(self.bufs):
                net.landed(buf.at[pl.ds(2, 2), idx], self.ck[j] + idx)

    def end(self):
        net = self.net

        @pl.loop(0, net.nz)
        def _(zb):
            for j, buf in enumerate(self.bufs):
                some = self.block(buf, 0)

                @pl.when((zb <= net.z) & (net.z < net.nz - 1))
                def _():
                    net.sent(some, self.zk[j] + zb)

                @pl.when((zb >= net.z) & (net.z > 0))
                def _():
                    net.sent(some, self.zk[j] + net.nz + zb)

                net.sent(some, self.xk[j] + zb)

        if self.wide:

            @pl.loop(0, net.n)
            def _(idx):
                for j, buf in enumerate(self.bufs):
                    net.sent(buf.at[0, 0], self.yk[j] + idx)
                    net.sent(buf.at[pl.ds(0, 2), 0], self.ck[j] + idx)


class Deal:
    def __init__(self, net, src, dst):
        self.net, self.src, self.dst, self.k = net, src, dst, net.take(net.n)
        net.ends.append(self.end)

    def begin(self):
        net = self.net

        @pl.loop(1, net.n)
        def _(m):
            to = (net.d + m) % net.n
            net.start(self.src(to), self.dst(net.d), self.k + m, net.dp(to))

    def done(self):
        net = self.net

        @pl.loop(1, net.n)
        def _(m):
            net.landed(self.dst((net.d - m + net.n) % net.n), self.k + m)

    def end(self):
        net = self.net

        @pl.loop(1, net.n)
        def _(m):
            net.sent(self.src(0), self.k + m)


class Scatter:
    def __init__(self, net, at, xl, rl, ll, mem):
        self.net, self.at, self.xl, self.rl, self.ll, self.mem = net, at, xl, rl, ll, mem
        self.xk, self.rk, self.lk = net.take(net.nz), net.take(net.nz), net.take(net.nz)
        net.ends.append(self.end)

    def order(self, k):
        nz = self.net.nz
        odd = k % 2
        return odd * (k // 2) + (1 - odd) * (nz - 1 - k // 2)

    def send_x(self, zb):
        net = self.net
        net.start(self.at(2 * zb + 1 - net.x), self.xl.at[zb], self.xk + zb, net.dp(net.dx))

    def begin(self):
        @pl.loop(0, self.net.nz)
        def _(k):
            self.send_x(self.order(k))

    def add(self, block, other):
        mem = self.mem
        mem.put(block, (mem.get(block).astype(F32) + mem.get(other).astype(F32)).astype(BF16))

    def meet(self, zb):
        net = self.net
        net.landed(self.xl.at[zb], self.xk + zb)
        self.add(self.at(2 * zb + net.x), self.xl.at[zb])

    def lines(self):
        net = self.net
        nz = net.nz

        @pl.loop(0, nz - 1)
        def _(k):
            far = nz - 1 - k

            @pl.when(far > net.z)
            def _():
                self.meet(far)
                here = self.at(2 * far + net.x)

                @pl.when(net.z > 0)
                def _():
                    net.landed(self.rl.at[far], self.rk + far)
                    self.add(here, self.rl.at[far])

                net.start(here, self.rl.at[far], self.rk + far, net.dp(net.d + 2))

            @pl.when(k < net.z)
            def _():
                self.meet(k)
                here = self.at(2 * k + net.x)

                @pl.when(net.z < nz - 1)
                def _():
                    net.landed(self.ll.at[k], self.lk + k)
                    self.add(here, self.ll.at[k])

                net.start(here, self.ll.at[k], self.lk + k, net.dp(net.d - 2))

        self.meet(net.z)

    def total(self, acc):
        net, mem = self.net, self.mem
        acc[...] = mem.get(self.at(2 * net.z + net.x)).astype(F32)

        @pl.when(net.z > 0)
        def _():
            net.landed(self.rl.at[net.z], self.rk + net.z)
            acc[...] += mem.get(self.rl.at[net.z]).astype(F32)

        @pl.when(net.z < net.nz - 1)
        def _():
            net.landed(self.ll.at[net.z], self.lk + net.z)
            acc[...] += mem.get(self.ll.at[net.z]).astype(F32)

    def end(self):
        net = self.net

        @pl.loop(0, net.nz)
        def _(zb):
            net.sent(self.xl.at[0], self.xk + zb)

            @pl.when(zb > net.z)
            def _():
                net.sent(self.rl.at[0], self.rk + zb)

            @pl.when(zb < net.z)
            def _():
                net.sent(self.ll.at[0], self.lk + zb)


class WideScatter:
    def __init__(self, net, part, own, cl, yl, xl, rl, ll, mem):
        self.net, self.part, self.own, self.cl, self.yl, self.mem = net, part, own, cl, yl, mem
        self.ck, self.yk = net.take(net.n), net.take(net.n)
        net.ends.append(self.end)
        self.inner = Scatter(net, lambda idx: own.at[0, idx], xl, rl, ll, mem)

    def order(self, k):
        net = self.net
        mine = k // net.nz
        zb = self.inner.order(k % net.nz)
        return 2 * zb + mine * net.x + (1 - mine) * (1 - net.x)

    def begin(self):
        net = self.net

        @pl.loop(0, net.n)
        def _(k):
            idx = self.order(k)
            net.start(
                self.part.at[pl.ds(2, 2), idx], self.cl.at[:, idx], self.ck + idx, net.tensor(net.tc)
            )

    def core(self):
        net = self.net

        @pl.loop(0, net.n)
        def _(k):
            idx = self.order(k)
            net.landed(self.cl.at[:, idx], self.ck + idx)
            self.inner.add(self.own.at[1, idx], self.cl.at[1, idx])
            net.start(self.own.at[1, idx], self.yl.at[idx], self.yk + idx, net.tensor(net.ty))
            self.inner.add(self.own.at[0, idx], self.cl.at[0, idx])

    def over(self):
        net = self.net

        @pl.loop(0, net.n)
        def _(k):
            idx = self.order(k)
            net.landed(self.yl.at[idx], self.yk + idx)
            self.inner.add(self.own.at[0, idx], self.yl.at[idx])

            @pl.when(k < net.nz)
            def _():
                self.inner.send_x(idx // 2)

    def end(self):
        net = self.net

        @pl.loop(0, net.n)
        def _(idx):
            net.sent(self.cl.at[:, 0], self.ck + idx)
            net.sent(self.yl.at[0], self.yk + idx)


class Direct:
    def get(self, ref):
        return ref[...]

    def put(self, ref, value):
        ref[...] = value


class Staged:
    def __init__(self, buf, sem):
        self.buf, self.sem = buf, sem

    def get(self, ref):
        copy = pltpu.make_async_copy(ref, self.buf, self.sem)
        copy.start()
        copy.wait()
        return self.buf[...]

    def put(self, ref, value):
        self.buf[...] = value
        copy = pltpu.make_async_copy(self.buf, ref, self.sem)
        copy.start()
        copy.wait()


def lane_row(gains, row, n):
    return jnp.concatenate([gains[8 * i + row : 8 * i + row + 1, :] for i in range(n)], axis=1)


def allowed_pairs(lens, rows):
    place_i = lax.broadcasted_iota(jnp.int32, (rows, 1), 0)
    place_j = lax.broadcasted_iota(jnp.int32, (1, rows), 1)
    segment_i = jnp.zeros((rows, 1), jnp.int32)
    segment_j = jnp.zeros((1, rows), jnp.int32)
    total = 0
    for k in range(lens.shape[1]):
        total = total + lens[0, k]
        segment_i += (place_i >= total).astype(jnp.int32)
        segment_j += (place_j >= total).astype(jnp.int32)
    distance = place_i - place_j
    return (segment_i == segment_j) & (distance >= 0) & (distance < WINDOW)


def softmax_head(query, key, allowed):
    scores = dot_nt(query, key) * HD ** (-0.5)
    scores = jnp.where(allowed, scores, MASKED)
    weights = jnp.exp(scores - jnp.max(scores, axis=-1, keepdims=True))
    return weights / jnp.sum(weights, axis=-1, keepdims=True)


def inverse_root(rows):
    return lax.rsqrt(jnp.mean(rows * rows, axis=-1, keepdims=True) + NORM_EPS)


def first_kernel(
    n, counts,
    lens, tok, go, gains, wq, wkv, wo, wg, wu, wd,
    wg_all, wu_all, wd_all, x_all, g_all, wq_out, wkv_out, wo_out, gains_out,
    query_out, keyval_out, context_out, normed_out, middle_out,
    send, recv, local, wq_all, wkv_all, wo_all, gains_all,
    group, kv_parts, branch, branch_c, branch_y, own_normed,
):
    net = Net(n, send, recv)
    d, t = net.d, net.t
    depth = wq.shape[0]
    quarter = wkv_all.shape[1]
    width = wg_all.shape[1]
    rows = tok.shape[0]

    def block(buf, idx):
        step = buf.shape[0] // n
        return buf.at[pl.ds(pl.multiple_of(idx * step, step), step)]

    def wide_block(buf, idx):
        return buf.at[0, idx]

    wkv_own = wkv.at[:, pl.ds(pl.multiple_of(t * quarter, 128), quarter)]
    tokens_g = TensorGather(net, lambda i: group.at[i])
    kv_g = TensorGather(net, lambda i: kv_parts.at[i])
    branch_s = TensorScatter(net, branch, branch_c, branch_y)
    first_w = Spread(net, [wq_all, wkv_all, gains_all], block)
    second_w = Spread(net, [wo_all], block)
    spread_g = Spread(net, [g_all], wide_block, wide=True)
    spread_x = Spread(net, [x_all], wide_block, wide=True)
    deals = [
        Deal(
            net,
            lambda to, w=w: w.at[:, pl.ds(pl.multiple_of(to * width, 128), width)],
            lambda frm, full=full: block(full, frm),
        )
        for w, full in ((wg, wg_all), (wu, wu_all), (wd, wd_all))
    ]
    assert net.used <= counts

    own_copies = [
        (tok, group.at[t]),
        (wq, block(wq_all, d)),
        (wkv_own, block(wkv_all, d)),
        (gains, block(gains_all, d)),
        (wo, block(wo_all, d)),
        (go, g_all.at[0, d]),
    ] + [(deal.src(d), deal.dst(d)) for deal in deals]
    own_copies = [
        pltpu.make_async_copy(a, b, local.at[i]) for i, (a, b) in enumerate(own_copies)
    ]
    for copy in own_copies:
        copy.start()
    net.greet()

    for copy in own_copies[:5]:
        copy.wait()
    tokens_g.begin()
    first_w.begin()
    second_w.begin()
    deals[0].begin()
    spread_g.begin([go])
    tokens_g.rest()

    @pl.loop(1, net.nz)
    def _(h):
        first_w.hop(h)
        second_w.hop(h)
        spread_g.hop(h)

    inputs = group[...].reshape(4 * rows, -1).astype(F32)
    root = inverse_root(inputs)
    first_w.cross()
    spread_g.cross()
    gain = lane_row(gains_all, 0, n)
    normed = (inputs * root * gain).astype(BF16)
    normed_out[...] = normed
    kv_parts[t] = dot_nn(normed, wkv_all[...]).astype(BF16)
    kv_g.begin()
    deals[1].begin()
    query_out[...] = dot_nn(normed, wq_all[...]).astype(BF16)
    kv_g.rest()
    for i in range(4):
        keyval_out[:, i * quarter : (i + 1) * quarter] = kv_parts[i]
    allowed = allowed_pairs(lens, 4 * rows)
    for h in range(query_out.shape[1] // HD):
        lanes = slice(h * HD, (h + 1) * HD)
        probs = softmax_head(query_out[:, lanes], keyval_out[:, :HD], allowed).astype(BF16)
        context_out[:, lanes] = dot_nn(probs, keyval_out[:, HD:]).astype(BF16)
    second_w.cross()
    branch[...] = dot_nt(context_out[...], wo_all[...]).astype(BF16).reshape(branch.shape)
    branch_s.begin()
    middle = tok_rows(group, t) + branch_s.rest()
    middle_out[...] = middle
    own_normed[...] = (middle * inverse_root(middle) * lane_row(gains_all, 1, n)).astype(BF16)
    own_x = pltpu.make_async_copy(own_normed, x_all.at[0, d], local.at[0])
    own_x.start()
    spread_x.begin([own_normed])
    deals[2].begin()
    outs = [
        pltpu.make_async_copy(a, b, local.at[1 + i])
        for i, (a, b) in enumerate(
            (
                (wq_all, wq_out),
                (wkv_all, wkv_out),
                (wo_all, wo_out),
                (gains_all, gains_out),
            )
        )
    ]
    for copy in outs:
        copy.start()
    own_copies[5].wait()
    spread_x.hops()
    spread_x.cross()
    spread_g.over()
    own_x.wait()
    spread_x.over()
    spread_g.done()
    spread_x.done()
    for deal in deals:
        deal.done()
    for copy in own_copies[6:] + outs:
        copy.wait()
    net.finish()


def tok_rows(group, t):
    return group[t].astype(F32)


def ffn_kernel(
    x_ref, g_ref, wg, wu, wd, o_ref, dx_ref, dwg_ref, dwu_ref, dwd_ref, acc_g, acc_u, acc_d
):
    step = pl.program_id(0)
    x, g = x_ref[...], g_ref[...]
    gate = dot_nn(x, wg[...])
    up = dot_nn(x, wu[...])
    grad_hidden = dot_nn(g, wd[...])
    root = (2.0 / jnp.pi) ** 0.5
    square = gate * gate
    tanh = jnp.tanh(root * gate * (1.0 + 0.044715 * square))
    half = 0.5 * (1.0 + tanh)
    gelu = gate * half
    slope = half + 0.5 * gate * (1.0 - tanh * tanh) * (root * (1.0 + 3 * 0.044715 * square))
    hidden = (gelu * up).astype(BF16)
    grad_gate = (grad_hidden * up * slope).astype(BF16)
    grad_up = (grad_hidden * gelu).astype(BF16)
    o_ref[...] = dot_nt(hidden, wd[...]).astype(BF16)
    dx_ref[...] = (dot_nt(grad_gate, wg[...]) + dot_nt(grad_up, wu[...])).astype(BF16)

    @pl.when(step == 0)
    def _():
        acc_g[...] = dot_tn(x, grad_gate)
        acc_u[...] = dot_tn(x, grad_up)
        acc_d[...] = dot_tn(g, hidden)

    @pl.when(step > 0)
    def _():
        acc_g[...] += dot_tn(x, grad_gate)
        acc_u[...] += dot_tn(x, grad_up)
        acc_d[...] += dot_tn(g, hidden)

    @pl.when(step == pl.num_programs(0) - 1)
    def _():
        dwg_ref[...] = acc_g[...].astype(BF16)
        dwu_ref[...] = acc_u[...].astype(BF16)
        dwd_ref[...] = acc_d[...].astype(BF16)


def second_kernel(
    n, counts, staged,
    lens, o_part, dx_part, dwg, dwu, dwd, tok, go, wq_all, wkv_all, wo_all, gains_all,
    query, keyval, context, normed, middle,
    block_out, grad_tokens, grad_gains, grad_wq, grad_wkv, grad_wo, grad_wg, grad_wu, grad_wd,
    dx_own, dx_c, dx_y, dx_x, dx_r, dx_l, o_own, o_c, o_y, o_x, o_r, o_l,
    send, recv, local, stage,
    acc, branch_rows, gkv, gkv_c, gkv_y, qpart, qpart_c, qpart_y,
    pq, pq_x, pq_r, pq_l, po, po_x, po_r, po_l, pk, pk_x, pk_r, pk_l, k_rows, acc_w, acc_k,
    gain_parts, gain_land, gain_sum, grad_query, own_grad,
):
    net = Net(n, send, recv)
    d, t = net.d, net.t
    depth = grad_wq.shape[0]
    width = dwg.shape[1]
    rows, features = tok.shape
    quarter = wkv_all.shape[1]

    def block(buf, idx):
        step = buf.shape[0] // n
        return buf.at[pl.ds(pl.multiple_of(idx * step, step), step)]

    mem = Staged(stage, local.at[0]) if staged else Direct()
    scatter_dx = WideScatter(net, dx_part, dx_own, dx_c, dx_y, dx_x, dx_r, dx_l, mem)
    scatter_o = WideScatter(net, o_part, o_own, o_c, o_y, o_x, o_r, o_l, mem)
    direct = Direct()
    scatter_q = Scatter(net, lambda i: block(pq, i), pq_x, pq_r, pq_l, direct)
    scatter_w = Scatter(net, lambda i: block(po, i), po_x, po_r, po_l, direct)
    scatter_k = Scatter(net, lambda i: block(pk, i), pk_x, pk_r, pk_l, direct)
    branch_g = TensorGather(net, lambda i: branch_rows.at[i])
    kv_s = TensorScatter(net, gkv, gkv_c, gkv_y)
    query_s = TensorScatter(net, qpart, qpart_c, qpart_y)
    kv_g = TensorGather(net, lambda i: k_rows.at[i])
    gain_deal = Deal(net, lambda to: gain_parts.at[to], lambda frm: gain_land.at[frm])
    gain_g = TensorGather(net, lambda i: gain_sum.at[i])
    deals = [
        Deal(
            net,
            lambda to, p=part: block(p, to),
            lambda frm, o=out: o.at[:, pl.ds(pl.multiple_of(frm * width, 128), width)],
        )
        for part, out in ((dwg, grad_wg), (dwu, grad_wu), (dwd, grad_wd))
    ]
    assert net.used <= counts
    copies = [(dx_part.at[pl.ds(0, 2)], dx_own), (o_part.at[pl.ds(0, 2)], o_own)] + [
        (deal.src(d), deal.dst(d)) for deal in deals
    ]
    copies = [pltpu.make_async_copy(a, b, local.at[1 + i]) for i, (a, b) in enumerate(copies)]
    for copy in copies:
        copy.start()
    net.greet()
    scatter_dx.begin()
    scatter_o.begin()
    copies[0].wait()
    scatter_dx.core()
    deals[0].begin()
    scatter_dx.over()
    copies[1].wait()
    scatter_o.core()
    scatter_dx.inner.lines()
    scatter_dx.inner.total(acc)

    rows_in = middle[...]
    root = inverse_root(rows_in)
    grad_normed = acc[...]
    gain = lane_row(gains_all, 1, n)
    scaled = grad_normed * gain
    inner = jnp.mean(scaled * rows_in, axis=-1, keepdims=True)
    grad_middle = go[...].astype(F32) + root * (scaled - rows_in * (root * root) * inner)
    own_grad[...] = grad_middle
    gain_ffn = jnp.sum(grad_normed * rows_in * root, axis=0, keepdims=True)
    branch_rows[t] = grad_middle.astype(BF16)
    branch_g.begin()
    deals[1].begin()
    scatter_o.over()
    branch_g.rest()
    grad_branch = branch_rows[...].reshape(4 * rows, features)
    grad_context = dot_nn(grad_branch, wo_all[...]).astype(BF16)
    chunk = 512
    for i in range(features // chunk):
        part = slice(i * chunk, (i + 1) * chunk)
        po[part, :] = dot_tn(grad_branch[:, part], context[...]).astype(BF16)
    scatter_w.begin()

    allowed = allowed_pairs(lens, 4 * rows)
    key, value = keyval[:, :HD], keyval[:, HD:]
    grad_key = jnp.zeros((4 * rows, HD), F32)
    grad_value = jnp.zeros((4 * rows, HD), F32)
    factor = HD ** (-0.5)
    for h in range(query.shape[1] // HD):
        lanes = slice(h * HD, (h + 1) * HD)
        probs = softmax_head(query[:, lanes], key, allowed)
        grad_head = grad_context[:, lanes]
        grad_probs = dot_nt(grad_head, value)
        inner = jnp.sum(grad_probs * probs, axis=-1, keepdims=True)
        grad_scores = (probs * (grad_probs - inner)).astype(BF16)
        grad_query[:, lanes] = (dot_nn(grad_scores, key) * factor).astype(BF16)
        grad_key += dot_tn(grad_scores, query[:, lanes]) * factor
        grad_value += dot_tn(probs.astype(BF16), grad_head)
    both = jnp.concatenate([grad_key, grad_value], axis=1).astype(BF16)
    for i in range(4):
        gkv[i] = both[:, i * quarter : (i + 1) * quarter]
    kv_s.begin()
    scatter_o.inner.lines()
    grad_kv = kv_s.rest().astype(BF16)
    term = dot_nt(grad_query[...], wq_all[...]) + dot_nt(grad_kv, wkv_all[...])
    qpart[...] = term.astype(BF16).reshape(qpart.shape)
    query_s.begin()
    for i in range(features // chunk):
        part = slice(i * chunk, (i + 1) * chunk)
        pq[part, :] = dot_tn(normed[:, part], grad_query[...]).astype(BF16)
        pk[part, :] = dot_tn(normed[:, part], grad_kv).astype(BF16)
    scatter_q.begin()
    scatter_k.begin()
    grad_normed = query_s.rest()

    rows_in = tok[...].astype(F32)
    root = inverse_root(rows_in)
    gain = lane_row(gains_all, 0, n)
    scaled = grad_normed * gain
    inner = jnp.mean(scaled * rows_in, axis=-1, keepdims=True)
    grad_tokens[...] = own_grad[...] + root * (scaled - rows_in * (root * root) * inner)
    gain_attn = jnp.sum(grad_normed * rows_in * root, axis=0, keepdims=True)
    for i in range(n):
        lanes = slice(i * depth, (i + 1) * depth)
        gain_parts[i, 0:1, :] = gain_attn[:, lanes]
        gain_parts[i, 1:2, :] = gain_ffn[:, lanes]
        gain_parts[i, 2:8, :] = jnp.zeros((6, depth), F32)
    gain_deal.begin()
    deals[2].begin()

    scatter_o.inner.total(acc)
    block_out[...] = (middle[...] + acc[...]).astype(BF16)
    scatter_w.lines()
    scatter_q.lines()
    scatter_k.lines()
    gain_land[d] = gain_parts[d]
    gain_deal.done()
    gain_sum[t] = jnp.sum(gain_land[...], axis=0)
    gain_g.begin()
    scatter_w.total(acc_w)
    grad_wo[...] = acc_w[...]
    scatter_q.total(acc_w)
    grad_wq[...] = acc_w[...]
    scatter_k.total(acc_k)
    k_rows[t] = acc_k[...]
    kv_g.begin()
    gain_g.rest()
    grad_gains[...] = jnp.sum(gain_sum[...], axis=0)
    kv_g.rest()
    for i in range(4):
        grad_wkv[:, i * quarter : (i + 1) * quarter] = k_rows[i]
    for deal in deals:
        deal.done()
    for copy in copies[2:]:
        copy.wait()
    net.finish()


def params(collective_id):
    return pltpu.CompilerParams(
        collective_id=collective_id, has_side_effects=True, vmem_limit_bytes=60 * MIB
    )


def body(
    n, tokens, grad_out, lengths, gain_attn, gain_ffn, w_query, w_keyval, w_out, w_gate, w_up, w_down
):
    nz = n // 2
    rows, features = tokens.shape
    depth, heads = w_query.shape
    quarter = w_keyval.shape[1] // 4
    width = w_gate.shape[1] // n
    group_rows = 4 * rows
    shape = jax.ShapeDtypeStruct
    gains = jnp.concatenate(
        [gain_attn[None], gain_ffn[None], jnp.zeros((6, depth), gain_attn.dtype)]
    ).astype(F32)

    counts = 9 + 4 * 3 * nz + 2 * (3 * nz + 2 * n) + 3 * n
    full = shape((features, width), BF16)
    wide = shape((4, n, rows, features), BF16)
    (
        wg_all, wu_all, wd_all, x_all, g_all, wq_all, wkv_all, wo_all, gains_all,
        query, keyval, context, normed, middle,
    ) = pl.pallas_call(
        functools.partial(first_kernel, n, counts),
        out_shape=(
            full, full, full, wide, wide,
            shape((features, heads), BF16),
            shape((features, quarter), BF16),
            shape((features, heads), BF16),
            shape((8 * n, depth), F32),
            shape((group_rows, heads), BF16),
            shape((group_rows, 2 * HD), BF16),
            shape((group_rows, heads), BF16),
            shape((group_rows, features), BF16),
            shape((rows, features), F32),
        ),
        in_specs=[SMEM] + [ANY] * 9,
        out_specs=(ANY,) * 9 + (VMEM,) * 5,
        scratch_shapes=[
            pltpu.SemaphoreType.DMA((counts,)),
            pltpu.SemaphoreType.DMA((counts,)),
            pltpu.SemaphoreType.DMA((9,)),
            pltpu.VMEM((features, heads), BF16),
            pltpu.VMEM((features, quarter), BF16),
            pltpu.VMEM((features, heads), BF16),
            pltpu.VMEM((8 * n, depth), F32),
            pltpu.VMEM((4, rows, features), BF16),
            pltpu.VMEM((4, group_rows, quarter), BF16),
            pltpu.VMEM((4, rows, features), BF16),
            pltpu.VMEM((2, rows, features), BF16),
            pltpu.VMEM((rows, features), BF16),
            pltpu.VMEM((rows, features), BF16),
        ],
        compiler_params=params(0),
        name="forward_attention",
    )(lengths, tokens, grad_out, gains, w_query, w_keyval, w_out, w_gate, w_up, w_down)

    all_rows = 4 * n * rows
    tile = 256
    row_tile = pl.BlockSpec((tile, features), lambda i: (i, 0))
    whole = pl.BlockSpec((features, width), lambda i: (0, 0), pipeline_mode=pl.Buffered(1))
    o_part, dx_part, dwg, dwu, dwd = pl.pallas_call(
        ffn_kernel,
        grid=(all_rows // tile,),
        out_shape=(
            shape((all_rows, features), BF16), shape((all_rows, features), BF16), full, full, full,
        ),
        in_specs=[row_tile, row_tile, whole, whole, whole],
        out_specs=(row_tile, row_tile, whole, whole, whole),
        scratch_shapes=[pltpu.VMEM((features, width), F32)] * 3,
        compiler_params=pltpu.CompilerParams(vmem_limit_bytes=60 * MIB),
        cost_estimate=pl.CostEstimate(
            flops=18 * all_rows * features * width,
            bytes_accessed=8 * all_rows * features,
            transcendentals=all_rows * width,
        ),
        name="feed_forward",
    )(
        x_all.reshape(all_rows, features), g_all.reshape(all_rows, features), wg_all, wu_all, wd_all
    )

    staged = n > 8
    counts = 2 * (2 * n + 3 * nz) + 3 * 3 * nz + 15 + n + 3 * n
    landing = [
        shape((2, n, rows, features), BF16),
        shape((2, n, rows, features), BF16),
        shape((n, rows, features), BF16),
        shape((nz, rows, features), BF16),
        shape((nz, rows, features), BF16),
        shape((nz, rows, features), BF16),
    ] * 2
    out_shape = [
        shape((rows, features), BF16),
        shape((rows, features), F32),
        shape((8, depth), F32),
        shape((depth, heads), F32),
        shape((depth, 4 * quarter), F32),
        shape((depth, heads), F32),
        shape((depth, n * width), BF16),
        shape((depth, n * width), BF16),
        shape((depth, n * width), BF16),
    ]
    out_specs = [VMEM] * 6 + [ANY] * 3
    in_vmem = []
    if staged:
        out_shape += landing
        out_specs += [ANY] * len(landing)
    else:
        in_vmem = [pltpu.VMEM(place.shape, place.dtype) for place in landing]

    def reduced(columns):
        return [pltpu.VMEM((features, columns), BF16)] + [
            pltpu.VMEM((nz, depth, columns), BF16)
        ] * 3

    results = pl.pallas_call(
        functools.partial(second_kernel, n, counts, staged),
        out_shape=tuple(out_shape),
        in_specs=[SMEM] + [ANY] * 5 + [VMEM] * 11,
        out_specs=tuple(out_specs),
        scratch_shapes=in_vmem
        + [
            pltpu.SemaphoreType.DMA((counts,)),
            pltpu.SemaphoreType.DMA((counts,)),
            pltpu.SemaphoreType.DMA((6,)),
            pltpu.VMEM((rows, features), BF16),
            pltpu.VMEM((rows, features), F32),
            pltpu.VMEM((4, rows, features), BF16),
            pltpu.VMEM((4, group_rows, quarter), BF16),
            pltpu.VMEM((2, group_rows, quarter), BF16),
            pltpu.VMEM((group_rows, quarter), BF16),
            pltpu.VMEM((4, rows, features), BF16),
            pltpu.VMEM((2, rows, features), BF16),
            pltpu.VMEM((rows, features), BF16),
        ]
        + reduced(heads)
        + reduced(heads)
        + reduced(quarter)
        + [
            pltpu.VMEM((4, depth, quarter), F32),
            pltpu.VMEM((depth, heads), F32),
            pltpu.VMEM((depth, quarter), F32),
            pltpu.VMEM((n, 8, depth), F32),
            pltpu.VMEM((n, 8, depth), F32),
            pltpu.VMEM((4, 8, depth), F32),
            pltpu.VMEM((group_rows, heads), BF16),
            pltpu.VMEM((rows, features), F32),
        ],
        compiler_params=params(1),
        name="backward_attention",
    )(
        lengths, o_part.reshape(4, n, rows, features), dx_part.reshape(4, n, rows, features),
        dwg, dwu, dwd, tokens, grad_out, wq_all, wkv_all, wo_all, gains_all,
        query, keyval, context, normed, middle,
    )
    block_out, grad_tokens, grad_gains, grad_wq, grad_wkv, grad_wo, grad_wg, grad_wu, grad_wd = (
        results[:9]
    )
    return (
        block_out,
        grad_tokens,
        grad_gains[0],
        grad_gains[1],
        grad_wq,
        grad_wkv,
        grad_wo,
        grad_wg.astype(F32),
        grad_wu.astype(F32),
        grad_wd.astype(F32),
    )


def solution(mesh):
    rows = P(("dp", "tensor"), None)
    both = P("dp", "tensor")
    return jax.shard_map(
        functools.partial(body, mesh.shape["dp"]),
        mesh=mesh,
        in_specs=(rows, rows, P("dp", None), P("dp"), P("dp"), both, P("dp", None), both, both, both, both),
        out_specs=(rows, rows, P("dp"), P("dp"), both, P("dp", None), both, both, both, both),
        check_vma=False,
    )
```

```python
import functools

import jax
import jax.numpy as jnp
from jax import lax
from jax.experimental import pallas as pl
from jax.experimental.pallas import tpu as pltpu
from jax.sharding import PartitionSpec as P

HD = 256
WINDOW = 2048
NORM_EPS = 1e-06
MASKED = -1e30
BF16, F32 = jnp.bfloat16, jnp.float32
MESH = pl.DeviceIdType.MESH
ANY = pl.BlockSpec(memory_space=pl.ANY)
VMEM = pl.BlockSpec(memory_space=pltpu.VMEM)
SMEM = pl.BlockSpec(memory_space=pltpu.SMEM)
MIB = 1 << 20


def dot_nn(a, b):
    return lax.dot_general(a, b, (((1,), (0,)), ((), ())), preferred_element_type=F32)


def dot_nt(a, b):
    return lax.dot_general(a, b, (((1,), (1,)), ((), ())), preferred_element_type=F32)


def dot_tn(a, b):
    return lax.dot_general(a, b, (((0,), (0,)), ((), ())), preferred_element_type=F32)


class Net:
    def __init__(self, n, send, recv):
        self.n, self.nz = n, n // 2
        self.send, self.recv, self.used = send, recv, 0
        self.d = lax.axis_index("dp")
        self.t = lax.axis_index("tensor")
        self.z = self.d // 2
        self.x = self.d % 2
        self.dx = self.d + 1 - 2 * self.x
        self.ty = (self.t + 2) % 4
        self.tc = self.t + 1 - 2 * (self.t % 2)
        self.tcy = (self.tc + 2) % 4
        self.ends = []

    def take(self, count):
        first = self.used
        self.used += count
        return first

    def dp(self, other):
        return (other, self.t)

    def tensor(self, other):
        return (self.d, other)

    def make(self, src, dst, k, device):
        return pltpu.make_async_remote_copy(
            src_ref=src,
            dst_ref=dst,
            send_sem=self.send.at[k],
            recv_sem=self.recv.at[k],
            device_id=device,
            device_id_type=MESH,
        )

    def start(self, src, dst, k, device):
        self.make(src, dst, k, device).start()

    def landed(self, ref, k):
        self.make(ref, ref, k, self.tensor(self.tc)).wait_recv()

    def sent(self, ref, k):
        self.make(ref, ref, k, self.tensor(self.tc)).wait_send()

    def greet(self):
        barrier = pltpu.get_barrier_semaphore()

        @pl.loop(1, self.n)
        def _(m):
            pl.semaphore_signal(
                barrier, inc=1, device_id=self.dp((self.d + m) % self.n), device_id_type=MESH
            )

        for other in (self.ty, self.tc):
            pl.semaphore_signal(
                barrier, inc=1, device_id=self.tensor(other), device_id_type=MESH
            )
        pl.semaphore_wait(barrier, self.n + 1)

    def finish(self):
        for end in self.ends:
            end()


class TensorGather:
    def __init__(self, net, at):
        self.net, self.at, self.k = net, at, net.take(3)
        net.ends.append(self.end)

    def begin(self):
        net = self.net
        net.start(self.at(net.t), self.at(net.t), self.k, net.tensor(net.ty))
        net.start(self.at(net.t), self.at(net.t), self.k + 1, net.tensor(net.tc))

    def rest(self):
        net = self.net
        net.landed(self.at(net.ty), self.k)
        net.start(self.at(net.ty), self.at(net.ty), self.k + 2, net.tensor(net.tc))
        net.landed(self.at(net.tc), self.k + 1)
        net.landed(self.at(net.tcy), self.k + 2)

    def end(self):
        for i in range(3):
            self.net.sent(self.at(0), self.k + i)


class TensorScatter:
    def __init__(self, net, part, cl, yl):
        self.net, self.part, self.cl, self.yl, self.k = net, part, cl, yl, net.take(3)
        net.ends.append(self.end)

    def begin(self):
        net = self.net
        net.start(self.part.at[net.tcy], self.cl.at[1], self.k + 1, net.tensor(net.tc))
        net.start(self.part.at[net.tc], self.cl.at[0], self.k, net.tensor(net.tc))

    def rest(self):
        net = self.net
        net.landed(self.cl.at[1], self.k + 1)
        pair = self.part[net.ty].astype(F32) + self.cl[1].astype(F32)
        self.part[net.ty] = pair.astype(self.part.dtype)
        net.start(self.part.at[net.ty], self.yl, self.k + 2, net.tensor(net.ty))
        net.landed(self.cl.at[0], self.k)
        own = self.part[net.t].astype(F32) + self.cl[0].astype(F32)
        net.landed(self.yl, self.k + 2)
        return own + self.yl[...].astype(F32)

    def end(self):
        for i in range(3):
            self.net.sent(self.yl, self.k + i)


class Spread:
    def __init__(self, net, bufs, block):
        self.net, self.bufs, self.block = net, bufs, block
        self.zk = [net.take(2 * net.nz) for _ in bufs]
        self.xk = [net.take(net.nz) for _ in bufs]
        net.ends.append(self.end)

    def line(self, j, zb, right):
        net = self.net
        here = self.block(self.bufs[j], 2 * zb + net.x)
        if right:
            net.start(here, here, self.zk[j] + zb, net.dp(net.d + 2))
        else:
            net.start(here, here, self.zk[j] + net.nz + zb, net.dp(net.d - 2))

    def over_x(self, j, zb):
        net = self.net
        here = self.block(self.bufs[j], 2 * zb + net.x)
        net.start(here, here, self.xk[j] + zb, net.dp(net.dx))

    def begin(self):
        net = self.net
        for j in range(len(self.bufs)):

            @pl.when(net.z < net.nz - 1)
            def _():
                self.line(j, net.z, True)

            @pl.when(net.z > 0)
            def _():
                self.line(j, net.z, False)

            self.over_x(j, net.z)

    def hop(self, h):
        net = self.net
        nz = net.nz
        for j, buf in enumerate(self.bufs):

            @pl.when(net.z - h >= 0)
            def _():
                zb = net.z - h
                net.landed(self.block(buf, 2 * zb + net.x), self.zk[j] + zb)

                @pl.when(net.z < nz - 1)
                def _():
                    self.line(j, zb, True)

                self.over_x(j, zb)

            @pl.when(net.z + h <= nz - 1)
            def _():
                zb = net.z + h
                net.landed(self.block(buf, 2 * zb + net.x), self.zk[j] + nz + zb)

                @pl.when(net.z > 0)
                def _():
                    self.line(j, zb, False)

                self.over_x(j, zb)

    def cross(self):
        net = self.net

        @pl.loop(0, net.nz)
        def _(k):
            zb = (net.z + k) % net.nz
            for j, buf in enumerate(self.bufs):
                net.landed(self.block(buf, 2 * zb + 1 - net.x), self.xk[j] + zb)

    def end(self):
        net = self.net

        @pl.loop(0, net.nz)
        def _(zb):
            for j, buf in enumerate(self.bufs):
                some = self.block(buf, 0)

                @pl.when((zb <= net.z) & (net.z < net.nz - 1))
                def _():
                    net.sent(some, self.zk[j] + zb)

                @pl.when((zb >= net.z) & (net.z > 0))
                def _():
                    net.sent(some, self.zk[j] + net.nz + zb)

                net.sent(some, self.xk[j] + zb)


class WideSpread:
    def __init__(self, net, buf):
        self.net, self.buf = net, buf
        self.zk, self.xk = net.take(2 * net.nz), net.take(net.nz)
        self.yk, self.ck = net.take(2 * net.nz), net.take(4)
        net.ends.append(self.end)

    def onward(self, src, zb, right, left):
        net, buf = self.net, self.buf
        if right:

            @pl.when(net.z < net.nz - 1)
            def _():
                net.start(src, buf.at[0, zb], self.zk + zb, net.dp(net.d + 2))

        if left:

            @pl.when(net.z > 0)
            def _():
                net.start(src, buf.at[0, zb], self.zk + net.nz + zb, net.dp(net.d - 2))

        net.start(src, buf.at[2, zb], self.yk + zb, net.tensor(net.ty))
        net.start(src, buf.at[1, zb], self.xk + zb, net.dp(net.dx))

    def begin(self, own):
        self.onward(own, self.net.z, True, True)

    def hop(self, h):
        net, buf = self.net, self.buf

        @pl.when(net.z - h >= 0)
        def _():
            zb = net.z - h
            net.landed(buf.at[0, zb], self.zk + zb)
            self.onward(buf.at[0, zb], zb, True, False)

        @pl.when(net.z + h <= net.nz - 1)
        def _():
            zb = net.z + h
            net.landed(buf.at[0, zb], self.zk + net.nz + zb)
            self.onward(buf.at[0, zb], zb, False, True)

    def hops(self):
        @pl.loop(1, self.net.nz)
        def _(h):
            self.hop(h)

    def cross(self):
        net, buf = self.net, self.buf

        @pl.loop(0, net.nz)
        def _(k):
            zb = (net.z + k) % net.nz
            net.landed(buf.at[1, zb], self.xk + zb)
            net.start(buf.at[1, zb], buf.at[3, zb], self.yk + net.nz + zb, net.tensor(net.ty))

    def over(self, x):
        net = self.net

        @pl.loop(0, net.nz)
        def _(k):
            zb = (net.z + k) % net.nz
            net.landed(self.buf.at[2 + x, zb], self.yk + x * net.nz + zb)

    def core(self, slot):
        net = self.net
        net.start(self.buf.at[slot], self.buf.at[4 + slot], self.ck + slot, net.tensor(net.tc))

    def core_done(self, slot):
        self.net.landed(self.buf.at[4 + slot], self.ck + slot)

    def end(self):
        net = self.net
        some = self.buf.at[0, 0]

        @pl.loop(0, net.nz)
        def _(zb):
            @pl.when((zb <= net.z) & (net.z < net.nz - 1))
            def _():
                net.sent(some, self.zk + zb)

            @pl.when((zb >= net.z) & (net.z > 0))
            def _():
                net.sent(some, self.zk + net.nz + zb)

            net.sent(some, self.xk + zb)
            net.sent(some, self.yk + zb)
            net.sent(some, self.yk + net.nz + zb)

        for slot in range(4):
            net.sent(self.buf.at[0], self.ck + slot)


class Deal:
    def __init__(self, net, src, dst):
        self.net, self.src, self.dst, self.k = net, src, dst, net.take(net.n)
        net.ends.append(self.end)

    def send(self, m):
        net = self.net
        to = (net.d + m) % net.n
        net.start(self.src(to), self.dst(net.d), self.k + m, net.dp(to))

    def begin(self):
        pl.loop(1, self.net.n)(self.send)

    def done(self):
        net = self.net

        @pl.loop(1, net.n)
        def _(m):
            net.landed(self.dst((net.d - m + net.n) % net.n), self.k + m)

    def end(self):
        net = self.net

        @pl.loop(1, net.n)
        def _(m):
            net.sent(self.src(0), self.k + m)


class Flow:
    def __init__(self, deals):
        self.todo = [(deal, m) for deal in deals for m in range(1, deal.net.n)]
        self.total, self.gone, self.share = len(self.todo), 0, 0.0

    def pump(self, share):
        self.share += share
        upto = min(self.total, round(self.share * self.total))
        for deal, m in self.todo[self.gone : upto]:
            deal.send(m)
        self.gone = max(upto, self.gone)

    def rest(self):
        self.pump(1.0)


class Scatter:
    def __init__(self, net, own, other, xl, zl, mem):
        self.net, self.own, self.other, self.xl, self.zl, self.mem = net, own, other, xl, zl, mem
        self.xk, self.rk, self.lk = net.take(net.nz), net.take(net.nz), net.take(net.nz)
        net.ends.append(self.end)

    def order(self, k):
        odd = k % 2
        return odd * (k // 2) + (1 - odd) * (self.net.nz - 1 - k // 2)

    def send_x(self, zb):
        net = self.net
        net.start(self.other(zb), self.xl.at[zb], self.xk + zb, net.dp(net.dx))

    def begin(self):
        @pl.loop(0, self.net.nz)
        def _(k):
            self.send_x(self.order(k))

    def add(self, block, other):
        mem = self.mem
        mem.put(block, (mem.get(block).astype(F32) + mem.get(other).astype(F32)).astype(BF16))

    def meet(self, zb):
        net = self.net
        net.landed(self.xl.at[zb], self.xk + zb)
        self.add(self.own(zb), self.xl.at[zb])

    def lines(self):
        net = self.net
        nz = net.nz

        @pl.loop(0, nz - 1)
        def _(k):
            far = nz - 1 - k

            @pl.when(far > net.z)
            def _():
                self.meet(far)
                here = self.own(far)

                @pl.when(net.z > 0)
                def _():
                    net.landed(self.zl.at[far], self.rk + far)
                    self.add(here, self.zl.at[far])

                net.start(here, self.zl.at[far], self.rk + far, net.dp(net.d + 2))

            @pl.when(k < net.z)
            def _():
                self.meet(k)
                here = self.own(k)

                @pl.when(net.z < nz - 1)
                def _():
                    net.landed(self.zl.at[k], self.lk + k)
                    self.add(here, self.zl.at[k])

                last = (k == net.z - 1).astype(jnp.int32)
                net.start(
                    here, self.zl.at[last * nz + (1 - last) * k], self.lk + k, net.dp(net.d - 2)
                )

        self.meet(net.z)

    def total(self, acc):
        net, mem = self.net, self.mem
        acc[...] = mem.get(self.own(net.z)).astype(F32)

        @pl.when(net.z > 0)
        def _():
            net.landed(self.zl.at[net.z], self.rk + net.z)
            acc[...] += mem.get(self.zl.at[net.z]).astype(F32)

        @pl.when(net.z < net.nz - 1)
        def _():
            net.landed(self.zl.at[net.nz], self.lk + net.z)
            acc[...] += mem.get(self.zl.at[net.nz]).astype(F32)

    def end(self):
        net = self.net

        @pl.loop(0, net.nz)
        def _(zb):
            net.sent(self.xl.at[0], self.xk + zb)

            @pl.when(zb > net.z)
            def _():
                net.sent(self.zl.at[0], self.rk + zb)

            @pl.when(zb < net.z)
            def _():
                net.sent(self.zl.at[0], self.lk + zb)


class WideScatter(Scatter):
    def __init__(self, net, cl, yl, xl, zl, mem, tiles):
        self.cl, self.yl, self.tiles = cl, yl, tiles
        self.ck, self.yk = net.take(4 * tiles), net.take(2 * net.nz)
        super().__init__(net, lambda zb: cl.at[0, zb], lambda zb: cl.at[1, zb], xl, zl, mem)
        net.ends.append(self.wide_end)

    def place(self, yx, sub):
        blocks = self.net.nz // self.tiles
        return self.cl.at[yx, pl.ds(sub * blocks, blocks)]

    def to_core(self, stage, yx, sub):
        net = self.net
        net.start(stage, self.place(yx, sub), self.ck + yx * self.tiles + sub, net.tensor(net.tc))

    def core_sent(self, yx, sub):
        self.net.sent(self.place(0, 0), self.ck + yx * self.tiles + sub)

    def keep(self, value, yx, sub):
        place = self.place(yx, sub)
        self.net.landed(place, self.ck + yx * self.tiles + sub)
        value = value.reshape(place.shape) + self.mem.get(place).astype(F32)
        self.mem.put(place, value.astype(BF16))

    def to_y(self, x, zb):
        net = self.net
        net.start(
            self.cl.at[2 + x, zb], self.yl.at[x, zb], self.yk + x * net.nz + zb, net.tensor(net.ty)
        )

    def all_to_y(self, x):
        @pl.loop(0, self.net.nz)
        def _(k):
            self.to_y(x, self.order(k))

    def from_y(self, x, zb):
        net = self.net
        net.landed(self.yl.at[x, zb], self.yk + x * net.nz + zb)
        self.add(self.cl.at[x, zb], self.yl.at[x, zb])

    def over(self):
        @pl.loop(0, self.net.nz)
        def _(k):
            zb = self.order(k)
            self.from_y(1, zb)
            self.send_x(zb)

    def meet(self, zb):
        self.from_y(0, zb)
        super().meet(zb)

    def wide_end(self):
        net = self.net

        @pl.loop(0, net.nz)
        def _(zb):
            net.sent(self.yl.at[0, 0], self.yk + zb)
            net.sent(self.yl.at[0, 0], self.yk + net.nz + zb)


class Direct:
    def get(self, ref):
        return ref[...]

    def put(self, ref, value):
        ref[...] = value


class Staged:
    def __init__(self, buf, sem):
        self.buf, self.sem = buf, sem

    def view(self, ref):
        return self.buf if len(ref.shape) == 3 else self.buf.at[0]

    def get(self, ref):
        view = self.view(ref)
        copy = pltpu.make_async_copy(ref, view, self.sem)
        copy.start()
        copy.wait()
        return view[...]

    def put(self, ref, value):
        view = self.view(ref)
        view[...] = value
        copy = pltpu.make_async_copy(view, ref, self.sem)
        copy.start()
        copy.wait()


def lane_row(gains, row, n):
    return jnp.concatenate([gains[8 * i + row : 8 * i + row + 1, :] for i in range(n)], axis=1)


def allowed_pairs(lens, rows):
    place_i = lax.broadcasted_iota(jnp.int32, (rows, 1), 0)
    place_j = lax.broadcasted_iota(jnp.int32, (1, rows), 1)
    segment_i = jnp.zeros((rows, 1), jnp.int32)
    segment_j = jnp.zeros((1, rows), jnp.int32)
    total = 0
    for k in range(lens.shape[1]):
        total = total + lens[0, k]
        segment_i += (place_i >= total).astype(jnp.int32)
        segment_j += (place_j >= total).astype(jnp.int32)
    distance = place_i - place_j
    return (segment_i == segment_j) & (distance >= 0) & (distance < WINDOW)


def softmax_head(query, key, allowed):
    scores = dot_nt(query, key) * HD ** (-0.5)
    scores = jnp.where(allowed, scores, MASKED)
    weights = jnp.exp(scores - jnp.max(scores, axis=-1, keepdims=True))
    return weights / jnp.sum(weights, axis=-1, keepdims=True)


def inverse_root(rows):
    return lax.rsqrt(jnp.mean(rows * rows, axis=-1, keepdims=True) + NORM_EPS)


def feed_forward(x, g, wg, wu, wd):
    gate = dot_nn(x, wg)
    up = dot_nn(x, wu)
    grad_hidden = dot_nn(g, wd)
    root = (2.0 / jnp.pi) ** 0.5
    square = gate * gate
    tanh = jnp.tanh(root * gate * (1.0 + 0.044715 * square))
    half = 0.5 * (1.0 + tanh)
    gelu = gate * half
    slope = half + 0.5 * gate * (1.0 - tanh * tanh) * (root * (1.0 + 3 * 0.044715 * square))
    hidden = (gelu * up).astype(BF16)
    grad_gate = (grad_hidden * up * slope).astype(BF16)
    grad_up = (grad_hidden * gelu).astype(BF16)
    return hidden, grad_gate, grad_up


def row_block(n, buf, idx):
    step = buf.shape[0] // n
    return buf.at[pl.ds(pl.multiple_of(idx * step, step), step)]


def lanes_at(start, size):
    return pl.ds(pl.multiple_of(start, 128), size)


def first_kernel(
    n, counts, pumps,
    lens, tok, go, gains, wq, wkv, wo, wg, wu, wd,
    wg_all, wu_all, wd_all, x_all, g_all, wq_out, wkv_out, wo_out, gains_out,
    query_out, keyval_out, context_out, normed_out, middle_out, acts_out, dwg_out, dwu_out, dwd_out,
    send, recv, local, wq_all, wkv_all, wo_all, gains_all,
    group, kv_parts, branch, branch_c, branch_y, own_normed,
    w_part, x_tile, g_tile, acc_g, acc_u, acc_d,
):
    net = Net(n, send, recv)
    d, t = net.d, net.t
    quarter = wkv_all.shape[1]
    width = wg_all.shape[1]
    cut = acts_out.shape[2]
    rows, features = tok.shape

    def block(buf, idx):
        return row_block(n, buf, idx)

    wkv_own = wkv.at[:, lanes_at(t * quarter, quarter)]
    tokens_g = TensorGather(net, lambda i: group.at[i])
    kv_g = TensorGather(net, lambda i: kv_parts.at[i])
    branch_s = TensorScatter(net, branch, branch_c, branch_y)
    first_w = Spread(net, [wq_all, wkv_all, gains_all], block)
    second_w = Spread(net, [wo_all], block)
    spread_g = WideSpread(net, g_all)
    spread_x = WideSpread(net, x_all)
    deals = [
        Deal(
            net,
            lambda to, w=w, at=at: w.at[:, lanes_at(to * width + at, cut)],
            lambda frm, full=full, at=at: block(full, frm).at[:, pl.ds(at, cut)],
        )
        for at in range(0, width, cut)
        for w, full in ((wg, wg_all), (wu, wu_all), (wd, wd_all))
    ]
    assert net.used <= counts
    flow = Flow(deals)

    own_copies = [
        (tok, group.at[t]),
        (wq, block(wq_all, d)),
        (wkv_own, block(wkv_all, d)),
        (gains, block(gains_all, d)),
        (wo, block(wo_all, d)),
        (go, g_all.at[0, net.z]),
    ] + [
        (w.at[:, lanes_at(d * width, width)], block(full, d))
        for w, full in ((wg, wg_all), (wu, wu_all), (wd, wd_all))
    ]
    own_copies = [
        pltpu.make_async_copy(a, b, local.at[i]) for i, (a, b) in enumerate(own_copies)
    ]
    for copy in own_copies:
        copy.start()
    net.greet()

    for copy in own_copies[:4]:
        copy.wait()
    tokens_g.begin()
    first_w.begin()
    flow.pump(pumps[0])
    own_copies[4].wait()
    tokens_g.rest()
    second_w.begin()

    @pl.loop(1, net.nz)
    def _(h):
        first_w.hop(h)

        @pl.when(h > 1)
        def _():
            second_w.hop(h - 1)

    flow.pump(pumps[1])
    inputs = group[...].reshape(4 * rows, features).astype(F32)
    root = inverse_root(inputs)
    first_w.cross()
    second_w.hop(net.nz - 1)
    spread_g.begin(go)
    flow.pump(pumps[2])
    gain = lane_row(gains_all, 0, n)
    normed = (inputs * root * gain).astype(BF16)
    normed_out[...] = normed
    kv_parts[t] = dot_nn(normed, wkv_all[...]).astype(BF16)
    kv_g.begin()
    query_out[...] = dot_nn(normed, wq_all[...]).astype(BF16)
    spread_g.hop(1)
    kv_g.rest()
    for i in range(4):
        keyval_out[:, i * quarter : (i + 1) * quarter] = kv_parts[i]
    allowed = allowed_pairs(lens, 4 * rows)
    flow.pump(pumps[3])
    for h in range(query_out.shape[1] // HD):
        lanes = slice(h * HD, (h + 1) * HD)
        probs = softmax_head(query_out[:, lanes], keyval_out[:, :HD], allowed).astype(BF16)
        context_out[:, lanes] = dot_nn(probs, keyval_out[:, HD:]).astype(BF16)
    pl.loop(2, net.nz)(spread_g.hop)
    second_w.cross()
    branch[...] = dot_nt(context_out[...], wo_all[...]).astype(BF16).reshape(branch.shape)
    branch_s.begin()
    flow.pump(pumps[4])
    spread_g.cross()
    middle = group[t].astype(F32) + branch_s.rest()
    middle_out[...] = middle
    own_normed[...] = (middle * inverse_root(middle) * lane_row(gains_all, 1, n)).astype(BF16)
    own_x = pltpu.make_async_copy(own_normed, x_all.at[0, net.z], local.at[0])
    own_x.start()
    spread_x.begin(own_normed)
    flow.pump(pumps[5])
    outs = [
        pltpu.make_async_copy(a, b, local.at[1 + i])
        for i, (a, b) in enumerate(
            (
                (wq_all, wq_out),
                (wkv_all, wkv_out),
                (wo_all, wo_out),
                (gains_all, gains_out),
            )
        )
    ]
    for copy in outs:
        copy.start()
    own_copies[5].wait()
    own_x.wait()
    spread_x.hops()
    flow.pump(pumps[6])
    spread_x.core(0)
    spread_g.core(0)
    spread_x.cross()
    flow.pump(pumps[7])
    spread_x.core(1)
    spread_g.core(1)
    for x in range(2):
        spread_g.over(x)
        spread_g.core(2 + x)
    flow.pump(pumps[8])
    for slot in range(4):
        spread_g.core_done(slot)

    for i, (copy, deal, full) in enumerate(
        zip(own_copies[6:], deals[:3], (wg_all, wu_all, wd_all))
    ):
        copy.wait()
        deal.done()
        pltpu.make_async_copy(full.at[:, pl.ds(0, cut)], w_part.at[i], local.at[5 + i]).start()
    for acc in (acc_g, acc_u, acc_d):
        acc[...] = jnp.zeros_like(acc)
    for i, full in enumerate((wg_all, wu_all, wd_all)):
        pltpu.make_async_copy(full.at[:, pl.ds(0, cut)], w_part.at[i], local.at[5 + i]).wait()
    flow.pump(pumps[9])
    tile_blocks = x_tile.shape[0]
    tile = tile_blocks * rows

    @pl.loop(0, 8)
    def _(k):
        slot = k % 2 + 4 * ((k // 2) % 2) + 2 * (k // 4)
        for at, slot_from in ((2, 0), (3, 1), (6, 2), (7, 3)):

            @pl.when(k == at)
            def _():
                spread_x.core_done(slot_from)

        for at, x in ((4, 0), (5, 1)):

            @pl.when(k == at)
            def _():
                spread_x.over(x)
                spread_x.core(2 + x)

        @pl.loop(0, net.nz // tile_blocks)
        def _(sub):
            part = pl.ds(sub * tile_blocks, tile_blocks)
            loads = [
                pltpu.make_async_copy(a.at[slot, part], b, local.at[5 + i])
                for i, (a, b) in enumerate(((x_all, x_tile), (g_all, g_tile)))
            ]
            for load in loads:
                load.start()
            for load in loads:
                load.wait()
            x = x_tile[...].reshape(tile, features)
            g = g_tile[...].reshape(tile, features)
            hidden, grad_gate, grad_up = feed_forward(x, g, w_part[0], w_part[1], w_part[2])
            start = pl.multiple_of((slot * net.nz + sub * tile_blocks) * rows, tile)
            acts_out[0, pl.ds(start, tile), :] = hidden
            acts_out[1, pl.ds(start, tile), :] = grad_gate
            acts_out[2, pl.ds(start, tile), :] = grad_up
            acc_g[...] += dot_tn(x, grad_gate)
            acc_u[...] += dot_tn(x, grad_up)
            acc_d[...] += dot_tn(g, hidden)

    dwg_out[...] = acc_g[...].astype(BF16)
    dwu_out[...] = acc_u[...].astype(BF16)
    dwd_out[...] = acc_d[...].astype(BF16)
    flow.rest()
    for deal in deals[3:]:
        deal.done()
    for copy in outs:
        copy.wait()
    net.finish()


def second_kernel(
    n, counts, staged, pumps,
    lens, x_all, g_all, acts, wg_all, wu_all, wd_all, dwg, dwu, dwd,
    wq_all, wkv_all, wo_all, normed,
    tok, go, gains_all, query, keyval, context, middle,
    block_out, grad_tokens, grad_gains, grad_wq, grad_wkv, grad_wo, grad_wg, grad_wu, grad_wd,
    dx_c, dx_y, dx_x, dx_z, o_c, o_y, o_x, o_z,
    send, recv, local, stage, dw_part,
    acc, branch_rows, gkv, gkv_c, gkv_y, qpart, qpart_c, qpart_y,
    pq_x, pq_z, po_x, po_z, pk_x, pk_z, k_rows, acc_w, acc_k,
    gain_parts, gain_land, gain_sum, grad_query, own_grad,
):
    net = Net(n, send, recv)
    d, t = net.d, net.t
    nz = net.nz
    depth, heads = grad_wq.shape
    features, width = wg_all.shape
    cut = acts.shape[2]
    two = cut < width
    rows = tok.shape[0]
    quarter = wkv_all.shape[1]
    blocks = 256 // rows
    tile = blocks * rows
    subs = nz // blocks

    def block(buf, idx):
        return row_block(n, buf, idx)

    def own_of(buf):
        return lambda zb: block(buf, 2 * zb + net.x)

    def other_of(buf):
        return lambda zb: block(buf, 2 * zb + 1 - net.x)

    mem = Staged(stage, local.at[0]) if staged else Direct()
    scatter_dx = WideScatter(net, dx_c, dx_y, dx_x, dx_z, mem, subs)
    scatter_o = WideScatter(net, o_c, o_y, o_x, o_z, mem, subs)
    branch_g = TensorGather(net, lambda i: branch_rows.at[i])
    kv_s = TensorScatter(net, gkv, gkv_c, gkv_y)
    query_s = TensorScatter(net, qpart, qpart_c, qpart_y)
    kv_g = TensorGather(net, lambda i: k_rows.at[i])
    gain_deal = Deal(net, lambda to: gain_parts.at[to], lambda frm: gain_land.at[frm])
    gain_g = TensorGather(net, lambda i: gain_sum.at[i])
    outs = (grad_wg, grad_wu, grad_wd)
    deals = [
        Deal(
            net,
            lambda to, p=part: block(p, to),
            lambda frm, o=out: o.at[:, lanes_at(frm * width, cut)],
        )
        for part, out in zip((dwg, dwu, dwd), outs)
    ]
    if two:
        deals += [
            Deal(
                net,
                lambda to, i=i: block(dw_part.at[i], to),
                lambda frm, o=out: o.at[:, lanes_at(frm * width + cut, cut)],
            )
            for i, out in enumerate(outs)
        ]
    flow = Flow(deals[:3])
    late = Flow(deals[3:])
    copies = [
        pltpu.make_async_copy(deal.src(d), deal.dst(d), local.at[1 + i])
        for i, deal in enumerate(deals)
    ]
    for copy in copies[:3]:
        copy.start()
    net.greet()
    flow.pump(pumps[0])

    def ffn(wg_v, wu_v, wd_v, acc_g, acc_u, acc_d, x_tiles, g_tiles, o_stage, dx_stage):
        w_loads = [
            pltpu.make_async_copy(a, b, local.at[7 + i])
            for i, (a, b) in enumerate(((wg_all, wg_v), (wu_all, wu_v), (wd_all, wd_v)))
        ]
        for load in w_loads:
            load.start()

        def slot_of(k):
            step = k // subs
            core, y, x = 1 - (step // 2) % 2, 1 - step // 4, 1 - step % 2
            return core, y, x, k % subs

        def loads(k):
            core, y, x, sub = slot_of(k)
            slot = 4 * core + 2 * y + x
            part = pl.ds(sub * blocks, blocks)
            return [
                pltpu.make_async_copy(a.at[slot, part], b.at[k % 2], local.at[10 + 2 * i + k % 2])
                for i, (a, b) in enumerate(((x_all, x_tiles), (g_all, g_tiles)))
            ]

        for load in loads(0):
            load.start()
        if two:
            for total in (acc_g, acc_u, acc_d):
                total[...] = jnp.zeros_like(total)
        for load in w_loads:
            load.wait()

        @pl.loop(0, 8 * subs)
        def _(k):
            core, y, x, sub = slot_of(k)

            @pl.when(k + 1 < 8 * subs)
            def _():
                for load in loads(k + 1):
                    load.start()

            for load in loads(k):
                load.wait()
            start = pl.multiple_of(((4 * core + 2 * y + x) * nz + sub * blocks) * rows, tile)
            x_rows = x_tiles[k % 2].reshape(tile, features)
            g_rows = g_tiles[k % 2].reshape(tile, features)
            hidden, grad_gate, grad_up = (acts[i, pl.ds(start, tile), :] for i in range(3))
            if two:
                part = slice(cut, width)
                more = feed_forward(
                    x_rows, g_rows, wg_v[:, part], wu_v[:, part], wd_v[:, part]
                )
                acc_g[...] += dot_tn(x_rows, more[1])
                acc_u[...] += dot_tn(x_rows, more[2])
                acc_d[...] += dot_tn(g_rows, more[0])
                hidden, grad_gate, grad_up = (
                    jnp.concatenate(pair, axis=1)
                    for pair in zip((hidden, grad_gate, grad_up), more)
                )
            dx = dot_nt(grad_gate, wg_v[...]) + dot_nt(grad_up, wu_v[...])
            o = dot_nt(hidden, wd_v[...])

            @pl.when(k > 0)
            def _():
                core_before, y_before, x_before, sub_before = slot_of(k - 1)

                @pl.when(core_before == 1)
                def _():
                    scatter_dx.core_sent(2 * y_before + x_before, sub_before)
                    scatter_o.core_sent(2 * y_before + x_before, sub_before)

            @pl.when(core == 1)
            def _():
                dx_stage[...] = dx.astype(BF16).reshape(dx_stage.shape)
                scatter_dx.to_core(dx_stage, 2 * y + x, sub)
                o_stage[...] = o.astype(BF16).reshape(o_stage.shape)
                scatter_o.to_core(o_stage, 2 * y + x, sub)

            @pl.when(core == 0)
            def _():
                scatter_dx.keep(dx, 2 * y + x, sub)

                @pl.when(y == 1)
                def _():
                    @pl.loop(0, blocks)
                    def _(i):
                        scatter_dx.to_y(x, sub * blocks + blocks - 1 - i)

                scatter_o.keep(o, 2 * y + x, sub)

        if two:
            for i, total in enumerate((acc_g, acc_u, acc_d)):
                dw_part[i] = total[...].astype(BF16)

    whole = pltpu.VMEM((features, width), BF16)
    total = pltpu.VMEM((features, cut), F32)
    tiles = pltpu.VMEM((2, blocks, rows, features), BF16)
    one = pltpu.VMEM((blocks, rows, features), BF16)
    pl.run_scoped(ffn, whole, whole, whole, total, total, total, tiles, tiles, one, one)
    flow.pump(pumps[1])
    late.pump(pumps[2])
    if two:
        for copy in copies[3:]:
            copy.start()
    scatter_dx.over()
    late.pump(pumps[3])
    scatter_dx.lines()
    scatter_dx.total(acc)

    def attention(wq_v, wo_v, wkv_v, normed_v, pq, po, pk):
        scatter_q = Scatter(net, own_of(pq), other_of(pq), pq_x, pq_z, Direct())
        scatter_w = Scatter(net, own_of(po), other_of(po), po_x, po_z, Direct())
        scatter_k = Scatter(net, own_of(pk), other_of(pk), pk_x, pk_z, Direct())
        assert net.used <= counts
        ends = net.ends[-3:]
        del net.ends[-3:]
        attn_loads = [
            pltpu.make_async_copy(a, b, local.at[7 + i])
            for i, (a, b) in enumerate(
                ((wq_all, wq_v), (wo_all, wo_v), (wkv_all, wkv_v), (normed, normed_v))
            )
        ]
        for load in attn_loads:
            load.start()
        rows_in = middle[...]
        root = inverse_root(rows_in)
        grad_normed = acc[...]
        gain = lane_row(gains_all, 1, n)
        scaled = grad_normed * gain
        inner = jnp.mean(scaled * rows_in, axis=-1, keepdims=True)
        grad_middle = go[...].astype(F32) + root * (scaled - rows_in * (root * root) * inner)
        own_grad[...] = grad_middle
        gain_ffn = jnp.sum(grad_normed * rows_in * root, axis=0, keepdims=True)
        branch_rows[t] = grad_middle.astype(BF16)
        branch_g.begin()
        late.pump(pumps[4])
        for load in attn_loads:
            load.wait()
        branch_g.rest()
        scatter_o.all_to_y(1)
        grad_branch = branch_rows[...].reshape(4 * rows, features)
        chunk = 512
        for i in range(features // chunk):
            part = slice(i * chunk, (i + 1) * chunk)
            po[part, :] = dot_tn(grad_branch[:, part], context[...]).astype(BF16)
        scatter_w.begin()
        grad_context = dot_nn(grad_branch, wo_v[...]).astype(BF16)
        late.pump(pumps[5])

        allowed = allowed_pairs(lens, 4 * rows)
        key, value = keyval[:, :HD], keyval[:, HD:]
        grad_key = jnp.zeros((4 * rows, HD), F32)
        grad_value = jnp.zeros((4 * rows, HD), F32)
        factor = HD ** (-0.5)
        for h in range(heads // HD):
            lanes = slice(h * HD, (h + 1) * HD)
            probs = softmax_head(query[:, lanes], key, allowed)
            grad_head = grad_context[:, lanes]
            grad_probs = dot_nt(grad_head, value)
            inner = jnp.sum(grad_probs * probs, axis=-1, keepdims=True)
            grad_scores = (probs * (grad_probs - inner)).astype(BF16)
            grad_query[:, lanes] = (dot_nn(grad_scores, key) * factor).astype(BF16)
            grad_key += dot_tn(grad_scores, query[:, lanes]) * factor
            grad_value += dot_tn(probs.astype(BF16), grad_head)
        both = jnp.concatenate([grad_key, grad_value], axis=1).astype(BF16)
        for i in range(4):
            gkv[i] = both[:, i * quarter : (i + 1) * quarter]
        kv_s.begin()
        for i in range(features // chunk):
            part = slice(i * chunk, (i + 1) * chunk)
            pq[part, :] = dot_tn(normed_v[:, part], grad_query[...]).astype(BF16)
        scatter_q.begin()
        grad_kv = kv_s.rest().astype(BF16)
        term = dot_nt(grad_query[...], wq_v[...]) + dot_nt(grad_kv, wkv_v[...])
        qpart[...] = term.astype(BF16).reshape(qpart.shape)
        query_s.begin()
        for i in range(features // chunk):
            part = slice(i * chunk, (i + 1) * chunk)
            pk[part, :] = dot_tn(normed_v[:, part], grad_kv).astype(BF16)
        scatter_k.begin()
        late.pump(pumps[6])
        scatter_w.lines()
        scatter_o.all_to_y(0)
        scatter_q.lines()
        grad_normed = query_s.rest()

        rows_in = tok[...].astype(F32)
        root = inverse_root(rows_in)
        gain = lane_row(gains_all, 0, n)
        scaled = grad_normed * gain
        inner = jnp.mean(scaled * rows_in, axis=-1, keepdims=True)
        grad_tokens[...] = own_grad[...] + root * (scaled - rows_in * (root * root) * inner)
        gain_attn = jnp.sum(grad_normed * rows_in * root, axis=0, keepdims=True)
        for i in range(n):
            lanes = slice(i * depth, (i + 1) * depth)
            gain_parts[i, 0:1, :] = gain_attn[:, lanes]
            gain_parts[i, 1:2, :] = gain_ffn[:, lanes]
            gain_parts[i, 2:8, :] = jnp.zeros((6, depth), F32)
        gain_deal.begin()
        late.pump(pumps[7])
        scatter_k.lines()
        scatter_o.over()
        gain_land[d] = gain_parts[d]
        gain_deal.done()
        gain_sum[t] = jnp.sum(gain_land[...], axis=0)
        gain_g.begin()
        scatter_k.total(acc_k)
        k_rows[t] = acc_k[...]
        kv_g.begin()
        late.rest()
        scatter_o.lines()
        scatter_w.total(acc_w)
        grad_wo[...] = acc_w[...]
        scatter_q.total(acc_w)
        grad_wq[...] = acc_w[...]
        gain_g.rest()
        grad_gains[...] = jnp.sum(gain_sum[...], axis=0)
        kv_g.rest()
        for i in range(4):
            grad_wkv[:, i * quarter : (i + 1) * quarter] = k_rows[i]
        scatter_o.total(acc)
        block_out[...] = (middle[...] + acc[...]).astype(BF16)
        for end in ends:
            end()

    flow.rest()
    projection = pltpu.VMEM((features, heads), BF16)
    part = pltpu.VMEM((features, quarter), BF16)
    pl.run_scoped(
        attention, projection, projection, part, pltpu.VMEM((4 * rows, features), BF16),
        projection, projection, part,
    )
    for deal in deals:
        deal.done()
    for copy in copies:
        copy.wait()
    net.finish()


def params(collective_id):
    return pltpu.CompilerParams(
        collective_id=collective_id, has_side_effects=True, vmem_limit_bytes=63 * MIB
    )


PUMPS_1 = (0.12, 0.1, 0.1, 0.1, 0.06, 0.1, 0.1, 0.1, 0.1, 0.12)
PUMPS_2 = (1.0, 0.0, 0.2, 0.2, 0.1, 0.1, 0.2, 0.2)


def body(
    n, tokens, grad_out, lengths, gain_attn, gain_ffn, w_query, w_keyval, w_out, w_gate, w_up, w_down
):
    nz = n // 2
    rows, features = tokens.shape
    depth, heads = w_query.shape
    quarter = w_keyval.shape[1] // 4
    width = w_gate.shape[1] // n
    group_rows = 4 * rows
    shape = jax.ShapeDtypeStruct
    gains = jnp.concatenate(
        [gain_attn[None], gain_ffn[None], jnp.zeros((6, depth), gain_attn.dtype)]
    ).astype(F32)

    cut = width // 2 if width // 2 % 128 == 0 else width
    parts = width // cut
    tile_blocks = 256 // rows
    counts = 9 + 4 * 3 * nz + 2 * (5 * nz + 4) + 3 * parts * n
    full = shape((features, width), BF16)
    part = shape((features, cut), BF16)
    wide = shape((8, nz, rows, features), BF16)
    all_rows = 4 * n * rows
    (
        wg_all, wu_all, wd_all, x_all, g_all, wq_all, wkv_all, wo_all, gains_all,
        query, keyval, context, normed, middle, acts, dwg, dwu, dwd,
    ) = pl.pallas_call(
        functools.partial(first_kernel, n, counts, PUMPS_1),
        out_shape=(
            full, full, full, wide, wide,
            shape((features, heads), BF16),
            shape((features, quarter), BF16),
            shape((features, heads), BF16),
            shape((8 * n, depth), F32),
            shape((group_rows, heads), BF16),
            shape((group_rows, 2 * HD), BF16),
            shape((group_rows, heads), BF16),
            shape((group_rows, features), BF16),
            shape((rows, features), F32),
            shape((3, all_rows, cut), BF16),
            part, part, part,
        ),
        in_specs=[SMEM] + [ANY] * 9,
        out_specs=(ANY,) * 9 + (VMEM,) * 9,
        scratch_shapes=[
            pltpu.SemaphoreType.DMA((counts,)),
            pltpu.SemaphoreType.DMA((counts,)),
            pltpu.SemaphoreType.DMA((9,)),
            pltpu.VMEM((features, heads), BF16),
            pltpu.VMEM((features, quarter), BF16),
            pltpu.VMEM((features, heads), BF16),
            pltpu.VMEM((8 * n, depth), F32),
            pltpu.VMEM((4, rows, features), BF16),
            pltpu.VMEM((4, group_rows, quarter), BF16),
            pltpu.VMEM((4, rows, features), BF16),
            pltpu.VMEM((2, rows, features), BF16),
            pltpu.VMEM((rows, features), BF16),
            pltpu.VMEM((rows, features), BF16),
            pltpu.VMEM((3, features, cut), BF16),
            pltpu.VMEM((tile_blocks, rows, features), BF16),
            pltpu.VMEM((tile_blocks, rows, features), BF16),
        ]
        + [pltpu.VMEM((features, cut), F32)] * 3,
        compiler_params=params(0),
        name="forward",
    )(lengths, tokens, grad_out, gains, w_query, w_keyval, w_out, w_gate, w_up, w_down)

    staged = n > 8
    subs = nz // tile_blocks
    counts = 2 * (4 * subs + 5 * nz) + 3 * 3 * nz + 15 + n + 3 * parts * n
    landing = [
        shape((4, nz, rows, features), BF16),
        shape((2, nz, rows, features), BF16),
        shape((nz, rows, features), BF16),
        shape((nz + 1, rows, features), BF16),
    ] * 2
    out_shape = [
        shape((rows, features), BF16),
        shape((rows, features), F32),
        shape((8, depth), F32),
        shape((depth, heads), F32),
        shape((depth, 4 * quarter), F32),
        shape((depth, heads), F32),
        shape((depth, n * width), BF16),
        shape((depth, n * width), BF16),
        shape((depth, n * width), BF16),
    ]
    out_specs = [VMEM] * 6 + [ANY] * 3
    in_vmem = []
    if staged:
        out_shape += landing
        out_specs += [ANY] * len(landing)
    else:
        in_vmem = [pltpu.VMEM(place.shape, place.dtype) for place in landing]

    def reduced(columns):
        return [
            pltpu.VMEM((nz, depth, columns), BF16),
            pltpu.VMEM((nz + 1, depth, columns), BF16),
        ]

    results = pl.pallas_call(
        functools.partial(second_kernel, n, counts, staged, PUMPS_2),
        out_shape=tuple(out_shape),
        in_specs=[SMEM, ANY, ANY, VMEM] + [ANY] * 10 + [VMEM] * 7,
        out_specs=tuple(out_specs),
        scratch_shapes=in_vmem
        + [
            pltpu.SemaphoreType.DMA((counts,)),
            pltpu.SemaphoreType.DMA((counts,)),
            pltpu.SemaphoreType.DMA((14,)),
            pltpu.VMEM((tile_blocks if staged else 1, rows, features), BF16),
            pltpu.VMEM((3, features, cut if parts > 1 else 128), BF16),
            pltpu.VMEM((rows, features), F32),
            pltpu.VMEM((4, rows, features), BF16),
            pltpu.VMEM((4, group_rows, quarter), BF16),
            pltpu.VMEM((2, group_rows, quarter), BF16),
            pltpu.VMEM((group_rows, quarter), BF16),
            pltpu.VMEM((4, rows, features), BF16),
            pltpu.VMEM((2, rows, features), BF16),
            pltpu.VMEM((rows, features), BF16),
        ]
        + reduced(heads)
        + reduced(heads)
        + reduced(quarter)
        + [
            pltpu.VMEM((4, depth, quarter), F32),
            pltpu.VMEM((depth, heads), F32),
            pltpu.VMEM((depth, quarter), F32),
            pltpu.VMEM((n, 8, depth), F32),
            pltpu.VMEM((n, 8, depth), F32),
            pltpu.VMEM((4, 8, depth), F32),
            pltpu.VMEM((group_rows, heads), BF16),
            pltpu.VMEM((rows, features), F32),
        ],
        compiler_params=params(1),
        name="backward",
    )(
        lengths, x_all, g_all, acts, wg_all, wu_all, wd_all, dwg, dwu, dwd,
        wq_all, wkv_all, wo_all, normed,
        tokens, grad_out, gains_all, query, keyval, context, middle,
    )
    block_out, grad_tokens, grad_gains, grad_wq, grad_wkv, grad_wo, grad_wg, grad_wu, grad_wd = (
        results[:9]
    )
    return (
        block_out,
        grad_tokens,
        grad_gains[0],
        grad_gains[1],
        grad_wq,
        grad_wkv,
        grad_wo,
        grad_wg.astype(F32),
        grad_wu.astype(F32),
        grad_wd.astype(F32),
    )


def solution(mesh):
    rows = P(("dp", "tensor"), None)
    both = P("dp", "tensor")
    return jax.shard_map(
        functools.partial(body, mesh.shape["dp"]),
        mesh=mesh,
        in_specs=(rows, rows, P("dp", None), P("dp"), P("dp"), both, P("dp", None), both, both, both, both),
        out_specs=(rows, rows, P("dp"), P("dp"), both, P("dp", None), both, both, both, both),
        check_vma=False,
    )
```

```python
import functools

import jax
import jax.numpy as jnp
from jax import lax
from jax.experimental import pallas as pl
from jax.experimental.pallas import tpu as pltpu
from jax.sharding import PartitionSpec as P

HD = 256
WINDOW = 2048
NORM_EPS = 1e-06
MASKED = -1e30
BF16, F32 = jnp.bfloat16, jnp.float32
MESH = pl.DeviceIdType.MESH
ANY = pl.BlockSpec(memory_space=pl.ANY)
VMEM = pl.BlockSpec(memory_space=pltpu.VMEM)
SMEM = pl.BlockSpec(memory_space=pltpu.SMEM)
MIB = 1 << 20


def dot_nn(a, b):
    return lax.dot_general(a, b, (((1,), (0,)), ((), ())), preferred_element_type=F32)


def dot_nt(a, b):
    return lax.dot_general(a, b, (((1,), (1,)), ((), ())), preferred_element_type=F32)


def dot_tn(a, b):
    return lax.dot_general(a, b, (((0,), (0,)), ((), ())), preferred_element_type=F32)


class Net:
    def __init__(self, n, send, recv):
        self.n, self.nz = n, n // 2
        self.send, self.recv, self.used = send, recv, 0
        self.d = lax.axis_index("dp")
        self.t = lax.axis_index("tensor")
        self.z = self.d // 2
        self.x = self.d % 2
        self.dx = self.d + 1 - 2 * self.x
        self.ty = (self.t + 2) % 4
        self.tc = self.t + 1 - 2 * (self.t % 2)
        self.tcy = (self.tc + 2) % 4
        self.ends = []

    def take(self, count):
        first = self.used
        self.used += count
        return first

    def dp(self, other):
        return (other, self.t)

    def tensor(self, other):
        return (self.d, other)

    def make(self, src, dst, k, device):
        return pltpu.make_async_remote_copy(
            src_ref=src,
            dst_ref=dst,
            send_sem=self.send.at[k],
            recv_sem=self.recv.at[k],
            device_id=device,
            device_id_type=MESH,
        )

    def start(self, src, dst, k, device):
        self.make(src, dst, k, device).start()

    def landed(self, ref, k):
        self.make(ref, ref, k, self.tensor(self.tc)).wait_recv()

    def sent(self, ref, k):
        self.make(ref, ref, k, self.tensor(self.tc)).wait_send()

    def greet(self):
        barrier = pltpu.get_barrier_semaphore()

        @pl.loop(1, self.n)
        def _(m):
            pl.semaphore_signal(
                barrier, inc=1, device_id=self.dp((self.d + m) % self.n), device_id_type=MESH
            )

        for other in (self.ty, self.tc):
            pl.semaphore_signal(
                barrier, inc=1, device_id=self.tensor(other), device_id_type=MESH
            )
        pl.semaphore_wait(barrier, self.n + 1)

    def finish(self):
        for end in self.ends:
            end()


class TensorGather:
    def __init__(self, net, at):
        self.net, self.at, self.k = net, at, net.take(3)
        net.ends.append(self.end)

    def begin(self):
        net = self.net
        net.start(self.at(net.t), self.at(net.t), self.k, net.tensor(net.ty))
        net.start(self.at(net.t), self.at(net.t), self.k + 1, net.tensor(net.tc))

    def rest(self):
        net = self.net
        net.landed(self.at(net.ty), self.k)
        net.start(self.at(net.ty), self.at(net.ty), self.k + 2, net.tensor(net.tc))
        net.landed(self.at(net.tc), self.k + 1)
        net.landed(self.at(net.tcy), self.k + 2)

    def end(self):
        for i in range(3):
            self.net.sent(self.at(0), self.k + i)


class TensorScatter:
    def __init__(self, net, part, cl, yl):
        self.net, self.part, self.cl, self.yl, self.k = net, part, cl, yl, net.take(3)
        net.ends.append(self.end)

    def begin(self):
        net = self.net
        net.start(self.part.at[net.tcy], self.cl.at[1], self.k + 1, net.tensor(net.tc))
        net.start(self.part.at[net.tc], self.cl.at[0], self.k, net.tensor(net.tc))

    def rest(self):
        net = self.net
        net.landed(self.cl.at[1], self.k + 1)
        pair = self.part[net.ty].astype(F32) + self.cl[1].astype(F32)
        self.part[net.ty] = pair.astype(self.part.dtype)
        net.start(self.part.at[net.ty], self.yl, self.k + 2, net.tensor(net.ty))
        net.landed(self.cl.at[0], self.k)
        own = self.part[net.t].astype(F32) + self.cl[0].astype(F32)
        net.landed(self.yl, self.k + 2)
        return own + self.yl[...].astype(F32)

    def end(self):
        for i in range(3):
            self.net.sent(self.yl, self.k + i)


class Spread:
    def __init__(self, net, bufs, block):
        self.net, self.bufs, self.block = net, bufs, block
        self.zk = [net.take(2 * net.nz) for _ in bufs]
        self.xk = [net.take(net.nz) for _ in bufs]
        net.ends.append(self.end)

    def line(self, j, zb, right):
        net = self.net
        here = self.block(self.bufs[j], 2 * zb + net.x)
        if right:
            net.start(here, here, self.zk[j] + zb, net.dp(net.d + 2))
        else:
            net.start(here, here, self.zk[j] + net.nz + zb, net.dp(net.d - 2))

    def over_x(self, j, zb):
        net = self.net
        here = self.block(self.bufs[j], 2 * zb + net.x)
        net.start(here, here, self.xk[j] + zb, net.dp(net.dx))

    def begin(self):
        net = self.net
        for j in range(len(self.bufs)):

            @pl.when(net.z < net.nz - 1)
            def _():
                self.line(j, net.z, True)

            @pl.when(net.z > 0)
            def _():
                self.line(j, net.z, False)

            self.over_x(j, net.z)

    def hop(self, h):
        net = self.net
        nz = net.nz
        for j, buf in enumerate(self.bufs):

            @pl.when(net.z - h >= 0)
            def _():
                zb = net.z - h
                net.landed(self.block(buf, 2 * zb + net.x), self.zk[j] + zb)

                @pl.when(net.z < nz - 1)
                def _():
                    self.line(j, zb, True)

                self.over_x(j, zb)

            @pl.when(net.z + h <= nz - 1)
            def _():
                zb = net.z + h
                net.landed(self.block(buf, 2 * zb + net.x), self.zk[j] + nz + zb)

                @pl.when(net.z > 0)
                def _():
                    self.line(j, zb, False)

                self.over_x(j, zb)

    def cross(self):
        net = self.net

        @pl.loop(0, net.nz)
        def _(k):
            zb = (net.z + k) % net.nz
            for j, buf in enumerate(self.bufs):
                net.landed(self.block(buf, 2 * zb + 1 - net.x), self.xk[j] + zb)

    def end(self):
        net = self.net

        @pl.loop(0, net.nz)
        def _(zb):
            for j, buf in enumerate(self.bufs):
                some = self.block(buf, 0)

                @pl.when((zb <= net.z) & (net.z < net.nz - 1))
                def _():
                    net.sent(some, self.zk[j] + zb)

                @pl.when((zb >= net.z) & (net.z > 0))
                def _():
                    net.sent(some, self.zk[j] + net.nz + zb)

                net.sent(some, self.xk[j] + zb)


class WideSpread:
    def __init__(self, net, buf, late_x=False):
        self.net, self.buf, self.late_x = net, buf, late_x
        self.zk, self.xk = net.take(2 * net.nz), net.take(net.nz)
        self.yk, self.ck = net.take(2 * net.nz), net.take(4)
        net.ends.append(self.end)

    def onward(self, src, zb, right, left):
        net, buf = self.net, self.buf
        if right:

            @pl.when(net.z < net.nz - 1)
            def _():
                net.start(src, buf.at[0, zb], self.zk + zb, net.dp(net.d + 2))

        if left:

            @pl.when(net.z > 0)
            def _():
                net.start(src, buf.at[0, zb], self.zk + net.nz + zb, net.dp(net.d - 2))

        net.start(src, buf.at[2, zb], self.yk + zb, net.tensor(net.ty))
        if not self.late_x:
            net.start(src, buf.at[1, zb], self.xk + zb, net.dp(net.dx))

    def send_x(self):
        net = self.net

        @pl.loop(0, net.nz)
        def _(k):
            zb = (net.z + k) % net.nz
            net.start(self.buf.at[0, zb], self.buf.at[1, zb], self.xk + zb, net.dp(net.dx))

    def begin(self, own):
        self.onward(own, self.net.z, True, True)

    def hop(self, h):
        net, buf = self.net, self.buf

        @pl.when(net.z - h >= 0)
        def _():
            zb = net.z - h
            net.landed(buf.at[0, zb], self.zk + zb)
            self.onward(buf.at[0, zb], zb, True, False)

        @pl.when(net.z + h <= net.nz - 1)
        def _():
            zb = net.z + h
            net.landed(buf.at[0, zb], self.zk + net.nz + zb)
            self.onward(buf.at[0, zb], zb, False, True)

    def hops(self):
        @pl.loop(1, self.net.nz)
        def _(h):
            self.hop(h)

    def cross(self):
        net, buf = self.net, self.buf

        @pl.loop(0, net.nz)
        def _(k):
            zb = (net.z + k) % net.nz
            net.landed(buf.at[1, zb], self.xk + zb)
            net.start(buf.at[1, zb], buf.at[3, zb], self.yk + net.nz + zb, net.tensor(net.ty))

    def over(self, x):
        net = self.net

        @pl.loop(0, net.nz)
        def _(k):
            zb = (net.z + k) % net.nz
            net.landed(self.buf.at[2 + x, zb], self.yk + x * net.nz + zb)

    def core(self, slot):
        net = self.net
        net.start(self.buf.at[slot], self.buf.at[4 + slot], self.ck + slot, net.tensor(net.tc))

    def core_done(self, slot):
        self.net.landed(self.buf.at[4 + slot], self.ck + slot)

    def end(self):
        net = self.net
        some = self.buf.at[0, 0]

        @pl.loop(0, net.nz)
        def _(zb):
            @pl.when((zb <= net.z) & (net.z < net.nz - 1))
            def _():
                net.sent(some, self.zk + zb)

            @pl.when((zb >= net.z) & (net.z > 0))
            def _():
                net.sent(some, self.zk + net.nz + zb)

            net.sent(some, self.xk + zb)
            net.sent(some, self.yk + zb)
            net.sent(some, self.yk + net.nz + zb)

        for slot in range(4):
            net.sent(self.buf.at[0], self.ck + slot)


class Deal:
    def __init__(self, net, src, dst):
        self.net, self.src, self.dst, self.k = net, src, dst, net.take(net.n)
        net.ends.append(self.end)

    def send(self, m):
        net = self.net
        to = (net.d + m) % net.n
        net.start(self.src(to), self.dst(net.d), self.k + m, net.dp(to))

    def begin(self):
        pl.loop(1, self.net.n)(self.send)

    def done(self):
        net = self.net

        @pl.loop(1, net.n)
        def _(m):
            net.landed(self.dst((net.d - m + net.n) % net.n), self.k + m)

    def end(self):
        net = self.net

        @pl.loop(1, net.n)
        def _(m):
            net.sent(self.src(0), self.k + m)


class Flow:
    def __init__(self, n, groups, even_first):
        self.todo = []
        for deals in groups:
            for parity in (0, 1) if even_first else (1, 0):
                self.todo += [(deal, m) for deal in deals for m in range(1, n) if m % 2 == parity]
        self.gone, self.share = 0, 0.0

    def pump(self, share, limit=None):
        self.share += share
        upto = min(round(self.share * len(self.todo)), len(self.todo) if limit is None else limit)
        for deal, m in self.todo[self.gone : upto]:
            deal.send(m)
        self.gone = max(upto, self.gone)

    def rest(self):
        self.pump(1.0)


class Columns:
    def __init__(self, net, parts, land):
        self.net, self.parts, self.land = net, parts, land
        self.deal = Deal(net, lambda to: parts.at[to], lambda frm: land.at[net.t, frm])
        self.over = TensorGather(net, lambda i: land.at[i])

    def begin(self, rows):
        depth = self.parts.shape[2]
        for i in range(self.net.n):
            self.parts[i] = rows[:, i * depth : (i + 1) * depth]
        self.land[self.net.t, self.net.d] = self.parts[self.net.d]
        self.deal.begin()

    def gather(self):
        self.deal.done()
        self.over.begin()

    def rest(self):
        self.over.rest()

    def times(self, other, acc):
        n = self.net.n
        depth = self.parts.shape[2]
        acc[...] = jnp.zeros_like(acc)

        @pl.loop(0, n)
        def _(i):
            mine = self.land[:, i].reshape(-1, depth)
            acc[...] += dot_tn(mine, row_block(n, other, i)[...])


class Scatter:
    def __init__(self, net, own, other, xl, zl, mem):
        self.net, self.own, self.other, self.xl, self.zl, self.mem = net, own, other, xl, zl, mem
        self.xk, self.rk, self.lk = net.take(net.nz), net.take(net.nz), net.take(net.nz)
        net.ends.append(self.end)

    def order(self, k):
        odd = k % 2
        return odd * (k // 2) + (1 - odd) * (self.net.nz - 1 - k // 2)

    def send_x(self, zb):
        net = self.net
        net.start(self.other(zb), self.xl.at[zb], self.xk + zb, net.dp(net.dx))

    def begin(self):
        @pl.loop(0, self.net.nz)
        def _(k):
            self.send_x(self.order(k))

    def add(self, block, other):
        mem = self.mem
        mem.put(block, (mem.get(block).astype(F32) + mem.get(other).astype(F32)).astype(BF16))

    def meet(self, zb):
        net = self.net
        net.landed(self.xl.at[zb], self.xk + zb)
        self.add(self.own(zb), self.xl.at[zb])

    def line_step(self, k):
        net = self.net
        nz = net.nz
        far = nz - 1 - k

        @pl.when(far > net.z)
        def _():
            self.meet(far)
            here = self.own(far)

            @pl.when(net.z > 0)
            def _():
                net.landed(self.zl.at[far], self.rk + far)
                self.add(here, self.zl.at[far])

            net.start(here, self.zl.at[far], self.rk + far, net.dp(net.d + 2))

        @pl.when(k < net.z)
        def _():
            self.meet(k)
            here = self.own(k)

            @pl.when(net.z < nz - 1)
            def _():
                net.landed(self.zl.at[k], self.lk + k)
                self.add(here, self.zl.at[k])

            last = (k == net.z - 1).astype(jnp.int32)
            net.start(here, self.zl.at[last * nz + (1 - last) * k], self.lk + k, net.dp(net.d - 2))

    def lines(self):
        pl.loop(0, self.net.nz - 1)(self.line_step)
        self.meet(self.net.z)

    def total(self, acc):
        net, mem = self.net, self.mem
        acc[...] = mem.get(self.own(net.z)).astype(F32)

        @pl.when(net.z > 0)
        def _():
            net.landed(self.zl.at[net.z], self.rk + net.z)
            acc[...] += mem.get(self.zl.at[net.z]).astype(F32)

        @pl.when(net.z < net.nz - 1)
        def _():
            net.landed(self.zl.at[net.nz], self.lk + net.z)
            acc[...] += mem.get(self.zl.at[net.nz]).astype(F32)

    def end(self):
        net = self.net

        @pl.loop(0, net.nz)
        def _(zb):
            net.sent(self.xl.at[0], self.xk + zb)

            @pl.when(zb > net.z)
            def _():
                net.sent(self.zl.at[0], self.rk + zb)

            @pl.when(zb < net.z)
            def _():
                net.sent(self.zl.at[0], self.lk + zb)


class WideScatter(Scatter):
    def __init__(self, net, cl, yl, xl, zl, mem, tiles):
        self.cl, self.yl, self.tiles = cl, yl, tiles
        self.ck, self.yk = net.take(4 * tiles), net.take(2 * net.nz)
        super().__init__(net, lambda zb: cl.at[0, zb], lambda zb: cl.at[1, zb], xl, zl, mem)
        net.ends.append(self.wide_end)

    def place(self, yx, sub):
        blocks = self.net.nz // self.tiles
        return self.cl.at[yx, pl.ds(sub * blocks, blocks)]

    def to_core(self, stage, yx, sub):
        net = self.net
        net.start(stage, self.place(yx, sub), self.ck + yx * self.tiles + sub, net.tensor(net.tc))

    def core_sent(self, yx, sub):
        self.net.sent(self.place(0, 0), self.ck + yx * self.tiles + sub)

    def keep(self, value, yx, sub):
        place = self.place(yx, sub)
        self.net.landed(place, self.ck + yx * self.tiles + sub)
        value = value.reshape(place.shape) + self.mem.get(place).astype(F32)
        self.mem.put(place, value.astype(BF16))

    def to_y(self, x, zb):
        net = self.net
        net.start(
            self.cl.at[2 + x, zb], self.yl.at[x, zb], self.yk + x * net.nz + zb, net.tensor(net.ty)
        )

    def all_to_y(self, x):
        @pl.loop(0, self.net.nz)
        def _(k):
            self.to_y(x, self.order(k))

    def from_y(self, x, zb):
        net = self.net
        net.landed(self.yl.at[x, zb], self.yk + x * net.nz + zb)
        self.add(self.cl.at[x, zb], self.yl.at[x, zb])

    def over(self):
        @pl.loop(0, self.net.nz)
        def _(k):
            zb = self.order(k)
            self.from_y(1, zb)
            self.send_x(zb)

    def meet(self, zb):
        self.from_y(0, zb)
        super().meet(zb)

    def wide_end(self):
        net = self.net

        @pl.loop(0, net.nz)
        def _(zb):
            net.sent(self.yl.at[0, 0], self.yk + zb)
            net.sent(self.yl.at[0, 0], self.yk + net.nz + zb)


class Direct:
    def get(self, ref):
        return ref[...]

    def put(self, ref, value):
        ref[...] = value


class Staged:
    def __init__(self, buf, sem):
        self.buf, self.sem = buf, sem

    def view(self, ref):
        return self.buf if len(ref.shape) == 3 else self.buf.at[0]

    def get(self, ref):
        view = self.view(ref)
        copy = pltpu.make_async_copy(ref, view, self.sem)
        copy.start()
        copy.wait()
        return view[...]

    def put(self, ref, value):
        view = self.view(ref)
        view[...] = value
        copy = pltpu.make_async_copy(view, ref, self.sem)
        copy.start()
        copy.wait()


def lane_row(gains, row, n):
    return jnp.concatenate([gains[8 * i + row : 8 * i + row + 1, :] for i in range(n)], axis=1)


def allowed_pairs(lens, rows):
    place_i = lax.broadcasted_iota(jnp.int32, (rows, 1), 0)
    place_j = lax.broadcasted_iota(jnp.int32, (1, rows), 1)
    segment_i = jnp.zeros((rows, 1), jnp.int32)
    segment_j = jnp.zeros((1, rows), jnp.int32)
    total = 0
    for k in range(lens.shape[1]):
        total = total + lens[0, k]
        segment_i += (place_i >= total).astype(jnp.int32)
        segment_j += (place_j >= total).astype(jnp.int32)
    distance = place_i - place_j
    return (segment_i == segment_j) & (distance >= 0) & (distance < WINDOW)


def softmax_head(query, key, allowed):
    scores = dot_nt(query, key) * HD ** (-0.5)
    scores = jnp.where(allowed, scores, MASKED)
    weights = jnp.exp(scores - jnp.max(scores, axis=-1, keepdims=True))
    return weights / jnp.sum(weights, axis=-1, keepdims=True)


def inverse_root(rows):
    return lax.rsqrt(jnp.mean(rows * rows, axis=-1, keepdims=True) + NORM_EPS)


def feed_forward(x, g, wg, wu, wd):
    gate = dot_nn(x, wg)
    up = dot_nn(x, wu)
    grad_hidden = dot_nn(g, wd)
    root = (2.0 / jnp.pi) ** 0.5
    square = gate * gate
    tanh = jnp.tanh(root * gate * (1.0 + 0.044715 * square))
    half = 0.5 * (1.0 + tanh)
    gelu = gate * half
    slope = half + 0.5 * gate * (1.0 - tanh * tanh) * (root * (1.0 + 3 * 0.044715 * square))
    hidden = (gelu * up).astype(BF16)
    grad_gate = (grad_hidden * up * slope).astype(BF16)
    grad_up = (grad_hidden * gelu).astype(BF16)
    return hidden, grad_gate, grad_up


def row_block(n, buf, idx):
    step = buf.shape[0] // n
    return buf.at[pl.ds(pl.multiple_of(idx * step, step), step)]


def lanes_at(start, size):
    return pl.ds(pl.multiple_of(start, 128), size)


def weight_blocks(columns, acts, cols):
    x_cols, g_cols = columns
    return (
        dot_tn(x_cols, acts[1, :, cols]),
        dot_tn(x_cols, acts[2, :, cols]),
        dot_tn(g_cols, acts[0, :, cols]),
    )


def by_columns(x_all, g_all, x_cols, g_cols, sems, use):
    features = x_all.shape[3]
    chunk = x_cols.shape[4]
    count = features // chunk

    def loads(c):
        lanes = lanes_at(c * chunk, chunk)
        return [
            pltpu.make_async_copy(a.at[:, :, :, lanes], b.at[c % 2], sems.at[2 * i + c % 2])
            for i, (a, b) in enumerate(((x_all, x_cols), (g_all, g_cols)))
        ]

    for load in loads(0):
        load.start()

    @pl.loop(0, count)
    def _(c):
        @pl.when(c + 1 < count)
        def _():
            for load in loads(c + 1):
                load.start()

        for load in loads(c):
            load.wait()
        use(pl.multiple_of(c * chunk, chunk), [b[c % 2].reshape(-1, chunk) for b in (x_cols, g_cols)])


def first_kernel(
    n, counts, pumps,
    lens, tok, go, gains, wq, wkv, wo, wg, wu, wd,
    wg_all, wu_all, wd_all, x_all, g_all, wq_out, wkv_out, wo_out, gains_out,
    query_out, keyval_out, context_out, normed_out, middle_out, acts_out, dwg_out, dwu_out, dwd_out,
    send, recv, local, wq_all, wkv_all, wo_all, gains_all,
    group, kv_parts, branch, branch_c, branch_y, own_normed,
    w_part, x_tile, g_tile, acc_g, acc_u, acc_d,
):
    net = Net(n, send, recv)
    d, t = net.d, net.t
    quarter = wkv_all.shape[1]
    width = wg_all.shape[1]
    cut = acts_out.shape[2]
    rows, features = tok.shape

    def block(buf, idx):
        return row_block(n, buf, idx)

    wkv_own = wkv.at[:, lanes_at(t * quarter, quarter)]
    tokens_g = TensorGather(net, lambda i: group.at[i])
    kv_g = TensorGather(net, lambda i: kv_parts.at[i])
    branch_s = TensorScatter(net, branch, branch_c, branch_y)
    first_w = Spread(net, [wq_all, wkv_all, gains_all], block)
    second_w = Spread(net, [wo_all], block)
    spread_g = WideSpread(net, g_all, late_x=True)
    spread_x = WideSpread(net, x_all)
    deals = [
        Deal(
            net,
            lambda to, w=w, at=at: w.at[:, lanes_at(to * width + at, cut)],
            lambda frm, full=full, at=at: block(full, frm).at[:, pl.ds(at, cut)],
        )
        for at in range(0, width, cut)
        for w, full in ((wg, wg_all), (wu, wu_all), (wd, wd_all))
    ]
    assert net.used <= counts
    flow = Flow(n, [deals[:3], deals[3:]], True)

    own_copies = [
        (tok, group.at[t]),
        (wq, block(wq_all, d)),
        (wkv_own, block(wkv_all, d)),
        (gains, block(gains_all, d)),
        (wo, block(wo_all, d)),
        (go, g_all.at[0, net.z]),
    ] + [
        (w.at[:, lanes_at(d * width, width)], block(full, d))
        for w, full in ((wg, wg_all), (wu, wu_all), (wd, wd_all))
    ]
    own_copies = [
        pltpu.make_async_copy(a, b, local.at[i]) for i, (a, b) in enumerate(own_copies)
    ]
    for copy in own_copies:
        copy.start()
    net.greet()

    for copy in own_copies[:4]:
        copy.wait()
    tokens_g.begin()
    first_w.begin()
    flow.pump(pumps[0])
    own_copies[4].wait()
    own_copies[5].wait()
    tokens_g.rest()
    second_w.begin()
    spread_g.begin(go)
    flow.pump(pumps[1])

    @pl.loop(1, net.nz)
    def _(h):
        first_w.hop(h)

        @pl.when(h > 1)
        def _():
            second_w.hop(h - 1)

        spread_g.hop(h)

    flow.pump(pumps[2])
    inputs = group[...].reshape(4 * rows, features).astype(F32)
    root = inverse_root(inputs)
    first_w.cross()
    second_w.hop(net.nz - 1)
    spread_g.send_x()
    flow.pump(pumps[3])
    gain = lane_row(gains_all, 0, n)
    normed = (inputs * root * gain).astype(BF16)
    normed_out[...] = normed
    kv_parts[t] = dot_nn(normed, wkv_all[...]).astype(BF16)
    kv_g.begin()
    query_out[...] = dot_nn(normed, wq_all[...]).astype(BF16)
    flow.pump(pumps[4])
    kv_g.rest()
    for i in range(4):
        keyval_out[:, i * quarter : (i + 1) * quarter] = kv_parts[i]
    allowed = allowed_pairs(lens, 4 * rows)
    for h in range(query_out.shape[1] // HD):
        lanes = slice(h * HD, (h + 1) * HD)
        probs = softmax_head(query_out[:, lanes], keyval_out[:, :HD], allowed).astype(BF16)
        context_out[:, lanes] = dot_nn(probs, keyval_out[:, HD:]).astype(BF16)
    flow.pump(pumps[5])
    second_w.cross()
    branch[...] = dot_nt(context_out[...], wo_all[...]).astype(BF16).reshape(branch.shape)
    branch_s.begin()
    flow.pump(pumps[6])
    middle = group[t].astype(F32) + branch_s.rest()
    middle_out[...] = middle
    own_normed[...] = (middle * inverse_root(middle) * lane_row(gains_all, 1, n)).astype(BF16)
    own_x = pltpu.make_async_copy(own_normed, x_all.at[0, net.z], local.at[0])
    own_x.start()
    spread_x.begin(own_normed)
    spread_g.cross()
    flow.pump(pumps[7])
    outs = [
        pltpu.make_async_copy(a, b, local.at[1 + i])
        for i, (a, b) in enumerate(
            (
                (wq_all, wq_out),
                (wkv_all, wkv_out),
                (wo_all, wo_out),
                (gains_all, gains_out),
            )
        )
    ]
    for copy in outs:
        copy.start()
    own_x.wait()
    spread_x.hops()
    flow.pump(pumps[8])
    spread_x.core(0)
    spread_g.core(0)
    spread_g.core(1)
    spread_x.cross()
    flow.pump(pumps[9])
    spread_x.core(1)
    for x in range(2):
        spread_g.over(x)
        spread_g.core(2 + x)
    flow.pump(pumps[10])
    for slot in range(4):
        spread_g.core_done(slot)

    for i, (copy, deal, full) in enumerate(
        zip(own_copies[6:], deals[:3], (wg_all, wu_all, wd_all))
    ):
        copy.wait()
        deal.done()
        pltpu.make_async_copy(full.at[:, pl.ds(0, cut)], w_part.at[i], local.at[5 + i]).start()
    for acc in (acc_g, acc_u, acc_d):
        acc[...] = jnp.zeros_like(acc)
    for i, full in enumerate((wg_all, wu_all, wd_all)):
        pltpu.make_async_copy(full.at[:, pl.ds(0, cut)], w_part.at[i], local.at[5 + i]).wait()
    flow.pump(pumps[11])
    tile_blocks = x_tile.shape[0]
    tile = tile_blocks * rows

    @pl.loop(0, 8)
    def _(k):
        slot = k % 2 + 4 * ((k // 2) % 2) + 2 * (k // 4)
        for at in range(1, 8):

            @pl.when(k == at)
            def _():
                flow.pump(pumps[11 + at])

        for at, slot_from in ((2, 0), (3, 1), (6, 2), (7, 3)):

            @pl.when(k == at)
            def _():
                spread_x.core_done(slot_from)

        for at, x in ((4, 0), (5, 1)):

            @pl.when(k == at)
            def _():
                spread_x.over(x)
                spread_x.core(2 + x)

        @pl.loop(0, net.nz // tile_blocks)
        def _(sub):
            part = pl.ds(sub * tile_blocks, tile_blocks)
            loads = [
                pltpu.make_async_copy(a.at[slot, part], b, local.at[5 + i])
                for i, (a, b) in enumerate(((x_all, x_tile), (g_all, g_tile)))
            ]
            for load in loads:
                load.start()
            for load in loads:
                load.wait()
            x = x_tile[...].reshape(tile, features)
            g = g_tile[...].reshape(tile, features)
            hidden, grad_gate, grad_up = feed_forward(x, g, w_part[0], w_part[1], w_part[2])
            start = pl.multiple_of((slot * net.nz + sub * tile_blocks) * rows, tile)
            acts_out[0, pl.ds(start, tile), :] = hidden
            acts_out[1, pl.ds(start, tile), :] = grad_gate
            acts_out[2, pl.ds(start, tile), :] = grad_up
            acc_g[...] += dot_tn(x, grad_gate)
            acc_u[...] += dot_tn(x, grad_up)
            acc_d[...] += dot_tn(g, hidden)

    dwg_out[...] = acc_g[...].astype(BF16)
    dwu_out[...] = acc_u[...].astype(BF16)
    dwd_out[...] = acc_d[...].astype(BF16)
    flow.rest()
    for deal in deals[3:]:
        deal.done()
    for copy in outs:
        copy.wait()
    net.finish()


def second_kernel(
    n, counts, staged, pumps,
    lens, x_all, g_all, acts_first, wg_all, wu_all, wd_all, dwg, dwu, dwd,
    wq_all, wkv_all, wo_all, normed,
    tok, go, gains_all, query, keyval, context, middle,
    block_out, grad_tokens, grad_gains, grad_wq, grad_wkv, grad_wo, grad_wg, grad_wu, grad_wd,
    dx_c, dx_y, dx_x, dx_z, o_c, o_y, o_x, o_z,
    send, recv, local, stage, dw_part,
    acc, branch_rows, gkv, gkv_c, gkv_y, qpart, qpart_c, qpart_y,
    context_all, query_all, key_all, norm_parts, norm_land, branch_parts, branch_land, k_rows,
    gain_parts, gain_land, gain_sum, grad_query, normed_own,
):
    net = Net(n, send, recv)
    d, t = net.d, net.t
    nz = net.nz
    depth, heads = grad_wq.shape
    features, width = wg_all.shape
    cut = acts_first.shape[2]
    two = cut < width
    rows = tok.shape[0]
    quarter = wkv_all.shape[1]
    blocks = 256 // rows
    tile = blocks * rows
    subs = nz // blocks

    def block(buf, idx):
        return row_block(n, buf, idx)

    mem = Staged(stage, local.at[0]) if staged else Direct()
    scatter_dx = WideScatter(net, dx_c, dx_y, dx_x, dx_z, mem, subs)
    scatter_o = WideScatter(net, o_c, o_y, o_x, o_z, mem, subs)
    branch_g = TensorGather(net, lambda i: branch_rows.at[i])
    kv_s = TensorScatter(net, gkv, gkv_c, gkv_y)
    query_s = TensorScatter(net, qpart, qpart_c, qpart_y)
    kv_g = TensorGather(net, lambda i: k_rows.at[i])
    gain_deal = Deal(net, lambda to: gain_parts.at[to], lambda frm: gain_land.at[frm])
    gain_g = TensorGather(net, lambda i: gain_sum.at[i])
    context_s = Spread(net, [context_all], block)
    query_g = Spread(net, [query_all], block)
    key_g = Spread(net, [key_all], block)
    norm_cols = Columns(net, norm_parts, norm_land)
    branch_cols = Columns(net, branch_parts, branch_land)
    outs = (grad_wg, grad_wu, grad_wd)
    deals = [
        Deal(
            net,
            lambda to, p=part: block(p, to),
            lambda frm, o=out: o.at[:, lanes_at(frm * width, cut)],
        )
        for part, out in zip((dwg, dwu, dwd), outs)
    ]
    if two:
        deals += [
            Deal(
                net,
                lambda to, i=i: block(dw_part.at[i], to),
                lambda frm, o=out: o.at[:, lanes_at(frm * width + cut, cut)],
            )
            for i, out in enumerate(outs)
        ]
    flow = Flow(n, [deals[:3], deals[3:]], False)
    first_half = 3 * (n - 1)
    copies = [
        pltpu.make_async_copy(deal.src(d), deal.dst(d), local.at[1 + i])
        for i, deal in enumerate(deals)
    ]
    for copy in copies[:3]:
        copy.start()
    own_rows = pltpu.make_async_copy(
        normed.at[pl.ds(pl.multiple_of(t * rows, rows), rows)], normed_own, local.at[6]
    )
    own_rows.start()
    block(context_all, d)[...] = context[...]
    net.greet()
    context_s.begin()
    own_rows.wait()
    norm_cols.begin(normed_own[...])
    flow.pump(pumps[0], first_half)

    def ffn(wg_v, wu_v, wd_v, acts, x_tiles, g_tiles, x_cols, g_cols, one):
        w_loads = [
            pltpu.make_async_copy(a, b, local.at[7 + i])
            for i, (a, b) in enumerate(
                (
                    (wg_all, wg_v), (wu_all, wu_v), (wd_all, wd_v),
                    (acts_first, acts.at[:, :, pl.ds(0, cut)]),
                )
            )
        ]
        for load in w_loads:
            load.start()

        def place(k):
            step = k // subs
            core, y, x, sub = 1 - (step // 2) % 2, 1 - step // 4, 1 - step % 2, k % subs
            start = pl.multiple_of(((4 * core + 2 * y + x) * nz + sub * blocks) * rows, tile)
            return core, y, x, sub, pl.ds(start, tile)

        def loads(k):
            core, y, x, sub, _ = place(k)
            part = pl.ds(sub * blocks, blocks)
            return [
                pltpu.make_async_copy(
                    a.at[4 * core + 2 * y + x, part], b.at[k % 2], local.at[11 + 2 * i + k % 2]
                )
                for i, (a, b) in enumerate(((x_all, x_tiles), (g_all, g_tiles)))
            ]

        def hand_over(scatter, value, k):
            core, y, x, sub, _ = place(k)

            @pl.when(k > 0)
            def _():
                core_before, y_before, x_before, sub_before, _ = place(k - 1)

                @pl.when(core_before == 1)
                def _():
                    scatter.core_sent(2 * y_before + x_before, sub_before)

            @pl.when(core == 1)
            def _():
                one[...] = value.astype(BF16).reshape(one.shape)
                scatter.to_core(one, 2 * y + x, sub)

            @pl.when(core == 0)
            def _():
                scatter.keep(value, 2 * y + x, sub)

        if two:
            for load in loads(0):
                load.start()
        for load in w_loads:
            load.wait()
        more = slice(cut, width)

        @pl.loop(0, 8 * subs)
        def _(k):
            core, y, x, sub, here = place(k)
            if two:

                @pl.when(k + 1 < 8 * subs)
                def _():
                    for load in loads(k + 1):
                        load.start()

                for load in loads(k):
                    load.wait()
                done = feed_forward(
                    x_tiles[k % 2].reshape(tile, features),
                    g_tiles[k % 2].reshape(tile, features),
                    wg_v[:, more], wu_v[:, more], wd_v[:, more],
                )
                for i, act in enumerate(done):
                    acts[i, here, more] = act
            dx = dot_nt(acts[1, here, :], wg_v[...]) + dot_nt(acts[2, here, :], wu_v[...])
            hand_over(scatter_dx, dx, k)
            @pl.when((core == 0) & (y == 1))
            def _():
                @pl.loop(0, blocks)
                def _(i):
                    scatter_dx.to_y(x, sub * blocks + blocks - 1 - i)

        @pl.loop(0, 8 * subs)
        def _(k):
            hand_over(scatter_o, dot_nt(acts[0, place(k)[4], :], wd_v[...]), k)

        scatter_dx.over()
        if two:

            def second_gradients(start, columns):
                for i, block in enumerate(weight_blocks(columns, acts, more)):
                    dw_part[i, pl.ds(start, block.shape[0]), :] = block.astype(BF16)

            by_columns(x_all, g_all, x_cols, g_cols, local.at[pl.ds(11, 4)], second_gradients)

    weights = pltpu.VMEM((features, width), BF16)
    tiles = pltpu.VMEM((2, blocks, rows, features), BF16)
    chunks = pltpu.VMEM((2, 8, nz, rows, 256), BF16)
    pl.run_scoped(
        ffn, weights, weights, weights, pltpu.VMEM((3, 8 * nz * rows, width), BF16),
        tiles, tiles, chunks, chunks, pltpu.VMEM((blocks, rows, features), BF16),
    )
    if two:
        for copy in copies[3:]:
            copy.start()
    flow.pump(pumps[1])
    scatter_o.all_to_y(1)
    scatter_dx.lines()
    flow.pump(pumps[2])
    context_s.hop(1)
    scatter_dx.total(acc)

    def attention(wq_v, wo_v, wkv_v):
        attn_loads = [
            pltpu.make_async_copy(a, b, local.at[7 + i])
            for i, (a, b) in enumerate(((wq_all, wq_v), (wo_all, wo_v), (wkv_all, wkv_v)))
        ]
        for load in attn_loads:
            load.start()
        rows_in = middle[...]
        root = inverse_root(rows_in)
        grad_normed = acc[...]
        gain = lane_row(gains_all, 1, n)
        scaled = grad_normed * gain
        inner = jnp.mean(scaled * rows_in, axis=-1, keepdims=True)
        grad_middle = go[...].astype(F32) + root * (scaled - rows_in * (root * root) * inner)
        branch_rows[t] = grad_middle.astype(BF16)
        branch_g.begin()
        grad_tokens[...] = grad_middle
        gain_ffn = jnp.sum(grad_normed * rows_in * root, axis=0, keepdims=True)
        branch_cols.begin(grad_middle.astype(BF16))
        flow.pump(pumps[3])
        for load in attn_loads:
            load.wait()
        branch_g.rest()
        scatter_o.all_to_y(0)
        context_s.hop(2)
        grad_branch = branch_rows[...].reshape(4 * rows, features)
        grad_context = dot_nn(grad_branch, wo_v[...]).astype(BF16)
        pl.loop(3, nz)(context_s.hop)
        scatter_o.over()
        norm_cols.gather()
        flow.pump(pumps[4])

        allowed = allowed_pairs(lens, 4 * rows)
        key, value = keyval[:, :HD], keyval[:, HD:]
        grad_key = jnp.zeros((4 * rows, HD), F32)
        grad_value = jnp.zeros((4 * rows, HD), F32)
        factor = HD ** (-0.5)
        for h in range(heads // HD):
            lanes = slice(h * HD, (h + 1) * HD)
            probs = softmax_head(query[:, lanes], key, allowed)
            grad_head = grad_context[:, lanes]
            grad_probs = dot_nt(grad_head, value)
            inner = jnp.sum(grad_probs * probs, axis=-1, keepdims=True)
            grad_scores = (probs * (grad_probs - inner)).astype(BF16)
            grad_query[:, lanes] = (dot_nn(grad_scores, key) * factor).astype(BF16)
            grad_key += dot_tn(grad_scores, query[:, lanes]) * factor
            grad_value += dot_tn(probs.astype(BF16), grad_head)
        block(query_all, d)[...] = grad_query[...]
        query_g.begin()
        both = jnp.concatenate([grad_key, grad_value], axis=1).astype(BF16)
        for i in range(4):
            gkv[i] = both[:, i * quarter : (i + 1) * quarter]
        kv_s.begin()
        flow.pump(pumps[5])
        term = dot_nt(grad_query[...], wq_v[...])
        grad_kv = kv_s.rest().astype(BF16)
        block(key_all, d)[...] = grad_kv
        key_g.begin()
        term += dot_nt(grad_kv, wkv_v[...])
        qpart[...] = term.astype(BF16).reshape(qpart.shape)
        query_s.begin()
        branch_cols.gather()
        query_g.hop(1)
        key_g.hop(1)
        flow.pump(pumps[6])
        grad_normed = query_s.rest()

        rows_in = tok[...].astype(F32)
        root = inverse_root(rows_in)
        gain = lane_row(gains_all, 0, n)
        scaled = grad_normed * gain
        inner = jnp.mean(scaled * rows_in, axis=-1, keepdims=True)
        grad_tokens[...] += root * (scaled - rows_in * (root * root) * inner)
        gain_attn = jnp.sum(grad_normed * rows_in * root, axis=0, keepdims=True)
        for i in range(n):
            lanes = slice(i * depth, (i + 1) * depth)
            gain_parts[i, 0:1, :] = gain_attn[:, lanes]
            gain_parts[i, 1:2, :] = gain_ffn[:, lanes]
            gain_parts[i, 2:8, :] = jnp.zeros((6, depth), F32)
        gain_deal.begin()
        query_g.hop(2)
        key_g.hop(2)
        scatter_o.line_step(0)
        flow.pump(pumps[7])
        context_s.cross()
        branch_cols.rest()
        branch_cols.times(context_all, grad_wo)

        @pl.loop(3, nz)
        def _(h):
            query_g.hop(h)
            key_g.hop(h)
            scatter_o.line_step(h - 2)

        flow.pump(pumps[8])
        norm_cols.rest()
        key_g.cross()
        norm_cols.times(key_all, k_rows.at[t])
        kv_g.begin()
        gain_land[d] = gain_parts[d]
        gain_deal.done()
        gain_sum[t] = jnp.sum(gain_land[...], axis=0)
        gain_g.begin()
        flow.rest()
        scatter_o.line_step(nz - 2)
        scatter_o.meet(net.z)
        query_g.cross()
        norm_cols.times(query_all, grad_wq)
        gain_g.rest()
        grad_gains[...] = jnp.sum(gain_sum[...], axis=0)
        kv_g.rest()
        for i in range(4):
            grad_wkv[:, i * quarter : (i + 1) * quarter] = k_rows[i]
        scatter_o.total(acc)
        block_out[...] = (middle[...] + acc[...]).astype(BF16)

    assert net.used <= counts
    projection = pltpu.VMEM((features, heads), BF16)
    part = pltpu.VMEM((features, quarter), BF16)
    pl.run_scoped(attention, projection, projection, part)
    for deal in deals:
        deal.done()
    for copy in copies:
        copy.wait()
    net.finish()


def params(collective_id):
    return pltpu.CompilerParams(
        collective_id=collective_id, has_side_effects=True, vmem_limit_bytes=63 * MIB
    )


PUMPS_1 = (0.119, 0.0, 0.048, 0.048, 0.048, 0.048, 0.048, 0.095, 0.095, 0.095, 0.095, 0.095, 0.167, 0.0, 0.0, 0.0, 0.0, 0.0, 0.0)
PUMPS_2 = (0.452, 0.0, 0.024, 0.19, 0.143, 0.095, 0.095, 0.0, 0.0, 0.0)


def body(
    n, tokens, grad_out, lengths, gain_attn, gain_ffn, w_query, w_keyval, w_out, w_gate, w_up, w_down
):
    nz = n // 2
    rows, features = tokens.shape
    depth, heads = w_query.shape
    quarter = w_keyval.shape[1] // 4
    width = w_gate.shape[1] // n
    group_rows = 4 * rows
    shape = jax.ShapeDtypeStruct
    gains = jnp.concatenate(
        [gain_attn[None], gain_ffn[None], jnp.zeros((6, depth), gain_attn.dtype)]
    ).astype(F32)

    cut = width // 2 if width // 2 % 128 == 0 else width
    parts = width // cut
    tile_blocks = 256 // rows
    counts = 9 + 4 * 3 * nz + 2 * (5 * nz + 4) + 3 * parts * n
    full = shape((features, width), BF16)
    part = shape((features, cut), BF16)
    wide = shape((8, nz, rows, features), BF16)
    all_rows = 4 * n * rows
    (
        wg_all, wu_all, wd_all, x_all, g_all, wq_all, wkv_all, wo_all, gains_all,
        query, keyval, context, normed, middle, acts, dwg, dwu, dwd,
    ) = pl.pallas_call(
        functools.partial(first_kernel, n, counts, PUMPS_1),
        out_shape=(
            full, full, full, wide, wide,
            shape((features, heads), BF16),
            shape((features, quarter), BF16),
            shape((features, heads), BF16),
            shape((8 * n, depth), F32),
            shape((group_rows, heads), BF16),
            shape((group_rows, 2 * HD), BF16),
            shape((group_rows, heads), BF16),
            shape((group_rows, features), BF16),
            shape((rows, features), F32),
            shape((3, all_rows, cut), BF16),
            part, part, part,
        ),
        in_specs=[SMEM] + [ANY] * 9,
        out_specs=(ANY,) * 9 + (VMEM,) * 9,
        scratch_shapes=[
            pltpu.SemaphoreType.DMA((counts,)),
            pltpu.SemaphoreType.DMA((counts,)),
            pltpu.SemaphoreType.DMA((9,)),
            pltpu.VMEM((features, heads), BF16),
            pltpu.VMEM((features, quarter), BF16),
            pltpu.VMEM((features, heads), BF16),
            pltpu.VMEM((8 * n, depth), F32),
            pltpu.VMEM((4, rows, features), BF16),
            pltpu.VMEM((4, group_rows, quarter), BF16),
            pltpu.VMEM((4, rows, features), BF16),
            pltpu.VMEM((2, rows, features), BF16),
            pltpu.VMEM((rows, features), BF16),
            pltpu.VMEM((rows, features), BF16),
            pltpu.VMEM((3, features, cut), BF16),
            pltpu.VMEM((tile_blocks, rows, features), BF16),
            pltpu.VMEM((tile_blocks, rows, features), BF16),
        ]
        + [pltpu.VMEM((features, cut), F32)] * 3,
        compiler_params=params(0),
        name="forward",
    )(lengths, tokens, grad_out, gains, w_query, w_keyval, w_out, w_gate, w_up, w_down)

    staged = n > 8
    subs = nz // tile_blocks
    counts = 2 * (4 * subs + 5 * nz) + 3 * 3 * nz + 21 + 3 * n + 3 * parts * n
    landing = [
        shape((4, nz, rows, features), BF16),
        shape((2, nz, rows, features), BF16),
        shape((nz, rows, features), BF16),
        shape((nz + 1, rows, features), BF16),
    ] * 2
    out_shape = [
        shape((rows, features), BF16),
        shape((rows, features), F32),
        shape((8, depth), F32),
        shape((depth, heads), F32),
        shape((depth, 4 * quarter), F32),
        shape((depth, heads), F32),
        shape((depth, n * width), BF16),
        shape((depth, n * width), BF16),
        shape((depth, n * width), BF16),
    ]
    out_specs = [VMEM] * 6 + [ANY] * 3
    in_vmem = []
    if staged:
        out_shape += landing
        out_specs += [ANY] * len(landing)
    else:
        in_vmem = [pltpu.VMEM(place.shape, place.dtype) for place in landing]

    results = pl.pallas_call(
        functools.partial(second_kernel, n, counts, staged, PUMPS_2),
        out_shape=tuple(out_shape),
        in_specs=[SMEM] + [ANY] * 13 + [VMEM] * 7,
        out_specs=tuple(out_specs),
        scratch_shapes=in_vmem
        + [
            pltpu.SemaphoreType.DMA((counts,)),
            pltpu.SemaphoreType.DMA((counts,)),
            pltpu.SemaphoreType.DMA((15,)),
            pltpu.VMEM((tile_blocks if staged else 1, rows, features), BF16),
            pltpu.VMEM((3, features, cut if parts > 1 else 128), BF16),
            pltpu.VMEM((rows, features), F32),
            pltpu.VMEM((4, rows, features), BF16),
            pltpu.VMEM((4, group_rows, quarter), BF16),
            pltpu.VMEM((2, group_rows, quarter), BF16),
            pltpu.VMEM((group_rows, quarter), BF16),
            pltpu.VMEM((4, rows, features), BF16),
            pltpu.VMEM((2, rows, features), BF16),
            pltpu.VMEM((rows, features), BF16),
        ]
        + [
            pltpu.VMEM((n * group_rows, heads), BF16),
            pltpu.VMEM((n * group_rows, heads), BF16),
            pltpu.VMEM((n * group_rows, quarter), BF16),
            pltpu.VMEM((n, rows, depth), BF16),
            pltpu.VMEM((4, n, rows, depth), BF16),
            pltpu.VMEM((n, rows, depth), BF16),
            pltpu.VMEM((4, n, rows, depth), BF16),
            pltpu.VMEM((4, depth, quarter), F32),
            pltpu.VMEM((n, 8, depth), F32),
            pltpu.VMEM((n, 8, depth), F32),
            pltpu.VMEM((4, 8, depth), F32),
            pltpu.VMEM((group_rows, heads), BF16),
            pltpu.VMEM((rows, features), BF16),
        ],
        compiler_params=params(1),
        name="backward",
    )(
        lengths, x_all, g_all, acts, wg_all, wu_all, wd_all, dwg, dwu, dwd,
        wq_all, wkv_all, wo_all, normed,
        tokens, grad_out, gains_all, query, keyval, context, middle,
    )
    block_out, grad_tokens, grad_gains, grad_wq, grad_wkv, grad_wo, grad_wg, grad_wu, grad_wd = (
        results[:9]
    )
    return (
        block_out,
        grad_tokens,
        grad_gains[0],
        grad_gains[1],
        grad_wq,
        grad_wkv,
        grad_wo,
        grad_wg.astype(F32),
        grad_wu.astype(F32),
        grad_wd.astype(F32),
    )


def solution(mesh):
    rows = P(("dp", "tensor"), None)
    both = P("dp", "tensor")
    return jax.shard_map(
        functools.partial(body, mesh.shape["dp"]),
        mesh=mesh,
        in_specs=(rows, rows, P("dp", None), P("dp"), P("dp"), both, P("dp", None), both, both, both, both),
        out_specs=(rows, rows, P("dp"), P("dp"), both, P("dp", None), both, both, both, both),
        check_vma=False,
    )
```

```python
import functools

import jax
import jax.numpy as jnp
from jax import lax
from jax.experimental import pallas as pl
from jax.experimental.pallas import tpu as pltpu
from jax.sharding import PartitionSpec as P

HD = 256
WINDOW = 2048
NORM_EPS = 1e-06
MASKED = -1e30
BF16, F32 = jnp.bfloat16, jnp.float32
MESH = pl.DeviceIdType.MESH
ANY = pl.BlockSpec(memory_space=pl.ANY)
VMEM = pl.BlockSpec(memory_space=pltpu.VMEM)
SMEM = pl.BlockSpec(memory_space=pltpu.SMEM)
MIB = 1 << 20


def dot_nn(a, b):
    return lax.dot_general(a, b, (((1,), (0,)), ((), ())), preferred_element_type=F32)


def dot_nt(a, b):
    return lax.dot_general(a, b, (((1,), (1,)), ((), ())), preferred_element_type=F32)


def dot_tn(a, b):
    return lax.dot_general(a, b, (((0,), (0,)), ((), ())), preferred_element_type=F32)


class Net:
    def __init__(self, n, send, recv):
        self.n, self.nz = n, n // 2
        self.send, self.recv, self.used = send, recv, 0
        self.d = lax.axis_index("dp")
        self.t = lax.axis_index("tensor")
        self.z = self.d // 2
        self.x = self.d % 2
        self.dx = self.d + 1 - 2 * self.x
        self.ty = (self.t + 2) % 4
        self.tc = self.t + 1 - 2 * (self.t % 2)
        self.tcy = (self.tc + 2) % 4
        self.ends = []

    def take(self, count):
        first = self.used
        self.used += count
        return first

    def dp(self, other):
        return (other, self.t)

    def tensor(self, other):
        return (self.d, other)

    def make(self, src, dst, k, device):
        return pltpu.make_async_remote_copy(
            src_ref=src,
            dst_ref=dst,
            send_sem=self.send.at[k],
            recv_sem=self.recv.at[k],
            device_id=device,
            device_id_type=MESH,
        )

    def start(self, src, dst, k, device):
        self.make(src, dst, k, device).start()

    def landed(self, ref, k):
        self.make(ref, ref, k, self.tensor(self.tc)).wait_recv()

    def sent(self, ref, k):
        self.make(ref, ref, k, self.tensor(self.tc)).wait_send()

    def greet(self):
        barrier = pltpu.get_barrier_semaphore()

        @pl.loop(1, self.n)
        def _(m):
            pl.semaphore_signal(
                barrier, inc=1, device_id=self.dp((self.d + m) % self.n), device_id_type=MESH
            )

        for other in (self.ty, self.tc):
            pl.semaphore_signal(
                barrier, inc=1, device_id=self.tensor(other), device_id_type=MESH
            )
        pl.semaphore_wait(barrier, self.n + 1)

    def finish(self):
        for end in self.ends:
            end()


class TensorGather:
    def __init__(self, net, at):
        self.net, self.at, self.k = net, at, net.take(3)
        net.ends.append(self.end)

    def begin(self):
        net = self.net
        net.start(self.at(net.t), self.at(net.t), self.k, net.tensor(net.ty))
        net.start(self.at(net.t), self.at(net.t), self.k + 1, net.tensor(net.tc))

    def rest(self):
        net = self.net
        net.landed(self.at(net.ty), self.k)
        net.start(self.at(net.ty), self.at(net.ty), self.k + 2, net.tensor(net.tc))
        net.landed(self.at(net.tc), self.k + 1)
        net.landed(self.at(net.tcy), self.k + 2)

    def end(self):
        for i in range(3):
            self.net.sent(self.at(0), self.k + i)


class TensorScatter:
    def __init__(self, net, part, cl, yl):
        self.net, self.part, self.cl, self.yl, self.k = net, part, cl, yl, net.take(3)
        net.ends.append(self.end)

    def begin(self):
        net = self.net
        net.start(self.part.at[net.tcy], self.cl.at[1], self.k + 1, net.tensor(net.tc))
        net.start(self.part.at[net.tc], self.cl.at[0], self.k, net.tensor(net.tc))

    def rest(self):
        net = self.net
        net.landed(self.cl.at[1], self.k + 1)
        pair = self.part[net.ty].astype(F32) + self.cl[1].astype(F32)
        self.part[net.ty] = pair.astype(self.part.dtype)
        net.start(self.part.at[net.ty], self.yl, self.k + 2, net.tensor(net.ty))
        net.landed(self.cl.at[0], self.k)
        own = self.part[net.t].astype(F32) + self.cl[0].astype(F32)
        net.landed(self.yl, self.k + 2)
        return own + self.yl[...].astype(F32)

    def end(self):
        for i in range(3):
            self.net.sent(self.yl, self.k + i)


class Spread:
    def __init__(self, net, bufs, block):
        self.net, self.bufs, self.block = net, bufs, block
        self.zk = [net.take(2 * net.nz) for _ in bufs]
        self.xk = [net.take(net.nz) for _ in bufs]
        net.ends.append(self.end)

    def line(self, j, zb, right):
        net = self.net
        here = self.block(self.bufs[j], 2 * zb + net.x)
        if right:
            net.start(here, here, self.zk[j] + zb, net.dp(net.d + 2))
        else:
            net.start(here, here, self.zk[j] + net.nz + zb, net.dp(net.d - 2))

    def over_x(self, j, zb):
        net = self.net
        here = self.block(self.bufs[j], 2 * zb + net.x)
        net.start(here, here, self.xk[j] + zb, net.dp(net.dx))

    def begin(self):
        net = self.net
        for j in range(len(self.bufs)):

            @pl.when(net.z < net.nz - 1)
            def _():
                self.line(j, net.z, True)

            @pl.when(net.z > 0)
            def _():
                self.line(j, net.z, False)

            self.over_x(j, net.z)

    def hop(self, h):
        net = self.net
        nz = net.nz
        for j, buf in enumerate(self.bufs):

            @pl.when(net.z - h >= 0)
            def _():
                zb = net.z - h
                net.landed(self.block(buf, 2 * zb + net.x), self.zk[j] + zb)

                @pl.when(net.z < nz - 1)
                def _():
                    self.line(j, zb, True)

                self.over_x(j, zb)

            @pl.when(net.z + h <= nz - 1)
            def _():
                zb = net.z + h
                net.landed(self.block(buf, 2 * zb + net.x), self.zk[j] + nz + zb)

                @pl.when(net.z > 0)
                def _():
                    self.line(j, zb, False)

                self.over_x(j, zb)

    def cross(self):
        net = self.net

        @pl.loop(0, net.nz)
        def _(k):
            zb = (net.z + k) % net.nz
            for j, buf in enumerate(self.bufs):
                net.landed(self.block(buf, 2 * zb + 1 - net.x), self.xk[j] + zb)

    def end(self):
        net = self.net

        @pl.loop(0, net.nz)
        def _(zb):
            for j, buf in enumerate(self.bufs):
                some = self.block(buf, 0)

                @pl.when((zb <= net.z) & (net.z < net.nz - 1))
                def _():
                    net.sent(some, self.zk[j] + zb)

                @pl.when((zb >= net.z) & (net.z > 0))
                def _():
                    net.sent(some, self.zk[j] + net.nz + zb)

                net.sent(some, self.xk[j] + zb)


class WideSpread:
    def __init__(self, net, buf, late_x=False):
        self.net, self.buf, self.late_x = net, buf, late_x
        self.zk, self.xk = net.take(2 * net.nz), net.take(net.nz)
        self.yk, self.ck = net.take(2 * net.nz), net.take(4)
        net.ends.append(self.end)

    def onward(self, src, zb, right, left):
        net, buf = self.net, self.buf
        if right:

            @pl.when(net.z < net.nz - 1)
            def _():
                net.start(src, buf.at[0, zb], self.zk + zb, net.dp(net.d + 2))

        if left:

            @pl.when(net.z > 0)
            def _():
                net.start(src, buf.at[0, zb], self.zk + net.nz + zb, net.dp(net.d - 2))

        net.start(src, buf.at[2, zb], self.yk + zb, net.tensor(net.ty))
        if not self.late_x:
            net.start(src, buf.at[1, zb], self.xk + zb, net.dp(net.dx))

    def send_x(self):
        net = self.net

        @pl.loop(0, net.nz)
        def _(k):
            zb = (net.z + k) % net.nz
            net.start(self.buf.at[0, zb], self.buf.at[1, zb], self.xk + zb, net.dp(net.dx))

    def begin(self, own):
        self.onward(own, self.net.z, True, True)

    def hop(self, h):
        net, buf = self.net, self.buf

        @pl.when(net.z - h >= 0)
        def _():
            zb = net.z - h
            net.landed(buf.at[0, zb], self.zk + zb)
            self.onward(buf.at[0, zb], zb, True, False)

        @pl.when(net.z + h <= net.nz - 1)
        def _():
            zb = net.z + h
            net.landed(buf.at[0, zb], self.zk + net.nz + zb)
            self.onward(buf.at[0, zb], zb, False, True)

    def hops(self):
        @pl.loop(1, self.net.nz)
        def _(h):
            self.hop(h)

    def cross(self):
        net, buf = self.net, self.buf

        @pl.loop(0, net.nz)
        def _(k):
            zb = (net.z + k) % net.nz
            net.landed(buf.at[1, zb], self.xk + zb)
            net.start(buf.at[1, zb], buf.at[3, zb], self.yk + net.nz + zb, net.tensor(net.ty))

    def over(self, x):
        net = self.net

        @pl.loop(0, net.nz)
        def _(k):
            zb = (net.z + k) % net.nz
            net.landed(self.buf.at[2 + x, zb], self.yk + x * net.nz + zb)

    def core(self, slot):
        net = self.net
        net.start(self.buf.at[slot], self.buf.at[4 + slot], self.ck + slot, net.tensor(net.tc))

    def core_done(self, slot):
        self.net.landed(self.buf.at[4 + slot], self.ck + slot)

    def end(self):
        net = self.net
        some = self.buf.at[0, 0]

        @pl.loop(0, net.nz)
        def _(zb):
            @pl.when((zb <= net.z) & (net.z < net.nz - 1))
            def _():
                net.sent(some, self.zk + zb)

            @pl.when((zb >= net.z) & (net.z > 0))
            def _():
                net.sent(some, self.zk + net.nz + zb)

            net.sent(some, self.xk + zb)
            net.sent(some, self.yk + zb)
            net.sent(some, self.yk + net.nz + zb)

        for slot in range(4):
            net.sent(self.buf.at[0], self.ck + slot)


class Deal:
    def __init__(self, net, src, dst):
        self.net, self.src, self.dst, self.k = net, src, dst, net.take(net.n)
        net.ends.append(self.end)

    def send(self, m):
        net = self.net
        to = (net.d + m) % net.n
        net.start(self.src(to), self.dst(net.d), self.k + m, net.dp(to))

    def begin(self):
        pl.loop(1, self.net.n)(self.send)

    def done(self):
        net = self.net

        @pl.loop(1, net.n)
        def _(m):
            net.landed(self.dst((net.d - m + net.n) % net.n), self.k + m)

    def end(self):
        net = self.net

        @pl.loop(1, net.n)
        def _(m):
            net.sent(self.src(0), self.k + m)


class Flow:
    def __init__(self, n, groups, even_first):
        self.todo = []
        for deals in groups:
            for parity in (0, 1) if even_first else (1, 0):
                self.todo += [(deal, m) for deal in deals for m in range(1, n) if m % 2 == parity]
        self.gone, self.share = 0, 0.0

    def pump(self, share, limit=None):
        self.share += share
        upto = min(round(self.share * len(self.todo)), len(self.todo) if limit is None else limit)
        for deal, m in self.todo[self.gone : upto]:
            deal.send(m)
        self.gone = max(upto, self.gone)

    def rest(self):
        self.pump(1.0)


class Columns:
    def __init__(self, net, parts, land):
        self.net, self.parts, self.land = net, parts, land
        self.deal = Deal(net, lambda to: parts.at[to], lambda frm: land.at[net.t, frm])
        self.over = TensorGather(net, lambda i: land.at[i])

    def begin(self, rows):
        depth = self.parts.shape[2]
        for i in range(self.net.n):
            self.parts[i] = rows[:, i * depth : (i + 1) * depth]
        self.land[self.net.t, self.net.d] = self.parts[self.net.d]
        self.deal.begin()

    def gather(self):
        self.deal.done()
        self.over.begin()

    def rest(self):
        self.over.rest()

    def times(self, other, acc):
        n = self.net.n
        depth = self.parts.shape[2]
        acc[...] = jnp.zeros_like(acc)

        @pl.loop(0, n)
        def _(i):
            mine = self.land[:, i].reshape(-1, depth)
            acc[...] += dot_tn(mine, row_block(n, other, i)[...])


class Scatter:
    def __init__(self, net, own, other, xl, zl, mem):
        self.net, self.own, self.other, self.xl, self.zl, self.mem = net, own, other, xl, zl, mem
        self.xk, self.rk, self.lk = net.take(net.nz), net.take(net.nz), net.take(net.nz)
        net.ends.append(self.end)

    def order(self, k):
        odd = k % 2
        return odd * (k // 2) + (1 - odd) * (self.net.nz - 1 - k // 2)

    def send_x(self, zb):
        net = self.net
        net.start(self.other(zb), self.xl.at[zb], self.xk + zb, net.dp(net.dx))

    def begin(self):
        @pl.loop(0, self.net.nz)
        def _(k):
            self.send_x(self.order(k))

    def add(self, block, other):
        mem = self.mem
        mem.put(block, (mem.get(block).astype(F32) + mem.get(other).astype(F32)).astype(BF16))

    def meet(self, zb):
        net = self.net
        net.landed(self.xl.at[zb], self.xk + zb)
        self.add(self.own(zb), self.xl.at[zb])

    def line_step(self, k):
        net = self.net
        nz = net.nz
        far = nz - 1 - k

        @pl.when(far > net.z)
        def _():
            self.meet(far)
            here = self.own(far)

            @pl.when(net.z > 0)
            def _():
                net.landed(self.zl.at[far], self.rk + far)
                self.add(here, self.zl.at[far])

            net.start(here, self.zl.at[far], self.rk + far, net.dp(net.d + 2))

        @pl.when(k < net.z)
        def _():
            self.meet(k)
            here = self.own(k)

            @pl.when(net.z < nz - 1)
            def _():
                net.landed(self.zl.at[k], self.lk + k)
                self.add(here, self.zl.at[k])

            last = (k == net.z - 1).astype(jnp.int32)
            net.start(here, self.zl.at[last * nz + (1 - last) * k], self.lk + k, net.dp(net.d - 2))

    def lines(self):
        pl.loop(0, self.net.nz - 1)(self.line_step)
        self.meet(self.net.z)

    def total(self, acc):
        net, mem = self.net, self.mem
        acc[...] = mem.get(self.own(net.z)).astype(F32)

        @pl.when(net.z > 0)
        def _():
            net.landed(self.zl.at[net.z], self.rk + net.z)
            acc[...] += mem.get(self.zl.at[net.z]).astype(F32)

        @pl.when(net.z < net.nz - 1)
        def _():
            net.landed(self.zl.at[net.nz], self.lk + net.z)
            acc[...] += mem.get(self.zl.at[net.nz]).astype(F32)

    def end(self):
        net = self.net

        @pl.loop(0, net.nz)
        def _(zb):
            net.sent(self.xl.at[0], self.xk + zb)

            @pl.when(zb > net.z)
            def _():
                net.sent(self.zl.at[0], self.rk + zb)

            @pl.when(zb < net.z)
            def _():
                net.sent(self.zl.at[0], self.lk + zb)


class WideScatter(Scatter):
    def __init__(self, net, cl, yl, xl, zl, mem, tiles):
        self.cl, self.yl, self.tiles = cl, yl, tiles
        self.ck, self.yk = net.take(4 * tiles), net.take(2 * net.nz)
        super().__init__(net, lambda zb: cl.at[0, zb], lambda zb: cl.at[1, zb], xl, zl, mem)
        net.ends.append(self.wide_end)

    def place(self, yx, sub):
        blocks = self.net.nz // self.tiles
        return self.cl.at[yx, pl.ds(sub * blocks, blocks)]

    def to_core(self, stage, yx, sub):
        net = self.net
        net.start(stage, self.place(yx, sub), self.ck + yx * self.tiles + sub, net.tensor(net.tc))

    def core_sent(self, yx, sub):
        self.net.sent(self.place(0, 0), self.ck + yx * self.tiles + sub)

    def keep(self, value, yx, sub):
        place = self.place(yx, sub)
        self.net.landed(place, self.ck + yx * self.tiles + sub)
        value = value.reshape(place.shape) + self.mem.get(place).astype(F32)
        self.mem.put(place, value.astype(BF16))

    def to_y(self, x, zb):
        net = self.net
        net.start(
            self.cl.at[2 + x, zb], self.yl.at[x, zb], self.yk + x * net.nz + zb, net.tensor(net.ty)
        )

    def all_to_y(self, x):
        @pl.loop(0, self.net.nz)
        def _(k):
            self.to_y(x, self.order(k))

    def from_y(self, x, zb):
        net = self.net
        net.landed(self.yl.at[x, zb], self.yk + x * net.nz + zb)
        self.add(self.cl.at[x, zb], self.yl.at[x, zb])

    def over(self):
        @pl.loop(0, self.net.nz)
        def _(k):
            zb = self.order(k)
            self.from_y(1, zb)
            self.send_x(zb)

    def meet(self, zb):
        self.from_y(0, zb)
        super().meet(zb)

    def wide_end(self):
        net = self.net

        @pl.loop(0, net.nz)
        def _(zb):
            net.sent(self.yl.at[0, 0], self.yk + zb)
            net.sent(self.yl.at[0, 0], self.yk + net.nz + zb)


class Direct:
    def get(self, ref):
        return ref[...]

    def put(self, ref, value):
        ref[...] = value


class Staged:
    def __init__(self, buf, sem):
        self.buf, self.sem = buf, sem

    def view(self, ref):
        return self.buf if len(ref.shape) == 3 else self.buf.at[0]

    def get(self, ref):
        view = self.view(ref)
        copy = pltpu.make_async_copy(ref, view, self.sem)
        copy.start()
        copy.wait()
        return view[...]

    def put(self, ref, value):
        view = self.view(ref)
        view[...] = value
        copy = pltpu.make_async_copy(view, ref, self.sem)
        copy.start()
        copy.wait()


def lane_row(gains, row, n):
    return jnp.concatenate([gains[8 * i + row : 8 * i + row + 1, :] for i in range(n)], axis=1)


def allowed_pairs(lens, rows):
    place_i = lax.broadcasted_iota(jnp.int32, (rows, 1), 0)
    place_j = lax.broadcasted_iota(jnp.int32, (1, rows), 1)
    segment_i = jnp.zeros((rows, 1), jnp.int32)
    segment_j = jnp.zeros((1, rows), jnp.int32)
    total = 0
    for k in range(lens.shape[1]):
        total = total + lens[0, k]
        segment_i += (place_i >= total).astype(jnp.int32)
        segment_j += (place_j >= total).astype(jnp.int32)
    distance = place_i - place_j
    return (segment_i == segment_j) & (distance >= 0) & (distance < WINDOW)


def softmax_head(query, key, allowed):
    scores = dot_nt(query, key) * HD ** (-0.5)
    scores = jnp.where(allowed, scores, MASKED)
    weights = jnp.exp(scores - jnp.max(scores, axis=-1, keepdims=True))
    return weights / jnp.sum(weights, axis=-1, keepdims=True)


def inverse_root(rows):
    return lax.rsqrt(jnp.mean(rows * rows, axis=-1, keepdims=True) + NORM_EPS)


def feed_forward(x, g, wg, wu, wd):
    gate = dot_nn(x, wg)
    up = dot_nn(x, wu)
    grad_hidden = dot_nn(g, wd)
    root = (2.0 / jnp.pi) ** 0.5
    square = gate * gate
    tanh = jnp.tanh(root * gate * (1.0 + 0.044715 * square))
    half = 0.5 * (1.0 + tanh)
    gelu = gate * half
    slope = half + 0.5 * gate * (1.0 - tanh * tanh) * (root * (1.0 + 3 * 0.044715 * square))
    hidden = (gelu * up).astype(BF16)
    grad_gate = (grad_hidden * up * slope).astype(BF16)
    grad_up = (grad_hidden * gelu).astype(BF16)
    return hidden, grad_gate, grad_up


def row_block(n, buf, idx):
    step = buf.shape[0] // n
    return buf.at[pl.ds(pl.multiple_of(idx * step, step), step)]


def lanes_at(start, size):
    return pl.ds(pl.multiple_of(start, 128), size)


def weight_blocks(columns, acts, cols):
    x_cols, g_cols = columns
    return (
        dot_tn(x_cols, acts[1, :, cols]),
        dot_tn(x_cols, acts[2, :, cols]),
        dot_tn(g_cols, acts[0, :, cols]),
    )


def by_columns(x_all, g_all, x_cols, g_cols, sems, use):
    features = x_all.shape[3]
    chunk = x_cols.shape[4]
    count = features // chunk

    def loads(c):
        lanes = lanes_at(c * chunk, chunk)
        return [
            pltpu.make_async_copy(a.at[:, :, :, lanes], b.at[c % 2], sems.at[2 * i + c % 2])
            for i, (a, b) in enumerate(((x_all, x_cols), (g_all, g_cols)))
        ]

    for load in loads(0):
        load.start()

    @pl.loop(0, count)
    def _(c):
        @pl.when(c + 1 < count)
        def _():
            for load in loads(c + 1):
                load.start()

        for load in loads(c):
            load.wait()
        use(pl.multiple_of(c * chunk, chunk), [b[c % 2].reshape(-1, chunk) for b in (x_cols, g_cols)])


def first_kernel(
    n, counts, pumps,
    lens, tok, go, gains, wq, wkv, wo, wg, wu, wd,
    wg_all, wu_all, wd_all, x_all, g_all, wq_out, wkv_out, wo_out, gains_out,
    query_hbm, keyval_hbm, context_hbm, normed_hbm, middle_hbm, acts_hbm, dwg_hbm, dwu_hbm, dwd_hbm,
    query_out, keyval_out, context_out, normed_out, middle_out, acts_out, dw_out,
    send, recv, local, wq_all, wkv_all, wo_all, gains_all,
    group, kv_parts, branch, branch_c, branch_y, own_normed,
    w_part, x_tile, g_tile, acc_g, acc_u, acc_d,
):
    net = Net(n, send, recv)
    d, t = net.d, net.t
    quarter = wkv_all.shape[1]
    width = wg_all.shape[1]
    cut = acts_out.shape[2]
    rows, features = tok.shape

    def block(buf, idx):
        return row_block(n, buf, idx)

    wkv_own = wkv.at[:, lanes_at(t * quarter, quarter)]
    tokens_g = TensorGather(net, lambda i: group.at[i])
    kv_g = TensorGather(net, lambda i: kv_parts.at[i])
    branch_s = TensorScatter(net, branch, branch_c, branch_y)
    first_w = Spread(net, [wq_all, wkv_all, gains_all], block)
    second_w = Spread(net, [wo_all], block)
    spread_g = WideSpread(net, g_all, late_x=True)
    spread_x = WideSpread(net, x_all)
    deals = [
        Deal(
            net,
            lambda to, w=w, at=at: w.at[:, lanes_at(to * width + at, cut)],
            lambda frm, full=full, at=at: block(full, frm).at[:, pl.ds(at, cut)],
        )
        for at in range(0, width, cut)
        for w, full in ((wg, wg_all), (wu, wu_all), (wd, wd_all))
    ]
    assert net.used <= counts
    flow = Flow(n, [deals[:3], deals[3:]], True)

    own_copies = [
        (tok, group.at[t]),
        (wq, block(wq_all, d)),
        (wkv_own, block(wkv_all, d)),
        (gains, block(gains_all, d)),
        (wo, block(wo_all, d)),
        (go, g_all.at[0, net.z]),
    ] + [
        (w.at[:, lanes_at(d * width, width)], block(full, d))
        for w, full in ((wg, wg_all), (wu, wu_all), (wd, wd_all))
    ]
    own_copies = [
        pltpu.make_async_copy(a, b, local.at[i if i < 6 else 8 + i])
        for i, (a, b) in enumerate(own_copies)
    ]
    for copy in own_copies:
        copy.start()
    net.greet()

    for copy in own_copies[:4]:
        copy.wait()
    tokens_g.begin()
    first_w.begin()
    flow.pump(pumps[0])
    own_copies[4].wait()
    own_copies[5].wait()
    tokens_g.rest()
    second_w.begin()
    spread_g.begin(go)
    flow.pump(pumps[1])

    @pl.loop(1, net.nz)
    def _(h):
        first_w.hop(h)

        @pl.when(h > 1)
        def _():
            second_w.hop(h - 1)

        spread_g.hop(h)

    flow.pump(pumps[2])
    inputs = group[...].reshape(4 * rows, features).astype(F32)
    root = inverse_root(inputs)
    first_w.cross()
    second_w.hop(net.nz - 1)
    spread_g.send_x()
    flow.pump(pumps[3])
    gain = lane_row(gains_all, 0, n)
    normed = (inputs * root * gain).astype(BF16)
    normed_out[...] = normed
    kv_parts[t] = dot_nn(normed, wkv_all[...]).astype(BF16)
    kv_g.begin()
    query_out[...] = dot_nn(normed, wq_all[...]).astype(BF16)
    flow.pump(pumps[4])
    kv_g.rest()
    for i in range(4):
        keyval_out[:, i * quarter : (i + 1) * quarter] = kv_parts[i]
    allowed = allowed_pairs(lens, 4 * rows)
    for h in range(query_out.shape[1] // HD):
        lanes = slice(h * HD, (h + 1) * HD)
        probs = softmax_head(query_out[:, lanes], keyval_out[:, :HD], allowed).astype(BF16)
        context_out[:, lanes] = dot_nn(probs, keyval_out[:, HD:]).astype(BF16)
    flow.pump(pumps[5])
    second_w.cross()
    branch[...] = dot_nt(context_out[...], wo_all[...]).astype(BF16).reshape(branch.shape)
    branch_s.begin()
    flow.pump(pumps[6])
    middle = group[t].astype(F32) + branch_s.rest()
    middle_out[...] = middle
    own_normed[...] = (middle * inverse_root(middle) * lane_row(gains_all, 1, n)).astype(BF16)
    own_x = pltpu.make_async_copy(own_normed, x_all.at[0, net.z], local.at[0])
    own_x.start()
    spread_x.begin(own_normed)
    spread_g.cross()
    flow.pump(pumps[7])
    outs = [
        pltpu.make_async_copy(a, b, local.at[1 + i])
        for i, (a, b) in enumerate(
            (
                (wq_all, wq_out),
                (wkv_all, wkv_out),
                (wo_all, wo_out),
                (gains_all, gains_out),
                (query_out, query_hbm),
                (keyval_out, keyval_hbm),
                (context_out, context_hbm),
                (normed_out, normed_hbm),
                (middle_out, middle_hbm),
            )
        )
    ]
    for copy in outs:
        copy.start()
    own_x.wait()
    spread_x.hops()
    flow.pump(pumps[8])
    spread_x.core(0)
    spread_g.core(0)
    spread_g.core(1)
    spread_x.cross()
    flow.pump(pumps[9])
    spread_x.core(1)
    for x in range(2):
        spread_g.over(x)
        spread_g.core(2 + x)
    flow.pump(pumps[10])
    for slot in range(4):
        spread_g.core_done(slot)

    for i, (copy, deal, full) in enumerate(
        zip(own_copies[6:], deals[:3], (wg_all, wu_all, wd_all))
    ):
        copy.wait()
        deal.done()
        pltpu.make_async_copy(full.at[:, pl.ds(0, cut)], w_part.at[i], local.at[14 + i]).start()
    for acc in (acc_g, acc_u, acc_d):
        acc[...] = jnp.zeros_like(acc)
    for i, full in enumerate((wg_all, wu_all, wd_all)):
        pltpu.make_async_copy(full.at[:, pl.ds(0, cut)], w_part.at[i], local.at[14 + i]).wait()
    flow.pump(pumps[11])
    tile_blocks = x_tile.shape[0]
    tile = tile_blocks * rows

    @pl.loop(0, 8)
    def _(k):
        slot = k % 2 + 4 * ((k // 2) % 2) + 2 * (k // 4)
        for at in range(1, 8):

            @pl.when(k == at)
            def _():
                flow.pump(pumps[11 + at])

        for at, slot_from in ((2, 0), (3, 1), (6, 2), (7, 3)):

            @pl.when(k == at)
            def _():
                spread_x.core_done(slot_from)

        for at, x in ((4, 0), (5, 1)):

            @pl.when(k == at)
            def _():
                spread_x.over(x)
                spread_x.core(2 + x)

        @pl.loop(0, net.nz // tile_blocks)
        def _(sub):
            part = pl.ds(sub * tile_blocks, tile_blocks)
            loads = [
                pltpu.make_async_copy(a.at[slot, part], b, local.at[14 + i])
                for i, (a, b) in enumerate(((x_all, x_tile), (g_all, g_tile)))
            ]
            for load in loads:
                load.start()
            for load in loads:
                load.wait()
            x = x_tile[...].reshape(tile, features)
            g = g_tile[...].reshape(tile, features)
            hidden, grad_gate, grad_up = feed_forward(x, g, w_part[0], w_part[1], w_part[2])
            start = pl.multiple_of((slot * net.nz + sub * tile_blocks) * rows, tile)
            acts_out[0, pl.ds(start, tile), :] = hidden
            acts_out[1, pl.ds(start, tile), :] = grad_gate
            acts_out[2, pl.ds(start, tile), :] = grad_up
            acc_g[...] += dot_tn(x, grad_gate)
            acc_u[...] += dot_tn(x, grad_up)
            acc_d[...] += dot_tn(g, hidden)

    flow.rest()
    more_outs = [pltpu.make_async_copy(acts_out, acts_hbm, local.at[10])]
    for i, (total, place) in enumerate(((acc_g, dwg_hbm), (acc_u, dwu_hbm), (acc_d, dwd_hbm))):
        dw_out[i] = total[...].astype(BF16)
        more_outs.append(pltpu.make_async_copy(dw_out.at[i], place, local.at[11 + i]))
    for copy in more_outs:
        copy.start()
    for deal in deals[3:]:
        deal.done()
    for copy in outs + more_outs:
        copy.wait()
    net.finish()


def second_kernel(
    n, counts, staged, pumps,
    lens, x_all, g_all, acts_first, wg_all, wu_all, wd_all, dwg, dwu, dwd,
    wq_all, wkv_all, wo_all, normed,
    tok, go, gains_all, query, keyval, context, middle,
    block_out, grad_tokens, grad_gains, grad_wq, grad_wkv, grad_wo, grad_wg, grad_wu, grad_wd,
    dx_c, dx_y, dx_x, dx_z, o_c, o_y, o_x, o_z,
    send, recv, local, stage, dw_part,
    acc, branch_rows, gkv, gkv_c, gkv_y, qpart, qpart_c, qpart_y,
    context_all, query_all, key_all, norm_parts, norm_land, branch_parts, branch_land, k_rows,
    gain_parts, gain_land, gain_sum, grad_query, normed_own,
):
    net = Net(n, send, recv)
    d, t = net.d, net.t
    nz = net.nz
    depth, heads = grad_wq.shape
    features, width = wg_all.shape
    cut = acts_first.shape[2]
    two = cut < width
    rows = tok.shape[0]
    quarter = wkv_all.shape[1]
    blocks = 256 // rows
    tile = blocks * rows
    subs = nz // blocks

    def block(buf, idx):
        return row_block(n, buf, idx)

    mem = Staged(stage, local.at[0]) if staged else Direct()
    scatter_dx = WideScatter(net, dx_c, dx_y, dx_x, dx_z, mem, subs)
    scatter_o = WideScatter(net, o_c, o_y, o_x, o_z, mem, subs)
    branch_g = TensorGather(net, lambda i: branch_rows.at[i])
    kv_s = TensorScatter(net, gkv, gkv_c, gkv_y)
    query_s = TensorScatter(net, qpart, qpart_c, qpart_y)
    kv_g = TensorGather(net, lambda i: k_rows.at[i])
    gain_deal = Deal(net, lambda to: gain_parts.at[to], lambda frm: gain_land.at[frm])
    gain_g = TensorGather(net, lambda i: gain_sum.at[i])
    context_s = Spread(net, [context_all], block)
    query_g = Spread(net, [query_all], block)
    key_g = Spread(net, [key_all], block)
    norm_cols = Columns(net, norm_parts, norm_land)
    branch_cols = Columns(net, branch_parts, branch_land)
    outs = (grad_wg, grad_wu, grad_wd)
    deals = [
        Deal(
            net,
            lambda to, p=part: block(p, to),
            lambda frm, o=out: o.at[:, lanes_at(frm * width, cut)],
        )
        for part, out in zip((dwg, dwu, dwd), outs)
    ]
    if two:
        deals += [
            Deal(
                net,
                lambda to, i=i: block(dw_part.at[i], to),
                lambda frm, o=out: o.at[:, lanes_at(frm * width + cut, cut)],
            )
            for i, out in enumerate(outs)
        ]
    flow = Flow(n, [deals[:3], deals[3:]], False)
    first_half = 3 * (n - 1)
    copies = [
        pltpu.make_async_copy(deal.src(d), deal.dst(d), local.at[1 + i])
        for i, deal in enumerate(deals)
    ]
    for copy in copies[:3]:
        copy.start()
    own_rows = pltpu.make_async_copy(
        normed.at[pl.ds(pl.multiple_of(t * rows, rows), rows)], normed_own, local.at[6]
    )
    own_rows.start()
    block(context_all, d)[...] = context[...]

    def ffn(wg_v, wu_v, wd_v, acts, x_tiles, g_tiles, x_cols, g_cols, one):
        w_loads = [
            pltpu.make_async_copy(a, b, local.at[7 + i])
            for i, (a, b) in enumerate(
                (
                    (wg_all, wg_v), (wu_all, wu_v), (wd_all, wd_v),
                    (acts_first, acts.at[:, :, pl.ds(0, cut)]),
                )
            )
        ]
        for load in w_loads:
            load.start()

        def place(k):
            step = k // subs
            core, y, x, sub = 1 - (step // 2) % 2, 1 - step // 4, 1 - step % 2, k % subs
            start = pl.multiple_of(((4 * core + 2 * y + x) * nz + sub * blocks) * rows, tile)
            return core, y, x, sub, pl.ds(start, tile)

        def loads(k):
            core, y, x, sub, _ = place(k)
            part = pl.ds(sub * blocks, blocks)
            return [
                pltpu.make_async_copy(
                    a.at[4 * core + 2 * y + x, part], b.at[k % 2], local.at[11 + 2 * i + k % 2]
                )
                for i, (a, b) in enumerate(((x_all, x_tiles), (g_all, g_tiles)))
            ]

        def hand_over(scatter, value, k):
            core, y, x, sub, _ = place(k)

            @pl.when(k > 0)
            def _():
                core_before, y_before, x_before, sub_before, _ = place(k - 1)

                @pl.when(core_before == 1)
                def _():
                    scatter.core_sent(2 * y_before + x_before, sub_before)

            @pl.when(core == 1)
            def _():
                one[...] = value.astype(BF16).reshape(one.shape)
                scatter.to_core(one, 2 * y + x, sub)

            @pl.when(core == 0)
            def _():
                scatter.keep(value, 2 * y + x, sub)

        if two:
            for load in loads(0):
                load.start()
        net.greet()
        context_s.begin()
        own_rows.wait()
        norm_cols.begin(normed_own[...])
        flow.pump(pumps[0], first_half)
        for load in w_loads:
            load.wait()
        more = slice(cut, width)

        @pl.loop(0, 8 * subs)
        def _(k):
            core, y, x, sub, here = place(k)
            if two:

                @pl.when(k + 1 < 8 * subs)
                def _():
                    for load in loads(k + 1):
                        load.start()

                for load in loads(k):
                    load.wait()
                done = feed_forward(
                    x_tiles[k % 2].reshape(tile, features),
                    g_tiles[k % 2].reshape(tile, features),
                    wg_v[:, more], wu_v[:, more], wd_v[:, more],
                )
                for i, act in enumerate(done):
                    acts[i, here, more] = act
            dx = dot_nt(acts[1, here, :], wg_v[...]) + dot_nt(acts[2, here, :], wu_v[...])
            hand_over(scatter_dx, dx, k)
            @pl.when((core == 0) & (y == 1))
            def _():
                @pl.loop(0, blocks)
                def _(i):
                    scatter_dx.to_y(x, sub * blocks + blocks - 1 - i)

        @pl.loop(0, 8 * subs)
        def _(k):
            hand_over(scatter_o, dot_nt(acts[0, place(k)[4], :], wd_v[...]), k)

        scatter_dx.over()
        if two:

            def second_gradients(start, columns):
                for i, block in enumerate(weight_blocks(columns, acts, more)):
                    dw_part[i, pl.ds(start, block.shape[0]), :] = block.astype(BF16)

            by_columns(x_all, g_all, x_cols, g_cols, local.at[pl.ds(11, 4)], second_gradients)

    weights = pltpu.VMEM((features, width), BF16)
    tiles = pltpu.VMEM((2, blocks, rows, features), BF16)
    chunks = pltpu.VMEM((2, 8, nz, rows, 256), BF16)
    pl.run_scoped(
        ffn, weights, weights, weights, pltpu.VMEM((3, 8 * nz * rows, width), BF16),
        tiles, tiles, chunks, chunks, pltpu.VMEM((blocks, rows, features), BF16),
    )
    if two:
        for copy in copies[3:]:
            copy.start()
    flow.pump(pumps[1])
    scatter_o.all_to_y(1)
    scatter_dx.lines()
    flow.pump(pumps[2])
    context_s.hop(1)
    scatter_dx.total(acc)

    def attention(wq_v, wo_v, wkv_v):
        attn_loads = [
            pltpu.make_async_copy(a, b, local.at[7 + i])
            for i, (a, b) in enumerate(((wq_all, wq_v), (wo_all, wo_v), (wkv_all, wkv_v)))
        ]
        for load in attn_loads:
            load.start()
        rows_in = middle[...]
        root = inverse_root(rows_in)
        grad_normed = acc[...]
        gain = lane_row(gains_all, 1, n)
        scaled = grad_normed * gain
        inner = jnp.mean(scaled * rows_in, axis=-1, keepdims=True)
        grad_middle = go[...].astype(F32) + root * (scaled - rows_in * (root * root) * inner)
        branch_rows[t] = grad_middle.astype(BF16)
        branch_g.begin()
        grad_tokens[...] = grad_middle
        gain_ffn = jnp.sum(grad_normed * rows_in * root, axis=0, keepdims=True)
        branch_cols.begin(grad_middle.astype(BF16))
        flow.pump(pumps[3])
        for load in attn_loads:
            load.wait()
        branch_g.rest()
        scatter_o.all_to_y(0)
        context_s.hop(2)
        grad_branch = branch_rows[...].reshape(4 * rows, features)
        grad_context = dot_nn(grad_branch, wo_v[...]).astype(BF16)
        pl.loop(3, nz)(context_s.hop)
        scatter_o.over()
        norm_cols.gather()
        flow.pump(pumps[4])

        allowed = allowed_pairs(lens, 4 * rows)
        key, value = keyval[:, :HD], keyval[:, HD:]
        grad_key = jnp.zeros((4 * rows, HD), F32)
        grad_value = jnp.zeros((4 * rows, HD), F32)
        factor = HD ** (-0.5)
        for h in range(heads // HD):
            lanes = slice(h * HD, (h + 1) * HD)
            probs = softmax_head(query[:, lanes], key, allowed)
            grad_head = grad_context[:, lanes]
            grad_probs = dot_nt(grad_head, value)
            inner = jnp.sum(grad_probs * probs, axis=-1, keepdims=True)
            grad_scores = (probs * (grad_probs - inner)).astype(BF16)
            grad_query[:, lanes] = (dot_nn(grad_scores, key) * factor).astype(BF16)
            grad_key += dot_tn(grad_scores, query[:, lanes]) * factor
            grad_value += dot_tn(probs.astype(BF16), grad_head)
        block(query_all, d)[...] = grad_query[...]
        query_g.begin()
        both = jnp.concatenate([grad_key, grad_value], axis=1).astype(BF16)
        for i in range(4):
            gkv[i] = both[:, i * quarter : (i + 1) * quarter]
        kv_s.begin()
        flow.pump(pumps[5])
        term = dot_nt(grad_query[...], wq_v[...])
        grad_kv = kv_s.rest().astype(BF16)
        block(key_all, d)[...] = grad_kv
        key_g.begin()
        term += dot_nt(grad_kv, wkv_v[...])
        qpart[...] = term.astype(BF16).reshape(qpart.shape)
        query_s.begin()
        branch_cols.gather()
        query_g.hop(1)
        key_g.hop(1)
        flow.pump(pumps[6])
        grad_normed = query_s.rest()

        rows_in = tok[...].astype(F32)
        root = inverse_root(rows_in)
        gain = lane_row(gains_all, 0, n)
        scaled = grad_normed * gain
        inner = jnp.mean(scaled * rows_in, axis=-1, keepdims=True)
        grad_tokens[...] += root * (scaled - rows_in * (root * root) * inner)
        gain_attn = jnp.sum(grad_normed * rows_in * root, axis=0, keepdims=True)
        for i in range(n):
            lanes = slice(i * depth, (i + 1) * depth)
            gain_parts[i, 0:1, :] = gain_attn[:, lanes]
            gain_parts[i, 1:2, :] = gain_ffn[:, lanes]
            gain_parts[i, 2:8, :] = jnp.zeros((6, depth), F32)
        gain_deal.begin()
        query_g.hop(2)
        key_g.hop(2)
        scatter_o.line_step(0)
        flow.pump(pumps[7])
        context_s.cross()
        branch_cols.rest()
        branch_cols.times(context_all, grad_wo)

        @pl.loop(3, nz)
        def _(h):
            query_g.hop(h)
            key_g.hop(h)
            scatter_o.line_step(h - 2)

        flow.pump(pumps[8])
        norm_cols.rest()
        key_g.cross()
        norm_cols.times(key_all, k_rows.at[t])
        kv_g.begin()
        gain_land[d] = gain_parts[d]
        gain_deal.done()
        gain_sum[t] = jnp.sum(gain_land[...], axis=0)
        gain_g.begin()
        flow.rest()
        scatter_o.line_step(nz - 2)
        scatter_o.meet(net.z)
        query_g.cross()
        norm_cols.times(query_all, grad_wq)
        gain_g.rest()
        grad_gains[...] = jnp.sum(gain_sum[...], axis=0)
        kv_g.rest()
        for i in range(4):
            grad_wkv[:, i * quarter : (i + 1) * quarter] = k_rows[i]
        scatter_o.total(acc)
        block_out[...] = (middle[...] + acc[...]).astype(BF16)

    assert net.used <= counts
    projection = pltpu.VMEM((features, heads), BF16)
    part = pltpu.VMEM((features, quarter), BF16)
    pl.run_scoped(attention, projection, projection, part)
    for deal in deals:
        deal.done()
    for copy in copies:
        copy.wait()
    net.finish()


def finish_kernel(wg, wu, wd, tokens, wq, wkv, wo, block, wg_o, wu_o, wd_o, tokens_o, wq_o, wkv_o, wo_o, block_o):
    for a, b in ((wg, wg_o), (wu, wu_o), (wd, wd_o)):
        b[...] = a[...].astype(F32)

    @pl.when(pl.program_id(0) == 0)
    def _():
        for a, b in ((tokens, tokens_o), (wq, wq_o), (wkv, wkv_o), (wo, wo_o), (block, block_o)):
            b[...] = a[...]


def params(collective_id):
    return pltpu.CompilerParams(
        collective_id=collective_id, has_side_effects=True, vmem_limit_bytes=63 * MIB
    )


PUMPS_1 = (0.119, 0.0, 0.048, 0.048, 0.048, 0.048, 0.048, 0.095, 0.095, 0.095, 0.095, 0.095, 0.167, 0.0, 0.0, 0.0, 0.0, 0.0, 0.0)
PUMPS_2 = (0.452, 0.0, 0.024, 0.19, 0.143, 0.095, 0.095, 0.0, 0.0, 0.0)


def body(
    n, tokens, grad_out, lengths, gain_attn, gain_ffn, w_query, w_keyval, w_out, w_gate, w_up, w_down
):
    nz = n // 2
    rows, features = tokens.shape
    depth, heads = w_query.shape
    quarter = w_keyval.shape[1] // 4
    width = w_gate.shape[1] // n
    group_rows = 4 * rows
    shape = jax.ShapeDtypeStruct
    gains = jnp.concatenate(
        [gain_attn[None], gain_ffn[None], jnp.zeros((6, depth), gain_attn.dtype)]
    ).astype(F32)

    cut = width // 2 if width // 2 % 128 == 0 else width
    parts = width // cut
    tile_blocks = 256 // rows
    counts = 9 + 4 * 3 * nz + 2 * (5 * nz + 4) + 3 * parts * n
    full = shape((features, width), BF16)
    part = shape((features, cut), BF16)
    wide = shape((8, nz, rows, features), BF16)
    all_rows = 4 * n * rows
    (
        wg_all, wu_all, wd_all, x_all, g_all, wq_all, wkv_all, wo_all, gains_all,
        query, keyval, context, normed, middle, acts, dwg, dwu, dwd,
    ) = pl.pallas_call(
        functools.partial(first_kernel, n, counts, PUMPS_1),
        out_shape=(
            full, full, full, wide, wide,
            shape((features, heads), BF16),
            shape((features, quarter), BF16),
            shape((features, heads), BF16),
            shape((8 * n, depth), F32),
            shape((group_rows, heads), BF16),
            shape((group_rows, 2 * HD), BF16),
            shape((group_rows, heads), BF16),
            shape((group_rows, features), BF16),
            shape((rows, features), F32),
            shape((3, all_rows, cut), BF16),
            part, part, part,
        ),
        in_specs=[SMEM] + [ANY] * 9,
        out_specs=(ANY,) * 18,
        scratch_shapes=[
            pltpu.VMEM((group_rows, heads), BF16),
            pltpu.VMEM((group_rows, 2 * HD), BF16),
            pltpu.VMEM((group_rows, heads), BF16),
            pltpu.VMEM((group_rows, features), BF16),
            pltpu.VMEM((rows, features), F32),
            pltpu.VMEM((3, all_rows, cut), BF16),
            pltpu.VMEM((3, features, cut), BF16),
            pltpu.SemaphoreType.DMA((counts,)),
            pltpu.SemaphoreType.DMA((counts,)),
            pltpu.SemaphoreType.DMA((17,)),
            pltpu.VMEM((features, heads), BF16),
            pltpu.VMEM((features, quarter), BF16),
            pltpu.VMEM((features, heads), BF16),
            pltpu.VMEM((8 * n, depth), F32),
            pltpu.VMEM((4, rows, features), BF16),
            pltpu.VMEM((4, group_rows, quarter), BF16),
            pltpu.VMEM((4, rows, features), BF16),
            pltpu.VMEM((2, rows, features), BF16),
            pltpu.VMEM((rows, features), BF16),
            pltpu.VMEM((rows, features), BF16),
            pltpu.VMEM((3, features, cut), BF16),
            pltpu.VMEM((tile_blocks, rows, features), BF16),
            pltpu.VMEM((tile_blocks, rows, features), BF16),
        ]
        + [pltpu.VMEM((features, cut), F32)] * 3,
        compiler_params=params(0),
        name="forward",
    )(lengths, tokens, grad_out, gains, w_query, w_keyval, w_out, w_gate, w_up, w_down)

    staged = n > 8
    subs = nz // tile_blocks
    counts = 2 * (4 * subs + 5 * nz) + 3 * 3 * nz + 21 + 3 * n + 3 * parts * n
    landing = [
        shape((4, nz, rows, features), BF16),
        shape((2, nz, rows, features), BF16),
        shape((nz, rows, features), BF16),
        shape((nz + 1, rows, features), BF16),
    ] * 2
    out_shape = [
        shape((rows, features), BF16),
        shape((rows, features), F32),
        shape((8, depth), F32),
        shape((depth, heads), F32),
        shape((depth, 4 * quarter), F32),
        shape((depth, heads), F32),
        shape((depth, n * width), BF16),
        shape((depth, n * width), BF16),
        shape((depth, n * width), BF16),
    ]
    out_specs = [VMEM] * 6 + [ANY] * 3
    in_vmem = []
    if staged:
        out_shape += landing
        out_specs += [ANY] * len(landing)
    else:
        in_vmem = [pltpu.VMEM(place.shape, place.dtype) for place in landing]

    results = pl.pallas_call(
        functools.partial(second_kernel, n, counts, staged, PUMPS_2),
        out_shape=tuple(out_shape),
        in_specs=[SMEM] + [ANY] * 13 + [VMEM] * 7,
        out_specs=tuple(out_specs),
        scratch_shapes=in_vmem
        + [
            pltpu.SemaphoreType.DMA((counts,)),
            pltpu.SemaphoreType.DMA((counts,)),
            pltpu.SemaphoreType.DMA((15,)),
            pltpu.VMEM((tile_blocks if staged else 1, rows, features), BF16),
            pltpu.VMEM((3, features, cut if parts > 1 else 128), BF16),
            pltpu.VMEM((rows, features), F32),
            pltpu.VMEM((4, rows, features), BF16),
            pltpu.VMEM((4, group_rows, quarter), BF16),
            pltpu.VMEM((2, group_rows, quarter), BF16),
            pltpu.VMEM((group_rows, quarter), BF16),
            pltpu.VMEM((4, rows, features), BF16),
            pltpu.VMEM((2, rows, features), BF16),
            pltpu.VMEM((rows, features), BF16),
        ]
        + [
            pltpu.VMEM((n * group_rows, heads), BF16),
            pltpu.VMEM((n * group_rows, heads), BF16),
            pltpu.VMEM((n * group_rows, quarter), BF16),
            pltpu.VMEM((n, rows, depth), BF16),
            pltpu.VMEM((4, n, rows, depth), BF16),
            pltpu.VMEM((n, rows, depth), BF16),
            pltpu.VMEM((4, n, rows, depth), BF16),
            pltpu.VMEM((4, depth, quarter), F32),
            pltpu.VMEM((n, 8, depth), F32),
            pltpu.VMEM((n, 8, depth), F32),
            pltpu.VMEM((4, 8, depth), F32),
            pltpu.VMEM((group_rows, heads), BF16),
            pltpu.VMEM((rows, features), BF16),
        ],
        compiler_params=params(1),
        name="backward",
    )(
        lengths, x_all, g_all, acts, wg_all, wu_all, wd_all, dwg, dwu, dwd,
        wq_all, wkv_all, wo_all, normed,
        tokens, grad_out, gains_all, query, keyval, context, middle,
    )
    block_out, grad_tokens, grad_gains, grad_wq, grad_wkv, grad_wo, grad_wg, grad_wu, grad_wd = (
        results[:9]
    )
    chunks = 4
    column_block = pl.BlockSpec((depth, n * width // chunks), lambda i: (0, i))
    small = [
        pl.BlockSpec(a.shape, lambda i: (0, 0)) for a in (grad_tokens, grad_wq, grad_wkv, grad_wo, block_out)
    ]
    grad_wg, grad_wu, grad_wd, grad_tokens, grad_wq, grad_wkv, grad_wo, block_out = pl.pallas_call(
        finish_kernel,
        grid=(chunks,),
        out_shape=tuple(shape((depth, n * width), F32) for _ in range(3))
        + tuple(
            shape(a.shape, a.dtype) for a in (grad_tokens, grad_wq, grad_wkv, grad_wo, block_out)
        ),
        in_specs=[column_block] * 3 + small,
        out_specs=[column_block] * 3 + small,
        compiler_params=pltpu.CompilerParams(vmem_limit_bytes=48 * MIB),
        name="results",
    )(grad_wg, grad_wu, grad_wd, grad_tokens, grad_wq, grad_wkv, grad_wo, block_out)
    return (
        block_out,
        grad_tokens,
        grad_gains[0],
        grad_gains[1],
        grad_wq,
        grad_wkv,
        grad_wo,
        grad_wg,
        grad_wu,
        grad_wd,
    )


def solution(mesh):
    rows = P(("dp", "tensor"), None)
    both = P("dp", "tensor")
    return jax.shard_map(
        functools.partial(body, mesh.shape["dp"]),
        mesh=mesh,
        in_specs=(rows, rows, P("dp", None), P("dp"), P("dp"), both, P("dp", None), both, both, both, both),
        out_specs=(rows, rows, P("dp"), P("dp"), both, P("dp", None), both, both, both, both),
        check_vma=False,
    )
```

```python
import functools

import jax
import jax.numpy as jnp
from jax import lax
from jax.experimental import pallas as pl
from jax.experimental.pallas import tpu as pltpu
from jax.sharding import PartitionSpec as P

HD = 256
WINDOW = 2048
NORM_EPS = 1e-06
MASKED = -1e30
BF16, F32 = jnp.bfloat16, jnp.float32
MESH = pl.DeviceIdType.MESH
ANY = pl.BlockSpec(memory_space=pl.ANY)
VMEM = pl.BlockSpec(memory_space=pltpu.VMEM)
SMEM = pl.BlockSpec(memory_space=pltpu.SMEM)
MIB = 1 << 20


def dot_nn(a, b):
    return lax.dot_general(a, b, (((1,), (0,)), ((), ())), preferred_element_type=F32)


def dot_nt(a, b):
    return lax.dot_general(a, b, (((1,), (1,)), ((), ())), preferred_element_type=F32)


def dot_tn(a, b):
    return lax.dot_general(a, b, (((0,), (0,)), ((), ())), preferred_element_type=F32)


class Net:
    def __init__(self, n, send, recv):
        self.n, self.nz = n, n // 2
        self.send, self.recv, self.used = send, recv, 0
        self.d = lax.axis_index("dp")
        self.t = lax.axis_index("tensor")
        self.z = self.d // 2
        self.x = self.d % 2
        self.dx = self.d + 1 - 2 * self.x
        self.ty = (self.t + 2) % 4
        self.tc = self.t + 1 - 2 * (self.t % 2)
        self.tcy = (self.tc + 2) % 4
        self.ends = []

    def take(self, count):
        first = self.used
        self.used += count
        return first

    def dp(self, other):
        return (other, self.t)

    def tensor(self, other):
        return (self.d, other)

    def make(self, src, dst, k, device):
        return pltpu.make_async_remote_copy(
            src_ref=src,
            dst_ref=dst,
            send_sem=self.send.at[k],
            recv_sem=self.recv.at[k],
            device_id=device,
            device_id_type=MESH,
        )

    def start(self, src, dst, k, device):
        self.make(src, dst, k, device).start()

    def landed(self, ref, k):
        self.make(ref, ref, k, self.tensor(self.tc)).wait_recv()

    def sent(self, ref, k):
        self.make(ref, ref, k, self.tensor(self.tc)).wait_send()

    def pair(self, m):
        other, bit = 0, 1
        while bit < self.n:
            low, mask = (self.d // bit) % 2, (m // bit) % 2
            other = other + bit * (low + mask - 2 * low * mask)
            bit *= 2
        return other

    def greet(self):
        barrier = pltpu.get_barrier_semaphore()

        @pl.loop(1, self.n)
        def _(m):
            pl.semaphore_signal(
                barrier, inc=1, device_id=self.dp((self.d + m) % self.n), device_id_type=MESH
            )

        for other in (self.ty, self.tc):
            pl.semaphore_signal(
                barrier, inc=1, device_id=self.tensor(other), device_id_type=MESH
            )
        pl.semaphore_wait(barrier, self.n + 1)

    def finish(self):
        for end in self.ends:
            end()


class TensorGather:
    def __init__(self, net, at):
        self.net, self.at, self.k = net, at, net.take(3)
        net.ends.append(self.end)

    def begin(self):
        net = self.net
        net.start(self.at(net.t), self.at(net.t), self.k, net.tensor(net.ty))
        net.start(self.at(net.t), self.at(net.t), self.k + 1, net.tensor(net.tc))

    def rest(self):
        net = self.net
        net.landed(self.at(net.ty), self.k)
        net.start(self.at(net.ty), self.at(net.ty), self.k + 2, net.tensor(net.tc))
        net.landed(self.at(net.tc), self.k + 1)
        net.landed(self.at(net.tcy), self.k + 2)

    def end(self):
        for i in range(3):
            self.net.sent(self.at(0), self.k + i)


class TensorScatter:
    def __init__(self, net, part, cl, yl):
        self.net, self.part, self.cl, self.yl, self.k = net, part, cl, yl, net.take(3)
        net.ends.append(self.end)

    def begin(self):
        net = self.net
        net.start(self.part.at[net.tcy], self.cl.at[1], self.k + 1, net.tensor(net.tc))
        net.start(self.part.at[net.tc], self.cl.at[0], self.k, net.tensor(net.tc))

    def rest(self):
        net = self.net
        net.landed(self.cl.at[1], self.k + 1)
        pair = self.part[net.ty].astype(F32) + self.cl[1].astype(F32)
        self.part[net.ty] = pair.astype(self.part.dtype)
        net.start(self.part.at[net.ty], self.yl, self.k + 2, net.tensor(net.ty))
        net.landed(self.cl.at[0], self.k)
        own = self.part[net.t].astype(F32) + self.cl[0].astype(F32)
        net.landed(self.yl, self.k + 2)
        return own + self.yl[...].astype(F32)

    def end(self):
        for i in range(3):
            self.net.sent(self.yl, self.k + i)


class Spread:
    def __init__(self, net, bufs, block):
        self.net, self.bufs, self.block = net, bufs, block
        self.zk = [net.take(2 * net.nz) for _ in bufs]
        self.xk = [net.take(net.nz) for _ in bufs]
        net.ends.append(self.end)

    def line(self, j, zb, right):
        net = self.net
        here = self.block(self.bufs[j], 2 * zb + net.x)
        if right:
            net.start(here, here, self.zk[j] + zb, net.dp(net.d + 2))
        else:
            net.start(here, here, self.zk[j] + net.nz + zb, net.dp(net.d - 2))

    def over_x(self, j, zb):
        net = self.net
        here = self.block(self.bufs[j], 2 * zb + net.x)
        net.start(here, here, self.xk[j] + zb, net.dp(net.dx))

    def begin(self):
        net = self.net
        for j in range(len(self.bufs)):

            @pl.when(net.z < net.nz - 1)
            def _():
                self.line(j, net.z, True)

            @pl.when(net.z > 0)
            def _():
                self.line(j, net.z, False)

            self.over_x(j, net.z)

    def hop(self, h):
        net = self.net
        nz = net.nz
        for j, buf in enumerate(self.bufs):

            @pl.when(net.z - h >= 0)
            def _():
                zb = net.z - h
                net.landed(self.block(buf, 2 * zb + net.x), self.zk[j] + zb)

                @pl.when(net.z < nz - 1)
                def _():
                    self.line(j, zb, True)

                self.over_x(j, zb)

            @pl.when(net.z + h <= nz - 1)
            def _():
                zb = net.z + h
                net.landed(self.block(buf, 2 * zb + net.x), self.zk[j] + nz + zb)

                @pl.when(net.z > 0)
                def _():
                    self.line(j, zb, False)

                self.over_x(j, zb)

    def cross(self):
        net = self.net

        @pl.loop(0, net.nz)
        def _(k):
            zb = (net.z + k) % net.nz
            for j, buf in enumerate(self.bufs):
                net.landed(self.block(buf, 2 * zb + 1 - net.x), self.xk[j] + zb)

    def end(self):
        net = self.net

        @pl.loop(0, net.nz)
        def _(zb):
            for j, buf in enumerate(self.bufs):
                some = self.block(buf, 0)

                @pl.when((zb <= net.z) & (net.z < net.nz - 1))
                def _():
                    net.sent(some, self.zk[j] + zb)

                @pl.when((zb >= net.z) & (net.z > 0))
                def _():
                    net.sent(some, self.zk[j] + net.nz + zb)

                net.sent(some, self.xk[j] + zb)


class WideSpread:
    def __init__(self, net, buf, late_x=False):
        self.net, self.buf, self.late_x = net, buf, late_x
        self.zk, self.xk = net.take(2 * net.nz), net.take(net.nz)
        self.yk, self.ck = net.take(2 * net.nz), net.take(4)
        net.ends.append(self.end)

    def onward(self, src, zb, right, left):
        net, buf = self.net, self.buf
        if right:

            @pl.when(net.z < net.nz - 1)
            def _():
                net.start(src, buf.at[0, zb], self.zk + zb, net.dp(net.d + 2))

        if left:

            @pl.when(net.z > 0)
            def _():
                net.start(src, buf.at[0, zb], self.zk + net.nz + zb, net.dp(net.d - 2))

        net.start(src, buf.at[2, zb], self.yk + zb, net.tensor(net.ty))
        if not self.late_x:
            net.start(src, buf.at[1, zb], self.xk + zb, net.dp(net.dx))

    def send_x(self):
        net = self.net

        @pl.loop(0, net.nz)
        def _(k):
            zb = (net.z + k) % net.nz
            net.start(self.buf.at[0, zb], self.buf.at[1, zb], self.xk + zb, net.dp(net.dx))

    def begin(self, own):
        self.onward(own, self.net.z, True, True)

    def hop(self, h):
        net, buf = self.net, self.buf

        @pl.when(net.z - h >= 0)
        def _():
            zb = net.z - h
            net.landed(buf.at[0, zb], self.zk + zb)
            self.onward(buf.at[0, zb], zb, True, False)

        @pl.when(net.z + h <= net.nz - 1)
        def _():
            zb = net.z + h
            net.landed(buf.at[0, zb], self.zk + net.nz + zb)
            self.onward(buf.at[0, zb], zb, False, True)

    def hops(self):
        @pl.loop(1, self.net.nz)
        def _(h):
            self.hop(h)

    def cross(self):
        net, buf = self.net, self.buf

        @pl.loop(0, net.nz)
        def _(k):
            zb = (net.z + k) % net.nz
            net.landed(buf.at[1, zb], self.xk + zb)
            net.start(buf.at[1, zb], buf.at[3, zb], self.yk + net.nz + zb, net.tensor(net.ty))

    def over(self, x):
        net = self.net

        @pl.loop(0, net.nz)
        def _(k):
            zb = (net.z + k) % net.nz
            net.landed(self.buf.at[2 + x, zb], self.yk + x * net.nz + zb)

    def core(self, slot):
        net = self.net
        net.start(self.buf.at[slot], self.buf.at[4 + slot], self.ck + slot, net.tensor(net.tc))

    def core_done(self, slot):
        self.net.landed(self.buf.at[4 + slot], self.ck + slot)

    def end(self):
        net = self.net
        some = self.buf.at[0, 0]

        @pl.loop(0, net.nz)
        def _(zb):
            @pl.when((zb <= net.z) & (net.z < net.nz - 1))
            def _():
                net.sent(some, self.zk + zb)

            @pl.when((zb >= net.z) & (net.z > 0))
            def _():
                net.sent(some, self.zk + net.nz + zb)

            net.sent(some, self.xk + zb)
            net.sent(some, self.yk + zb)
            net.sent(some, self.yk + net.nz + zb)

        for slot in range(4):
            net.sent(self.buf.at[0], self.ck + slot)


class Deal:
    def __init__(self, net, src, dst):
        self.net, self.src, self.dst, self.k = net, src, dst, net.take(net.n)
        net.ends.append(self.end)

    def send(self, m):
        net = self.net
        to = net.pair(m)
        net.start(self.src(to), self.dst(net.d), self.k + m, net.dp(to))

    def begin(self):
        pl.loop(1, self.net.n)(self.send)

    def done(self):
        net = self.net

        @pl.loop(1, net.n)
        def _(m):
            net.landed(self.dst(net.pair(m)), self.k + m)

    def end(self):
        net = self.net

        @pl.loop(1, net.n)
        def _(m):
            net.sent(self.src(0), self.k + m)


class Flow:
    def __init__(self, n, groups, key):
        self.todo = []
        for deals in groups:
            pairs = sorted(range(1, n), key=key)
            self.todo += [(deal, m) for deal in deals for m in pairs]
        self.gone, self.share = 0, 0.0

    def pump(self, share, limit=None):
        self.share += share
        upto = min(round(self.share * len(self.todo)), len(self.todo) if limit is None else limit)
        for deal, m in self.todo[self.gone : upto]:
            deal.send(m)
        self.gone = max(upto, self.gone)

    def rest(self):
        self.pump(1.0)


class Columns:
    def __init__(self, net, parts, land):
        self.net, self.parts, self.land = net, parts, land
        self.deal = Deal(net, lambda to: parts.at[to], lambda frm: land.at[net.t, frm])
        self.over = TensorGather(net, lambda i: land.at[i])

    def begin(self, rows):
        depth = self.parts.shape[2]
        for i in range(self.net.n):
            self.parts[i] = rows[:, i * depth : (i + 1) * depth]
        self.land[self.net.t, self.net.d] = self.parts[self.net.d]
        self.deal.begin()

    def gather(self):
        self.deal.done()
        self.over.begin()

    def rest(self):
        self.over.rest()

    def times(self, other, acc):
        n = self.net.n
        depth = self.parts.shape[2]
        acc[...] = jnp.zeros_like(acc)

        @pl.loop(0, n)
        def _(i):
            mine = self.land[:, i].reshape(-1, depth)
            acc[...] += dot_tn(mine, row_block(n, other, i)[...])


class Scatter:
    def __init__(self, net, own, other, xl, zl, mem):
        self.net, self.own, self.other, self.xl, self.zl, self.mem = net, own, other, xl, zl, mem
        self.xk, self.rk, self.lk = net.take(net.nz), net.take(net.nz), net.take(net.nz)
        net.ends.append(self.end)

    def order(self, k):
        odd = k % 2
        return odd * (k // 2) + (1 - odd) * (self.net.nz - 1 - k // 2)

    def send_x(self, zb):
        net = self.net
        net.start(self.other(zb), self.xl.at[zb], self.xk + zb, net.dp(net.dx))

    def begin(self):
        @pl.loop(0, self.net.nz)
        def _(k):
            self.send_x(self.order(k))

    def add(self, block, other):
        mem = self.mem
        mem.put(block, (mem.get(block).astype(F32) + mem.get(other).astype(F32)).astype(BF16))

    def meet(self, zb):
        net = self.net
        net.landed(self.xl.at[zb], self.xk + zb)
        self.add(self.own(zb), self.xl.at[zb])

    def line_step(self, k):
        net = self.net
        nz = net.nz
        far = nz - 1 - k

        @pl.when(far > net.z)
        def _():
            self.meet(far)
            here = self.own(far)

            @pl.when(net.z > 0)
            def _():
                net.landed(self.zl.at[far], self.rk + far)
                self.add(here, self.zl.at[far])

            net.start(here, self.zl.at[far], self.rk + far, net.dp(net.d + 2))

        @pl.when(k < net.z)
        def _():
            self.meet(k)
            here = self.own(k)

            @pl.when(net.z < nz - 1)
            def _():
                net.landed(self.zl.at[k], self.lk + k)
                self.add(here, self.zl.at[k])

            last = (k == net.z - 1).astype(jnp.int32)
            net.start(here, self.zl.at[last * nz + (1 - last) * k], self.lk + k, net.dp(net.d - 2))

    def lines(self):
        pl.loop(0, self.net.nz - 1)(self.line_step)
        self.meet(self.net.z)

    def total(self, acc):
        net, mem = self.net, self.mem
        acc[...] = mem.get(self.own(net.z)).astype(F32)

        @pl.when(net.z > 0)
        def _():
            net.landed(self.zl.at[net.z], self.rk + net.z)
            acc[...] += mem.get(self.zl.at[net.z]).astype(F32)

        @pl.when(net.z < net.nz - 1)
        def _():
            net.landed(self.zl.at[net.nz], self.lk + net.z)
            acc[...] += mem.get(self.zl.at[net.nz]).astype(F32)

    def end(self):
        net = self.net

        @pl.loop(0, net.nz)
        def _(zb):
            net.sent(self.xl.at[0], self.xk + zb)

            @pl.when(zb > net.z)
            def _():
                net.sent(self.zl.at[0], self.rk + zb)

            @pl.when(zb < net.z)
            def _():
                net.sent(self.zl.at[0], self.lk + zb)


class WideScatter(Scatter):
    def __init__(self, net, cl, yl, xl, zl, mem, tiles):
        self.cl, self.yl, self.tiles = cl, yl, tiles
        self.ck, self.yk = net.take(4 * tiles), net.take(2 * net.nz)
        super().__init__(net, lambda zb: cl.at[0, zb], lambda zb: cl.at[1, zb], xl, zl, mem)
        net.ends.append(self.wide_end)

    def place(self, yx, sub):
        blocks = self.net.nz // self.tiles
        return self.cl.at[yx, pl.ds(sub * blocks, blocks)]

    def to_core(self, stage, yx, sub):
        net = self.net
        net.start(stage, self.place(yx, sub), self.ck + yx * self.tiles + sub, net.tensor(net.tc))

    def core_sent(self, yx, sub):
        self.net.sent(self.place(0, 0), self.ck + yx * self.tiles + sub)

    def keep(self, value, yx, sub):
        place = self.place(yx, sub)
        self.net.landed(place, self.ck + yx * self.tiles + sub)
        value = value.reshape(place.shape) + self.mem.get(place).astype(F32)
        self.mem.put(place, value.astype(BF16))

    def to_y(self, x, zb):
        net = self.net
        net.start(
            self.cl.at[2 + x, zb], self.yl.at[x, zb], self.yk + x * net.nz + zb, net.tensor(net.ty)
        )

    def all_to_y(self, x):
        @pl.loop(0, self.net.nz)
        def _(k):
            self.to_y(x, self.order(k))

    def from_y(self, x, zb):
        net = self.net
        net.landed(self.yl.at[x, zb], self.yk + x * net.nz + zb)
        self.add(self.cl.at[x, zb], self.yl.at[x, zb])

    def over(self):
        @pl.loop(0, self.net.nz)
        def _(k):
            zb = self.order(k)
            self.from_y(1, zb)
            self.send_x(zb)

    def meet(self, zb):
        self.from_y(0, zb)
        super().meet(zb)

    def wide_end(self):
        net = self.net

        @pl.loop(0, net.nz)
        def _(zb):
            net.sent(self.yl.at[0, 0], self.yk + zb)
            net.sent(self.yl.at[0, 0], self.yk + net.nz + zb)


class Direct:
    def get(self, ref):
        return ref[...]

    def put(self, ref, value):
        ref[...] = value


class Staged:
    def __init__(self, buf, sem):
        self.buf, self.sem = buf, sem

    def view(self, ref):
        return self.buf if len(ref.shape) == 3 else self.buf.at[0]

    def get(self, ref):
        view = self.view(ref)
        copy = pltpu.make_async_copy(ref, view, self.sem)
        copy.start()
        copy.wait()
        return view[...]

    def put(self, ref, value):
        view = self.view(ref)
        view[...] = value
        copy = pltpu.make_async_copy(view, ref, self.sem)
        copy.start()
        copy.wait()


def lane_row(gains, row, n):
    return jnp.concatenate([gains[8 * i + row : 8 * i + row + 1, :] for i in range(n)], axis=1)


def allowed_pairs(lens, rows):
    place_i = lax.broadcasted_iota(jnp.int32, (rows, 1), 0)
    place_j = lax.broadcasted_iota(jnp.int32, (1, rows), 1)
    segment_i = jnp.zeros((rows, 1), jnp.int32)
    segment_j = jnp.zeros((1, rows), jnp.int32)
    total = 0
    for k in range(lens.shape[1]):
        total = total + lens[0, k]
        segment_i += (place_i >= total).astype(jnp.int32)
        segment_j += (place_j >= total).astype(jnp.int32)
    distance = place_i - place_j
    return (segment_i == segment_j) & (distance >= 0) & (distance < WINDOW)


def softmax_head(query, key, allowed):
    scores = dot_nt(query, key) * HD ** (-0.5)
    scores = jnp.where(allowed, scores, MASKED)
    weights = jnp.exp(scores - jnp.max(scores, axis=-1, keepdims=True))
    return weights / jnp.sum(weights, axis=-1, keepdims=True)


def inverse_root(rows):
    return lax.rsqrt(jnp.mean(rows * rows, axis=-1, keepdims=True) + NORM_EPS)


def feed_forward(x, g, wg, wu, wd):
    gate = dot_nn(x, wg)
    up = dot_nn(x, wu)
    grad_hidden = dot_nn(g, wd)
    root = (2.0 / jnp.pi) ** 0.5
    square = gate * gate
    tanh = jnp.tanh(root * gate * (1.0 + 0.044715 * square))
    half = 0.5 * (1.0 + tanh)
    gelu = gate * half
    slope = half + 0.5 * gate * (1.0 - tanh * tanh) * (root * (1.0 + 3 * 0.044715 * square))
    hidden = (gelu * up).astype(BF16)
    grad_gate = (grad_hidden * up * slope).astype(BF16)
    grad_up = (grad_hidden * gelu).astype(BF16)
    return hidden, grad_gate, grad_up


def row_block(n, buf, idx):
    step = buf.shape[0] // n
    return buf.at[pl.ds(pl.multiple_of(idx * step, step), step)]


def lanes_at(start, size):
    return pl.ds(pl.multiple_of(start, 128), size)


def weight_blocks(columns, acts, cols):
    x_cols, g_cols = columns
    return (
        dot_tn(x_cols, acts[1, :, cols]),
        dot_tn(x_cols, acts[2, :, cols]),
        dot_tn(g_cols, acts[0, :, cols]),
    )


def by_columns(x_all, g_all, x_cols, g_cols, sems, use):
    features = x_all.shape[3]
    chunk = x_cols.shape[4]
    count = features // chunk

    def loads(c):
        lanes = lanes_at(c * chunk, chunk)
        return [
            pltpu.make_async_copy(a.at[:, :, :, lanes], b.at[c % 2], sems.at[2 * i + c % 2])
            for i, (a, b) in enumerate(((x_all, x_cols), (g_all, g_cols)))
        ]

    for load in loads(0):
        load.start()

    @pl.loop(0, count)
    def _(c):
        @pl.when(c + 1 < count)
        def _():
            for load in loads(c + 1):
                load.start()

        for load in loads(c):
            load.wait()
        use(pl.multiple_of(c * chunk, chunk), [b[c % 2].reshape(-1, chunk) for b in (x_cols, g_cols)])


def first_kernel(
    n, counts, pumps,
    lens, tok, go, gain_attn, gain_ffn, wq, wkv, wo, wg, wu, wd,
    wg_all, wu_all, wd_all, x_all, g_all, wq_out, wkv_out, wo_out, gains_out,
    query_hbm, keyval_hbm, context_hbm, normed_hbm, middle_hbm, acts_hbm, dwg_hbm, dwu_hbm, dwd_hbm,
    query_out, keyval_out, context_out, normed_out, middle_out, acts_out, dw_out,
    send, recv, local, wq_all, wkv_all, wo_all, gains_all,
    group, kv_parts, branch, branch_c, branch_y, own_normed,
    w_part, x_tile, g_tile, acc_g, acc_u, acc_d,
):
    net = Net(n, send, recv)
    d, t = net.d, net.t
    quarter = wkv_all.shape[1]
    width = wg_all.shape[1]
    cut = acts_out.shape[2]
    rows, features = tok.shape

    def block(buf, idx):
        return row_block(n, buf, idx)

    wkv_own = wkv.at[:, lanes_at(t * quarter, quarter)]
    tokens_g = TensorGather(net, lambda i: group.at[i])
    kv_g = TensorGather(net, lambda i: kv_parts.at[i])
    branch_s = TensorScatter(net, branch, branch_c, branch_y)
    first_w = Spread(net, [wq_all, wkv_all, gains_all], block)
    second_w = Spread(net, [wo_all], block)
    spread_g = WideSpread(net, g_all, late_x=True)
    spread_x = WideSpread(net, x_all)
    deals = [
        Deal(
            net,
            lambda to, w=w, at=at: w.at[:, lanes_at(to * width + at, cut)],
            lambda frm, full=full, at=at: block(full, frm).at[:, pl.ds(at, cut)],
        )
        for at in range(0, width, cut)
        for w, full in ((wg, wg_all), (wu, wu_all), (wd, wd_all))
    ]
    assert net.used <= counts
    flow = Flow(n, [deals[:3], deals[3:]], KEY_1)

    own_gains = block(gains_all, d)
    own_gains[...] = jnp.zeros(own_gains.shape, F32)
    own_gains[0:1, :] = gain_attn[...].astype(F32).reshape(1, -1)
    own_gains[1:2, :] = gain_ffn[...].astype(F32).reshape(1, -1)
    own_copies = [
        (tok, group.at[t]),
        (wq, block(wq_all, d)),
        (wkv_own, block(wkv_all, d)),
        (wo, block(wo_all, d)),
        (go, g_all.at[0, net.z]),
    ] + [
        (w.at[:, lanes_at(d * width, width)], block(full, d))
        for w, full in ((wg, wg_all), (wu, wu_all), (wd, wd_all))
    ]
    own_copies = [
        pltpu.make_async_copy(a, b, local.at[i if i < 5 else 9 + i])
        for i, (a, b) in enumerate(own_copies)
    ]
    for copy in own_copies:
        copy.start()
    net.greet()

    for copy in own_copies[:3]:
        copy.wait()
    tokens_g.begin()
    first_w.begin()
    flow.pump(pumps[0])
    own_copies[3].wait()
    own_copies[4].wait()
    tokens_g.rest()
    second_w.begin()
    spread_g.begin(go)
    flow.pump(pumps[1])

    @pl.loop(1, net.nz)
    def _(h):
        first_w.hop(h)

        @pl.when(h > 1)
        def _():
            second_w.hop(h - 1)

        spread_g.hop(h)

    flow.pump(pumps[2])
    inputs = group[...].reshape(4 * rows, features).astype(F32)
    root = inverse_root(inputs)
    first_w.cross()
    second_w.hop(net.nz - 1)
    spread_g.send_x()
    flow.pump(pumps[3])
    gain = lane_row(gains_all, 0, n)
    normed = (inputs * root * gain).astype(BF16)
    normed_out[...] = normed
    kv_parts[t] = dot_nn(normed, wkv_all[...]).astype(BF16)
    kv_g.begin()
    query_out[...] = dot_nn(normed, wq_all[...]).astype(BF16)
    flow.pump(pumps[4])
    kv_g.rest()
    for i in range(4):
        keyval_out[:, i * quarter : (i + 1) * quarter] = kv_parts[i]
    allowed = allowed_pairs(lens, 4 * rows)
    for h in range(query_out.shape[1] // HD):
        lanes = slice(h * HD, (h + 1) * HD)
        probs = softmax_head(query_out[:, lanes], keyval_out[:, :HD], allowed).astype(BF16)
        context_out[:, lanes] = dot_nn(probs, keyval_out[:, HD:]).astype(BF16)
    flow.pump(pumps[5])
    second_w.cross()
    branch[...] = dot_nt(context_out[...], wo_all[...]).astype(BF16).reshape(branch.shape)
    branch_s.begin()
    flow.pump(pumps[6])
    middle = group[t].astype(F32) + branch_s.rest()
    middle_out[...] = middle
    own_normed[...] = (middle * inverse_root(middle) * lane_row(gains_all, 1, n)).astype(BF16)
    own_x = pltpu.make_async_copy(own_normed, x_all.at[0, net.z], local.at[0])
    own_x.start()
    spread_x.begin(own_normed)
    spread_g.cross()
    flow.pump(pumps[7])
    outs = [
        pltpu.make_async_copy(a, b, local.at[1 + i])
        for i, (a, b) in enumerate(
            (
                (wq_all, wq_out),
                (wkv_all, wkv_out),
                (wo_all, wo_out),
                (gains_all, gains_out),
                (query_out, query_hbm),
                (keyval_out, keyval_hbm),
                (context_out, context_hbm),
                (normed_out, normed_hbm),
                (middle_out, middle_hbm),
            )
        )
    ]
    for copy in outs:
        copy.start()
    own_x.wait()
    spread_x.hops()
    flow.pump(pumps[8])
    spread_x.core(0)
    spread_g.core(0)
    spread_g.core(1)
    spread_x.cross()
    flow.pump(pumps[9])
    spread_x.core(1)
    for x in range(2):
        spread_g.over(x)
        spread_g.core(2 + x)
    flow.pump(pumps[10])
    for slot in range(4):
        spread_g.core_done(slot)

    for i, (copy, deal, full) in enumerate(
        zip(own_copies[5:], deals[:3], (wg_all, wu_all, wd_all))
    ):
        copy.wait()
        deal.done()
        pltpu.make_async_copy(full.at[:, pl.ds(0, cut)], w_part.at[i], local.at[14 + i]).start()
    for acc in (acc_g, acc_u, acc_d):
        acc[...] = jnp.zeros_like(acc)
    for i, full in enumerate((wg_all, wu_all, wd_all)):
        pltpu.make_async_copy(full.at[:, pl.ds(0, cut)], w_part.at[i], local.at[14 + i]).wait()
    flow.pump(pumps[11])
    tile_blocks = x_tile.shape[0]
    tile = tile_blocks * rows

    @pl.loop(0, 8)
    def _(k):
        slot = k % 2 + 4 * ((k // 2) % 2) + 2 * (k // 4)
        for at in range(1, 8):

            @pl.when(k == at)
            def _():
                flow.pump(pumps[11 + at])

        for at, slot_from in ((2, 0), (3, 1), (6, 2), (7, 3)):

            @pl.when(k == at)
            def _():
                spread_x.core_done(slot_from)

        for at, x in ((4, 0), (5, 1)):

            @pl.when(k == at)
            def _():
                spread_x.over(x)
                spread_x.core(2 + x)

        @pl.loop(0, net.nz // tile_blocks)
        def _(sub):
            part = pl.ds(sub * tile_blocks, tile_blocks)
            loads = [
                pltpu.make_async_copy(a.at[slot, part], b, local.at[14 + i])
                for i, (a, b) in enumerate(((x_all, x_tile), (g_all, g_tile)))
            ]
            for load in loads:
                load.start()
            for load in loads:
                load.wait()
            x = x_tile[...].reshape(tile, features)
            g = g_tile[...].reshape(tile, features)
            hidden, grad_gate, grad_up = feed_forward(x, g, w_part[0], w_part[1], w_part[2])
            start = pl.multiple_of((slot * net.nz + sub * tile_blocks) * rows, tile)
            acts_out[0, pl.ds(start, tile), :] = hidden
            acts_out[1, pl.ds(start, tile), :] = grad_gate
            acts_out[2, pl.ds(start, tile), :] = grad_up
            acc_g[...] += dot_tn(x, grad_gate)
            acc_u[...] += dot_tn(x, grad_up)
            acc_d[...] += dot_tn(g, hidden)

    flow.rest()
    more_outs = [pltpu.make_async_copy(acts_out, acts_hbm, local.at[10])]
    for i, (total, place) in enumerate(((acc_g, dwg_hbm), (acc_u, dwu_hbm), (acc_d, dwd_hbm))):
        dw_out[i] = total[...].astype(BF16)
        more_outs.append(pltpu.make_async_copy(dw_out.at[i], place, local.at[11 + i]))
    for copy in more_outs:
        copy.start()
    for deal in deals[3:]:
        deal.done()
    for copy in outs + more_outs:
        copy.wait()
    net.finish()


def second_kernel(
    n, counts, staged, pumps,
    lens, x_all, g_all, acts_first, wg_all, wu_all, wd_all, dwg, dwu, dwd,
    wq_all, wkv_all, wo_all, normed,
    tok, go, gains_all, query, keyval, context, middle,
    block_out, grad_tokens, grad_gains, grad_wq, grad_wkv, grad_wo, grad_wg, grad_wu, grad_wd,
    dx_c, dx_y, dx_x, dx_z, o_c, o_y, o_x, o_z,
    send, recv, local, stage, dw_part,
    acc, branch_rows, gkv, gkv_c, gkv_y, qpart, qpart_c, qpart_y,
    context_all, query_all, key_all, norm_parts, norm_land, branch_parts, branch_land, k_rows,
    gain_parts, gain_land, gain_sum, grad_query, normed_own,
):
    net = Net(n, send, recv)
    d, t = net.d, net.t
    nz = net.nz
    depth, heads = grad_wq.shape
    features, width = wg_all.shape
    cut = acts_first.shape[2]
    two = cut < width
    rows = tok.shape[0]
    quarter = wkv_all.shape[1]
    blocks = 256 // rows
    tile = blocks * rows
    subs = nz // blocks

    def block(buf, idx):
        return row_block(n, buf, idx)

    mem = Staged(stage, local.at[0]) if staged else Direct()
    scatter_dx = WideScatter(net, dx_c, dx_y, dx_x, dx_z, mem, subs)
    scatter_o = WideScatter(net, o_c, o_y, o_x, o_z, mem, subs)
    branch_g = TensorGather(net, lambda i: branch_rows.at[i])
    kv_s = TensorScatter(net, gkv, gkv_c, gkv_y)
    query_s = TensorScatter(net, qpart, qpart_c, qpart_y)
    kv_g = TensorGather(net, lambda i: k_rows.at[i])
    gain_deal = Deal(net, lambda to: gain_parts.at[to], lambda frm: gain_land.at[frm])
    gain_g = TensorGather(net, lambda i: gain_sum.at[i])
    context_s = Spread(net, [context_all], block)
    query_g = Spread(net, [query_all], block)
    key_g = Spread(net, [key_all], block)
    norm_cols = Columns(net, norm_parts, norm_land)
    branch_cols = Columns(net, branch_parts, branch_land)
    outs = (grad_wg, grad_wu, grad_wd)
    deals = [
        Deal(
            net,
            lambda to, p=part: block(p, to),
            lambda frm, o=out: o.at[:, lanes_at(frm * width, cut)],
        )
        for part, out in zip((dwg, dwu, dwd), outs)
    ]
    if two:
        deals += [
            Deal(
                net,
                lambda to, i=i: block(dw_part.at[i], to),
                lambda frm, o=out: o.at[:, lanes_at(frm * width + cut, cut)],
            )
            for i, out in enumerate(outs)
        ]
    flow = Flow(n, [deals[:3], deals[3:]], KEY_2)
    first_half = 3 * (n - 1)
    copies = [
        pltpu.make_async_copy(deal.src(d), deal.dst(d), local.at[1 + i])
        for i, deal in enumerate(deals)
    ]
    for copy in copies[:3]:
        copy.start()
    own_rows = pltpu.make_async_copy(
        normed.at[pl.ds(pl.multiple_of(t * rows, rows), rows)], normed_own, local.at[6]
    )
    own_rows.start()
    block(context_all, d)[...] = context[...]

    def ffn(wg_v, wu_v, wd_v, acts, x_tiles, g_tiles, x_cols, g_cols, one):
        w_loads = [
            pltpu.make_async_copy(a, b, local.at[7 + i])
            for i, (a, b) in enumerate(
                (
                    (wg_all, wg_v), (wu_all, wu_v), (wd_all, wd_v),
                    (acts_first, acts.at[:, :, pl.ds(0, cut)]),
                )
            )
        ]
        for load in w_loads:
            load.start()

        def place(k):
            step = k // subs
            core, y, x, sub = 1 - (step // 2) % 2, 1 - step // 4, 1 - step % 2, k % subs
            start = pl.multiple_of(((4 * core + 2 * y + x) * nz + sub * blocks) * rows, tile)
            return core, y, x, sub, pl.ds(start, tile)

        def loads(k):
            core, y, x, sub, _ = place(k)
            part = pl.ds(sub * blocks, blocks)
            return [
                pltpu.make_async_copy(
                    a.at[4 * core + 2 * y + x, part], b.at[k % 2], local.at[11 + 2 * i + k % 2]
                )
                for i, (a, b) in enumerate(((x_all, x_tiles), (g_all, g_tiles)))
            ]

        def hand_over(scatter, value, k):
            core, y, x, sub, _ = place(k)

            @pl.when(k > 0)
            def _():
                core_before, y_before, x_before, sub_before, _ = place(k - 1)

                @pl.when(core_before == 1)
                def _():
                    scatter.core_sent(2 * y_before + x_before, sub_before)

            @pl.when(core == 1)
            def _():
                one[...] = value.astype(BF16).reshape(one.shape)
                scatter.to_core(one, 2 * y + x, sub)

            @pl.when(core == 0)
            def _():
                scatter.keep(value, 2 * y + x, sub)

        if two:
            for load in loads(0):
                load.start()
        net.greet()
        context_s.begin()
        own_rows.wait()
        norm_cols.begin(normed_own[...])
        flow.pump(pumps[0], first_half)
        for load in w_loads:
            load.wait()
        more = slice(cut, width)

        @pl.loop(0, 8 * subs)
        def _(k):
            core, y, x, sub, here = place(k)
            if two:

                @pl.when(k + 1 < 8 * subs)
                def _():
                    for load in loads(k + 1):
                        load.start()

                for load in loads(k):
                    load.wait()
                done = feed_forward(
                    x_tiles[k % 2].reshape(tile, features),
                    g_tiles[k % 2].reshape(tile, features),
                    wg_v[:, more], wu_v[:, more], wd_v[:, more],
                )
                for i, act in enumerate(done):
                    acts[i, here, more] = act
            dx = dot_nt(acts[1, here, :], wg_v[...]) + dot_nt(acts[2, here, :], wu_v[...])
            hand_over(scatter_dx, dx, k)
            @pl.when((core == 0) & (y == 1))
            def _():
                @pl.loop(0, blocks)
                def _(i):
                    scatter_dx.to_y(x, sub * blocks + blocks - 1 - i)

        @pl.loop(0, 8 * subs)
        def _(k):
            hand_over(scatter_o, dot_nt(acts[0, place(k)[4], :], wd_v[...]), k)

        scatter_dx.over()
        if two:

            def second_gradients(start, columns):
                for i, block in enumerate(weight_blocks(columns, acts, more)):
                    dw_part[i, pl.ds(start, block.shape[0]), :] = block.astype(BF16)

            by_columns(x_all, g_all, x_cols, g_cols, local.at[pl.ds(11, 4)], second_gradients)

    weights = pltpu.VMEM((features, width), BF16)
    tiles = pltpu.VMEM((2, blocks, rows, features), BF16)
    chunks = pltpu.VMEM((2, 8, nz, rows, 256), BF16)
    pl.run_scoped(
        ffn, weights, weights, weights, pltpu.VMEM((3, 8 * nz * rows, width), BF16),
        tiles, tiles, chunks, chunks, pltpu.VMEM((blocks, rows, features), BF16),
    )
    if two:
        for copy in copies[3:]:
            copy.start()
    flow.pump(pumps[1])
    scatter_o.all_to_y(1)
    scatter_dx.lines()
    flow.pump(pumps[2])
    context_s.hop(1)
    scatter_dx.total(acc)

    def attention(wq_v, wo_v, wkv_v):
        attn_loads = [
            pltpu.make_async_copy(a, b, local.at[7 + i])
            for i, (a, b) in enumerate(((wq_all, wq_v), (wo_all, wo_v), (wkv_all, wkv_v)))
        ]
        for load in attn_loads:
            load.start()
        rows_in = middle[...]
        root = inverse_root(rows_in)
        grad_normed = acc[...]
        gain = lane_row(gains_all, 1, n)
        scaled = grad_normed * gain
        inner = jnp.mean(scaled * rows_in, axis=-1, keepdims=True)
        grad_middle = go[...].astype(F32) + root * (scaled - rows_in * (root * root) * inner)
        branch_rows[t] = grad_middle.astype(BF16)
        branch_g.begin()
        grad_tokens[...] = grad_middle
        gain_ffn = jnp.sum(grad_normed * rows_in * root, axis=0, keepdims=True)
        branch_cols.begin(grad_middle.astype(BF16))
        flow.pump(pumps[3])
        for load in attn_loads:
            load.wait()
        branch_g.rest()
        scatter_o.all_to_y(0)
        context_s.hop(2)
        grad_branch = branch_rows[...].reshape(4 * rows, features)
        grad_context = dot_nn(grad_branch, wo_v[...]).astype(BF16)
        pl.loop(3, nz)(context_s.hop)
        scatter_o.over()
        norm_cols.gather()
        flow.pump(pumps[4])

        allowed = allowed_pairs(lens, 4 * rows)
        key, value = keyval[:, :HD], keyval[:, HD:]
        grad_key = jnp.zeros((4 * rows, HD), F32)
        grad_value = jnp.zeros((4 * rows, HD), F32)
        factor = HD ** (-0.5)
        for h in range(heads // HD):
            lanes = slice(h * HD, (h + 1) * HD)
            probs = softmax_head(query[:, lanes], key, allowed)
            grad_head = grad_context[:, lanes]
            grad_probs = dot_nt(grad_head, value)
            inner = jnp.sum(grad_probs * probs, axis=-1, keepdims=True)
            grad_scores = (probs * (grad_probs - inner)).astype(BF16)
            grad_query[:, lanes] = (dot_nn(grad_scores, key) * factor).astype(BF16)
            grad_key += dot_tn(grad_scores, query[:, lanes]) * factor
            grad_value += dot_tn(probs.astype(BF16), grad_head)
        block(query_all, d)[...] = grad_query[...]
        query_g.begin()
        both = jnp.concatenate([grad_key, grad_value], axis=1).astype(BF16)
        for i in range(4):
            gkv[i] = both[:, i * quarter : (i + 1) * quarter]
        kv_s.begin()
        flow.pump(pumps[5])
        term = dot_nt(grad_query[...], wq_v[...])
        grad_kv = kv_s.rest().astype(BF16)
        block(key_all, d)[...] = grad_kv
        key_g.begin()
        term += dot_nt(grad_kv, wkv_v[...])
        qpart[...] = term.astype(BF16).reshape(qpart.shape)
        query_s.begin()
        branch_cols.gather()
        query_g.hop(1)
        key_g.hop(1)
        flow.pump(pumps[6])
        grad_normed = query_s.rest()

        rows_in = tok[...].astype(F32)
        root = inverse_root(rows_in)
        gain = lane_row(gains_all, 0, n)
        scaled = grad_normed * gain
        inner = jnp.mean(scaled * rows_in, axis=-1, keepdims=True)
        grad_tokens[...] += root * (scaled - rows_in * (root * root) * inner)
        gain_attn = jnp.sum(grad_normed * rows_in * root, axis=0, keepdims=True)
        for i in range(n):
            lanes = slice(i * depth, (i + 1) * depth)
            gain_parts[i, 0:1, :] = gain_attn[:, lanes]
            gain_parts[i, 1:2, :] = gain_ffn[:, lanes]
            gain_parts[i, 2:8, :] = jnp.zeros((6, depth), F32)
        gain_deal.begin()
        query_g.hop(2)
        key_g.hop(2)
        scatter_o.line_step(0)
        flow.pump(pumps[7])
        context_s.cross()
        branch_cols.rest()
        branch_cols.times(context_all, grad_wo)

        @pl.loop(3, nz)
        def _(h):
            query_g.hop(h)
            key_g.hop(h)
            scatter_o.line_step(h - 2)

        flow.pump(pumps[8])
        norm_cols.rest()
        key_g.cross()
        norm_cols.times(key_all, k_rows.at[t])
        kv_g.begin()
        gain_land[d] = gain_parts[d]
        gain_deal.done()
        gain_sum[t] = jnp.sum(gain_land[...], axis=0)
        gain_g.begin()
        flow.rest()
        scatter_o.line_step(nz - 2)
        scatter_o.meet(net.z)
        query_g.cross()
        norm_cols.times(query_all, grad_wq)
        gain_g.rest()
        grad_gains[...] = jnp.sum(gain_sum[...], axis=0)
        kv_g.rest()
        for i in range(4):
            grad_wkv[:, i * quarter : (i + 1) * quarter] = k_rows[i]
        scatter_o.total(acc)
        block_out[...] = (middle[...] + acc[...]).astype(BF16)

    assert net.used <= counts
    projection = pltpu.VMEM((features, heads), BF16)
    part = pltpu.VMEM((features, quarter), BF16)
    pl.run_scoped(attention, projection, projection, part)
    for deal in deals:
        deal.done()
    for copy in copies:
        copy.wait()
    net.finish()


def finish_kernel(
    wg, wu, wd, tokens, wq, wkv, wo, block, gains,
    wg_o, wu_o, wd_o, tokens_o, wq_o, wkv_o, wo_o, block_o, gain_attn_o, gain_ffn_o,
):
    for a, b in ((wg, wg_o), (wu, wu_o), (wd, wd_o)):
        b[...] = a[...].astype(F32)

    @pl.when(pl.program_id(0) == 0)
    def _():
        for a, b in ((tokens, tokens_o), (wq, wq_o), (wkv, wkv_o), (wo, wo_o), (block, block_o)):
            b[...] = a[...]
        gain_attn_o[...] = gains[0:1, :]
        gain_ffn_o[...] = gains[1:2, :]


def params(collective_id):
    return pltpu.CompilerParams(
        collective_id=collective_id, has_side_effects=True, vmem_limit_bytes=63 * MIB
    )


KEY_1 = lambda m: -m
KEY_2 = lambda m: (1 - m % 2, m)
PUMPS_1 = (0.119, 0.0, 0.048, 0.048, 0.048, 0.048, 0.048, 0.095, 0.095, 0.095, 0.095, 0.095, 0.167, 0.0, 0.0, 0.0, 0.0, 0.0, 0.0)
PUMPS_2 = (0.452, 0.0, 0.024, 0.19, 0.143, 0.095, 0.095, 0.0, 0.0, 0.0)


def body(
    n, tokens, grad_out, lengths, gain_attn, gain_ffn, w_query, w_keyval, w_out, w_gate, w_up, w_down
):
    nz = n // 2
    rows, features = tokens.shape
    depth, heads = w_query.shape
    quarter = w_keyval.shape[1] // 4
    width = w_gate.shape[1] // n
    group_rows = 4 * rows
    shape = jax.ShapeDtypeStruct
    cut = width // 2 if width // 2 % 128 == 0 else width
    parts = width // cut
    tile_blocks = 256 // rows
    counts = 9 + 4 * 3 * nz + 2 * (5 * nz + 4) + 3 * parts * n
    full = shape((features, width), BF16)
    part = shape((features, cut), BF16)
    wide = shape((8, nz, rows, features), BF16)
    all_rows = 4 * n * rows
    (
        wg_all, wu_all, wd_all, x_all, g_all, wq_all, wkv_all, wo_all, gains_all,
        query, keyval, context, normed, middle, acts, dwg, dwu, dwd,
    ) = pl.pallas_call(
        functools.partial(first_kernel, n, counts, PUMPS_1),
        out_shape=(
            full, full, full, wide, wide,
            shape((features, heads), BF16),
            shape((features, quarter), BF16),
            shape((features, heads), BF16),
            shape((8 * n, depth), F32),
            shape((group_rows, heads), BF16),
            shape((group_rows, 2 * HD), BF16),
            shape((group_rows, heads), BF16),
            shape((group_rows, features), BF16),
            shape((rows, features), F32),
            shape((3, all_rows, cut), BF16),
            part, part, part,
        ),
        in_specs=[SMEM, ANY, ANY, VMEM, VMEM] + [ANY] * 6,
        out_specs=(ANY,) * 18,
        scratch_shapes=[
            pltpu.VMEM((group_rows, heads), BF16),
            pltpu.VMEM((group_rows, 2 * HD), BF16),
            pltpu.VMEM((group_rows, heads), BF16),
            pltpu.VMEM((group_rows, features), BF16),
            pltpu.VMEM((rows, features), F32),
            pltpu.VMEM((3, all_rows, cut), BF16),
            pltpu.VMEM((3, features, cut), BF16),
            pltpu.SemaphoreType.DMA((counts,)),
            pltpu.SemaphoreType.DMA((counts,)),
            pltpu.SemaphoreType.DMA((17,)),
            pltpu.VMEM((features, heads), BF16),
            pltpu.VMEM((features, quarter), BF16),
            pltpu.VMEM((features, heads), BF16),
            pltpu.VMEM((8 * n, depth), F32),
            pltpu.VMEM((4, rows, features), BF16),
            pltpu.VMEM((4, group_rows, quarter), BF16),
            pltpu.VMEM((4, rows, features), BF16),
            pltpu.VMEM((2, rows, features), BF16),
            pltpu.VMEM((rows, features), BF16),
            pltpu.VMEM((rows, features), BF16),
            pltpu.VMEM((3, features, cut), BF16),
            pltpu.VMEM((tile_blocks, rows, features), BF16),
            pltpu.VMEM((tile_blocks, rows, features), BF16),
        ]
        + [pltpu.VMEM((features, cut), F32)] * 3,
        compiler_params=params(0),
        name="forward",
    )(
        lengths, tokens, grad_out, gain_attn, gain_ffn, w_query, w_keyval, w_out, w_gate, w_up, w_down)

    staged = n > 8
    subs = nz // tile_blocks
    counts = 2 * (4 * subs + 5 * nz) + 3 * 3 * nz + 21 + 3 * n + 3 * parts * n
    landing = [
        shape((4, nz, rows, features), BF16),
        shape((2, nz, rows, features), BF16),
        shape((nz, rows, features), BF16),
        shape((nz + 1, rows, features), BF16),
    ] * 2
    out_shape = [
        shape((rows, features), BF16),
        shape((rows, features), F32),
        shape((8, depth), F32),
        shape((depth, heads), F32),
        shape((depth, 4 * quarter), F32),
        shape((depth, heads), F32),
        shape((depth, n * width), BF16),
        shape((depth, n * width), BF16),
        shape((depth, n * width), BF16),
    ]
    out_specs = [VMEM] * 6 + [ANY] * 3
    in_vmem = []
    if staged:
        out_shape += landing
        out_specs += [ANY] * len(landing)
    else:
        in_vmem = [pltpu.VMEM(place.shape, place.dtype) for place in landing]

    results = pl.pallas_call(
        functools.partial(second_kernel, n, counts, staged, PUMPS_2),
        out_shape=tuple(out_shape),
        in_specs=[SMEM] + [ANY] * 13 + [VMEM] * 7,
        out_specs=tuple(out_specs),
        scratch_shapes=in_vmem
        + [
            pltpu.SemaphoreType.DMA((counts,)),
            pltpu.SemaphoreType.DMA((counts,)),
            pltpu.SemaphoreType.DMA((15,)),
            pltpu.VMEM((tile_blocks if staged else 1, rows, features), BF16),
            pltpu.VMEM((3, features, cut if parts > 1 else 128), BF16),
            pltpu.VMEM((rows, features), F32),
            pltpu.VMEM((4, rows, features), BF16),
            pltpu.VMEM((4, group_rows, quarter), BF16),
            pltpu.VMEM((2, group_rows, quarter), BF16),
            pltpu.VMEM((group_rows, quarter), BF16),
            pltpu.VMEM((4, rows, features), BF16),
            pltpu.VMEM((2, rows, features), BF16),
            pltpu.VMEM((rows, features), BF16),
        ]
        + [
            pltpu.VMEM((n * group_rows, heads), BF16),
            pltpu.VMEM((n * group_rows, heads), BF16),
            pltpu.VMEM((n * group_rows, quarter), BF16),
            pltpu.VMEM((n, rows, depth), BF16),
            pltpu.VMEM((4, n, rows, depth), BF16),
            pltpu.VMEM((n, rows, depth), BF16),
            pltpu.VMEM((4, n, rows, depth), BF16),
            pltpu.VMEM((4, depth, quarter), F32),
            pltpu.VMEM((n, 8, depth), F32),
            pltpu.VMEM((n, 8, depth), F32),
            pltpu.VMEM((4, 8, depth), F32),
            pltpu.VMEM((group_rows, heads), BF16),
            pltpu.VMEM((rows, features), BF16),
        ],
        compiler_params=params(1),
        name="backward",
    )(
        lengths, x_all, g_all, acts, wg_all, wu_all, wd_all, dwg, dwu, dwd,
        wq_all, wkv_all, wo_all, normed,
        tokens, grad_out, gains_all, query, keyval, context, middle,
    )
    block_out, grad_tokens, grad_gains, grad_wq, grad_wkv, grad_wo, grad_wg, grad_wu, grad_wd = (
        results[:9]
    )
    chunks = 2
    column_block = pl.BlockSpec((depth, n * width // chunks), lambda i: (0, i))
    small = [
        pl.BlockSpec(a.shape, lambda i: (0, 0)) for a in (grad_tokens, grad_wq, grad_wkv, grad_wo, block_out)
    ]
    gain_spec = pl.BlockSpec((1, depth), lambda i: (0, 0))
    (
        grad_wg, grad_wu, grad_wd, grad_tokens, grad_wq, grad_wkv, grad_wo, block_out,
        grad_gain_attn, grad_gain_ffn,
    ) = pl.pallas_call(
        finish_kernel,
        grid=(chunks,),
        out_shape=tuple(shape((depth, n * width), F32) for _ in range(3))
        + tuple(
            shape(a.shape, a.dtype) for a in (grad_tokens, grad_wq, grad_wkv, grad_wo, block_out)
        )
        + (shape((1, depth), F32),) * 2,
        in_specs=[column_block] * 3 + small + [pl.BlockSpec((8, depth), lambda i: (0, 0))],
        out_specs=[column_block] * 3 + small + [gain_spec] * 2,
        compiler_params=pltpu.CompilerParams(vmem_limit_bytes=63 * MIB),
        name="results",
    )(grad_wg, grad_wu, grad_wd, grad_tokens, grad_wq, grad_wkv, grad_wo, block_out, grad_gains)
    return (
        block_out,
        grad_tokens,
        grad_gain_attn.reshape(depth),
        grad_gain_ffn.reshape(depth),
        grad_wq,
        grad_wkv,
        grad_wo,
        grad_wg,
        grad_wu,
        grad_wd,
    )


def solution(mesh):
    rows = P(("dp", "tensor"), None)
    both = P("dp", "tensor")
    return jax.shard_map(
        functools.partial(body, mesh.shape["dp"]),
        mesh=mesh,
        in_specs=(rows, rows, P("dp", None), P("dp"), P("dp"), both, P("dp", None), both, both, both, both),
        out_specs=(rows, rows, P("dp"), P("dp"), both, P("dp", None), both, both, both, both),
        check_vma=False,
    )
```

```python
import functools

import jax
import jax.numpy as jnp
from jax import lax
from jax.experimental import pallas as pl
from jax.experimental.pallas import tpu as pltpu
from jax.sharding import PartitionSpec as P

HD = 256
WINDOW = 2048
NORM_EPS = 1e-06
MASKED = -1e30
BF16, F32 = jnp.bfloat16, jnp.float32
MESH = pl.DeviceIdType.MESH
ANY = pl.BlockSpec(memory_space=pl.ANY)
VMEM = pl.BlockSpec(memory_space=pltpu.VMEM)
SMEM = pl.BlockSpec(memory_space=pltpu.SMEM)
MIB = 1 << 20


def dot_nn(a, b):
    return lax.dot_general(a, b, (((1,), (0,)), ((), ())), preferred_element_type=F32)


def dot_nt(a, b):
    return lax.dot_general(a, b, (((1,), (1,)), ((), ())), preferred_element_type=F32)


def dot_tn(a, b):
    return lax.dot_general(a, b, (((0,), (0,)), ((), ())), preferred_element_type=F32)


class Net:
    def __init__(self, n, send, recv):
        self.n, self.nz = n, n // 2
        self.send, self.recv, self.used = send, recv, 0
        self.d = lax.axis_index("dp")
        self.t = lax.axis_index("tensor")
        self.z = self.d // 2
        self.x = self.d % 2
        self.dx = self.d + 1 - 2 * self.x
        self.ty = (self.t + 2) % 4
        self.tc = self.t + 1 - 2 * (self.t % 2)
        self.tcy = (self.tc + 2) % 4
        self.ends = []

    def take(self, count):
        first = self.used
        self.used += count
        return first

    def dp(self, other):
        return (other, self.t)

    def tensor(self, other):
        return (self.d, other)

    def make(self, src, dst, k, device):
        return pltpu.make_async_remote_copy(
            src_ref=src,
            dst_ref=dst,
            send_sem=self.send.at[k],
            recv_sem=self.recv.at[k],
            device_id=device,
            device_id_type=MESH,
        )

    def start(self, src, dst, k, device):
        self.make(src, dst, k, device).start()

    def landed(self, ref, k):
        self.make(ref, ref, k, self.tensor(self.tc)).wait_recv()

    def sent(self, ref, k):
        self.make(ref, ref, k, self.tensor(self.tc)).wait_send()

    def pair(self, m):
        other, bit = 0, 1
        while bit < self.n:
            low, mask = (self.d // bit) % 2, (m // bit) % 2
            other = other + bit * (low + mask - 2 * low * mask)
            bit *= 2
        return other

    def greet(self):
        barrier = pltpu.get_barrier_semaphore()

        @pl.loop(1, self.n)
        def _(m):
            pl.semaphore_signal(
                barrier, inc=1, device_id=self.dp((self.d + m) % self.n), device_id_type=MESH
            )

        for other in (self.ty, self.tc):
            pl.semaphore_signal(
                barrier, inc=1, device_id=self.tensor(other), device_id_type=MESH
            )
        pl.semaphore_wait(barrier, self.n + 1)

    def finish(self):
        for end in self.ends:
            end()


class TensorGather:
    def __init__(self, net, at):
        self.net, self.at, self.k = net, at, net.take(3)
        net.ends.append(self.end)

    def begin(self):
        net = self.net
        net.start(self.at(net.t), self.at(net.t), self.k, net.tensor(net.ty))
        net.start(self.at(net.t), self.at(net.t), self.k + 1, net.tensor(net.tc))

    def rest(self):
        net = self.net
        net.landed(self.at(net.ty), self.k)
        net.start(self.at(net.ty), self.at(net.ty), self.k + 2, net.tensor(net.tc))
        net.landed(self.at(net.tc), self.k + 1)
        net.landed(self.at(net.tcy), self.k + 2)

    def end(self):
        for i in range(3):
            self.net.sent(self.at(0), self.k + i)


class TensorScatter:
    def __init__(self, net, part, cl, yl):
        self.net, self.part, self.cl, self.yl, self.k = net, part, cl, yl, net.take(3)
        net.ends.append(self.end)

    def begin(self):
        net = self.net
        net.start(self.part.at[net.tcy], self.cl.at[1], self.k + 1, net.tensor(net.tc))
        net.start(self.part.at[net.tc], self.cl.at[0], self.k, net.tensor(net.tc))

    def rest(self):
        net = self.net
        net.landed(self.cl.at[1], self.k + 1)
        pair = self.part[net.ty].astype(F32) + self.cl[1].astype(F32)
        self.part[net.ty] = pair.astype(self.part.dtype)
        net.start(self.part.at[net.ty], self.yl, self.k + 2, net.tensor(net.ty))
        net.landed(self.cl.at[0], self.k)
        own = self.part[net.t].astype(F32) + self.cl[0].astype(F32)
        net.landed(self.yl, self.k + 2)
        return own + self.yl[...].astype(F32)

    def end(self):
        for i in range(3):
            self.net.sent(self.yl, self.k + i)


class Spread:
    def __init__(self, net, bufs, block):
        self.net, self.bufs, self.block = net, bufs, block
        self.zk = [net.take(2 * net.nz) for _ in bufs]
        self.xk = [net.take(net.nz) for _ in bufs]
        net.ends.append(self.end)

    def line(self, j, zb, right):
        net = self.net
        here = self.block(self.bufs[j], 2 * zb + net.x)
        if right:
            net.start(here, here, self.zk[j] + zb, net.dp(net.d + 2))
        else:
            net.start(here, here, self.zk[j] + net.nz + zb, net.dp(net.d - 2))

    def over_x(self, j, zb):
        net = self.net
        here = self.block(self.bufs[j], 2 * zb + net.x)
        net.start(here, here, self.xk[j] + zb, net.dp(net.dx))

    def begin(self):
        net = self.net
        for j in range(len(self.bufs)):

            @pl.when(net.z < net.nz - 1)
            def _():
                self.line(j, net.z, True)

            @pl.when(net.z > 0)
            def _():
                self.line(j, net.z, False)

            self.over_x(j, net.z)

    def hop(self, h):
        net = self.net
        nz = net.nz
        for j, buf in enumerate(self.bufs):

            @pl.when(net.z - h >= 0)
            def _():
                zb = net.z - h
                net.landed(self.block(buf, 2 * zb + net.x), self.zk[j] + zb)

                @pl.when(net.z < nz - 1)
                def _():
                    self.line(j, zb, True)

                self.over_x(j, zb)

            @pl.when(net.z + h <= nz - 1)
            def _():
                zb = net.z + h
                net.landed(self.block(buf, 2 * zb + net.x), self.zk[j] + nz + zb)

                @pl.when(net.z > 0)
                def _():
                    self.line(j, zb, False)

                self.over_x(j, zb)

    def cross(self):
        net = self.net

        @pl.loop(0, net.nz)
        def _(k):
            zb = (net.z + k) % net.nz
            for j, buf in enumerate(self.bufs):
                net.landed(self.block(buf, 2 * zb + 1 - net.x), self.xk[j] + zb)

    def end(self):
        net = self.net

        @pl.loop(0, net.nz)
        def _(zb):
            for j, buf in enumerate(self.bufs):
                some = self.block(buf, 0)

                @pl.when((zb <= net.z) & (net.z < net.nz - 1))
                def _():
                    net.sent(some, self.zk[j] + zb)

                @pl.when((zb >= net.z) & (net.z > 0))
                def _():
                    net.sent(some, self.zk[j] + net.nz + zb)

                net.sent(some, self.xk[j] + zb)


class WideSpread:
    def __init__(self, net, buf, late_x=False):
        self.net, self.buf, self.late_x = net, buf, late_x
        self.zk, self.xk = net.take(2 * net.nz), net.take(net.nz)
        self.yk, self.ck = net.take(2 * net.nz), net.take(4)
        net.ends.append(self.end)

    def onward(self, src, zb, right, left):
        net, buf = self.net, self.buf
        if right:

            @pl.when(net.z < net.nz - 1)
            def _():
                net.start(src, buf.at[0, zb], self.zk + zb, net.dp(net.d + 2))

        if left:

            @pl.when(net.z > 0)
            def _():
                net.start(src, buf.at[0, zb], self.zk + net.nz + zb, net.dp(net.d - 2))

        net.start(src, buf.at[2, zb], self.yk + zb, net.tensor(net.ty))
        if not self.late_x:
            net.start(src, buf.at[1, zb], self.xk + zb, net.dp(net.dx))

    def send_x(self):
        net = self.net

        @pl.loop(0, net.nz)
        def _(k):
            zb = (net.z + k) % net.nz
            net.start(self.buf.at[0, zb], self.buf.at[1, zb], self.xk + zb, net.dp(net.dx))

    def begin(self, own):
        self.onward(own, self.net.z, True, True)

    def hop(self, h):
        net, buf = self.net, self.buf

        @pl.when(net.z - h >= 0)
        def _():
            zb = net.z - h
            net.landed(buf.at[0, zb], self.zk + zb)
            self.onward(buf.at[0, zb], zb, True, False)

        @pl.when(net.z + h <= net.nz - 1)
        def _():
            zb = net.z + h
            net.landed(buf.at[0, zb], self.zk + net.nz + zb)
            self.onward(buf.at[0, zb], zb, False, True)

    def hops(self):
        @pl.loop(1, self.net.nz)
        def _(h):
            self.hop(h)

    def cross(self):
        net, buf = self.net, self.buf

        @pl.loop(0, net.nz)
        def _(k):
            zb = (net.z + k) % net.nz
            net.landed(buf.at[1, zb], self.xk + zb)
            net.start(buf.at[1, zb], buf.at[3, zb], self.yk + net.nz + zb, net.tensor(net.ty))

    def over(self, x):
        net = self.net

        @pl.loop(0, net.nz)
        def _(k):
            zb = (net.z + k) % net.nz
            net.landed(self.buf.at[2 + x, zb], self.yk + x * net.nz + zb)

    def core(self, slot):
        net = self.net
        net.start(self.buf.at[slot], self.buf.at[4 + slot], self.ck + slot, net.tensor(net.tc))

    def core_done(self, slot):
        self.net.landed(self.buf.at[4 + slot], self.ck + slot)

    def end(self):
        net = self.net
        some = self.buf.at[0, 0]

        @pl.loop(0, net.nz)
        def _(zb):
            @pl.when((zb <= net.z) & (net.z < net.nz - 1))
            def _():
                net.sent(some, self.zk + zb)

            @pl.when((zb >= net.z) & (net.z > 0))
            def _():
                net.sent(some, self.zk + net.nz + zb)

            net.sent(some, self.xk + zb)
            net.sent(some, self.yk + zb)
            net.sent(some, self.yk + net.nz + zb)

        for slot in range(4):
            net.sent(self.buf.at[0], self.ck + slot)


class Deal:
    def __init__(self, net, src, dst):
        self.net, self.src, self.dst, self.k = net, src, dst, net.take(net.n)
        net.ends.append(self.end)

    def send(self, m):
        net = self.net
        to = net.pair(m)
        net.start(self.src(to), self.dst(net.d), self.k + m, net.dp(to))

    def begin(self):
        pl.loop(1, self.net.n)(self.send)

    def done(self):
        net = self.net

        @pl.loop(1, net.n)
        def _(m):
            net.landed(self.dst(net.pair(m)), self.k + m)

    def end(self):
        net = self.net

        @pl.loop(1, net.n)
        def _(m):
            net.sent(self.src(0), self.k + m)


class Flow:
    def __init__(self, n, groups, key):
        self.todo = []
        for deals in groups:
            pairs = sorted(range(1, n), key=key)
            self.todo += [(deal, m) for deal in deals for m in pairs]
        self.gone, self.share = 0, 0.0

    def pump(self, share, limit=None):
        self.share += share
        upto = min(round(self.share * len(self.todo)), len(self.todo) if limit is None else limit)
        for deal, m in self.todo[self.gone : upto]:
            deal.send(m)
        self.gone = max(upto, self.gone)

    def rest(self):
        self.pump(1.0)


class Columns:
    def __init__(self, net, parts, land):
        self.net, self.parts, self.land = net, parts, land
        self.deal = Deal(net, lambda to: parts.at[to], lambda frm: land.at[net.t, frm])
        self.over = TensorGather(net, lambda i: land.at[i])

    def begin(self, rows):
        depth = self.parts.shape[2]
        for i in range(self.net.n):
            self.parts[i] = rows[:, i * depth : (i + 1) * depth]
        self.land[self.net.t, self.net.d] = self.parts[self.net.d]
        self.deal.begin()

    def gather(self):
        self.deal.done()
        self.over.begin()

    def rest(self):
        self.over.rest()

    def times(self, other, acc):
        n = self.net.n
        depth = self.parts.shape[2]
        acc[...] = jnp.zeros_like(acc)

        @pl.loop(0, n)
        def _(i):
            mine = self.land[:, i].reshape(-1, depth)
            acc[...] += dot_tn(mine, row_block(n, other, i)[...])


class Scatter:
    def __init__(self, net, own, other, xl, zl, mem):
        self.net, self.own, self.other, self.xl, self.zl, self.mem = net, own, other, xl, zl, mem
        self.xk, self.rk, self.lk = net.take(net.nz), net.take(net.nz), net.take(net.nz)
        net.ends.append(self.end)

    def order(self, k):
        odd = k % 2
        return odd * (k // 2) + (1 - odd) * (self.net.nz - 1 - k // 2)

    def send_x(self, zb):
        net = self.net
        net.start(self.other(zb), self.xl.at[zb], self.xk + zb, net.dp(net.dx))

    def begin(self):
        @pl.loop(0, self.net.nz)
        def _(k):
            self.send_x(self.order(k))

    def add(self, block, other):
        mem = self.mem
        mem.put(block, (mem.get(block).astype(F32) + mem.get(other).astype(F32)).astype(BF16))

    def meet(self, zb):
        net = self.net
        net.landed(self.xl.at[zb], self.xk + zb)
        self.add(self.own(zb), self.xl.at[zb])

    def line_step(self, k):
        net = self.net
        nz = net.nz
        far = nz - 1 - k

        @pl.when(far > net.z)
        def _():
            self.meet(far)
            here = self.own(far)

            @pl.when(net.z > 0)
            def _():
                net.landed(self.zl.at[far], self.rk + far)
                self.add(here, self.zl.at[far])

            net.start(here, self.zl.at[far], self.rk + far, net.dp(net.d + 2))

        @pl.when(k < net.z)
        def _():
            self.meet(k)
            here = self.own(k)

            @pl.when(net.z < nz - 1)
            def _():
                net.landed(self.zl.at[k], self.lk + k)
                self.add(here, self.zl.at[k])

            last = (k == net.z - 1).astype(jnp.int32)
            net.start(here, self.zl.at[last * nz + (1 - last) * k], self.lk + k, net.dp(net.d - 2))

    def lines(self):
        pl.loop(0, self.net.nz - 1)(self.line_step)
        self.meet(self.net.z)

    def total(self, acc):
        net, mem = self.net, self.mem
        acc[...] = mem.get(self.own(net.z)).astype(F32)

        @pl.when(net.z > 0)
        def _():
            net.landed(self.zl.at[net.z], self.rk + net.z)
            acc[...] += mem.get(self.zl.at[net.z]).astype(F32)

        @pl.when(net.z < net.nz - 1)
        def _():
            net.landed(self.zl.at[net.nz], self.lk + net.z)
            acc[...] += mem.get(self.zl.at[net.nz]).astype(F32)

    def end(self):
        net = self.net

        @pl.loop(0, net.nz)
        def _(zb):
            net.sent(self.xl.at[0], self.xk + zb)

            @pl.when(zb > net.z)
            def _():
                net.sent(self.zl.at[0], self.rk + zb)

            @pl.when(zb < net.z)
            def _():
                net.sent(self.zl.at[0], self.lk + zb)


class WideScatter(Scatter):
    def __init__(self, net, cl, yl, xl, zl, mem, tiles):
        self.cl, self.yl, self.tiles = cl, yl, tiles
        self.ck, self.yk = net.take(4 * tiles), net.take(2 * net.nz)
        super().__init__(net, lambda zb: cl.at[0, zb], lambda zb: cl.at[1, zb], xl, zl, mem)
        net.ends.append(self.wide_end)

    def place(self, yx, sub):
        blocks = self.net.nz // self.tiles
        return self.cl.at[yx, pl.ds(sub * blocks, blocks)]

    def to_core(self, stage, yx, sub):
        net = self.net
        net.start(stage, self.place(yx, sub), self.ck + yx * self.tiles + sub, net.tensor(net.tc))

    def core_sent(self, yx, sub):
        self.net.sent(self.place(0, 0), self.ck + yx * self.tiles + sub)

    def keep(self, value, yx, sub):
        place = self.place(yx, sub)
        self.net.landed(place, self.ck + yx * self.tiles + sub)
        value = value.reshape(place.shape) + self.mem.get(place).astype(F32)
        self.mem.put(place, value.astype(BF16))

    def to_y(self, x, zb):
        net = self.net
        net.start(
            self.cl.at[2 + x, zb], self.yl.at[x, zb], self.yk + x * net.nz + zb, net.tensor(net.ty)
        )

    def all_to_y(self, x):
        @pl.loop(0, self.net.nz)
        def _(k):
            self.to_y(x, self.order(k))

    def from_y(self, x, zb):
        net = self.net
        net.landed(self.yl.at[x, zb], self.yk + x * net.nz + zb)
        self.add(self.cl.at[x, zb], self.yl.at[x, zb])

    def over(self):
        @pl.loop(0, self.net.nz)
        def _(k):
            zb = self.order(k)
            self.from_y(1, zb)
            self.send_x(zb)

    def meet(self, zb):
        self.from_y(0, zb)
        super().meet(zb)

    def wide_end(self):
        net = self.net

        @pl.loop(0, net.nz)
        def _(zb):
            net.sent(self.yl.at[0, 0], self.yk + zb)
            net.sent(self.yl.at[0, 0], self.yk + net.nz + zb)


class Direct:
    def get(self, ref):
        return ref[...]

    def put(self, ref, value):
        ref[...] = value


class Staged:
    def __init__(self, buf, sem):
        self.buf, self.sem = buf, sem

    def view(self, ref):
        return self.buf if len(ref.shape) == 3 else self.buf.at[0]

    def get(self, ref):
        view = self.view(ref)
        copy = pltpu.make_async_copy(ref, view, self.sem)
        copy.start()
        copy.wait()
        return view[...]

    def put(self, ref, value):
        view = self.view(ref)
        view[...] = value
        copy = pltpu.make_async_copy(view, ref, self.sem)
        copy.start()
        copy.wait()


def lane_row(gains, row, n):
    return jnp.concatenate([gains[8 * i + row : 8 * i + row + 1, :] for i in range(n)], axis=1)


def allowed_pairs(lens, rows):
    place_i = lax.broadcasted_iota(jnp.int32, (rows, 1), 0)
    place_j = lax.broadcasted_iota(jnp.int32, (1, rows), 1)
    segment_i = jnp.zeros((rows, 1), jnp.int32)
    segment_j = jnp.zeros((1, rows), jnp.int32)
    total = 0
    for k in range(lens.shape[1]):
        total = total + lens[0, k]
        segment_i += (place_i >= total).astype(jnp.int32)
        segment_j += (place_j >= total).astype(jnp.int32)
    distance = place_i - place_j
    return (segment_i == segment_j) & (distance >= 0) & (distance < WINDOW)


def softmax_head(query, key, allowed):
    scores = dot_nt(query, key) * HD ** (-0.5)
    scores = jnp.where(allowed, scores, MASKED)
    weights = jnp.exp(scores - jnp.max(scores, axis=-1, keepdims=True))
    return weights / jnp.sum(weights, axis=-1, keepdims=True)


def inverse_root(rows):
    return lax.rsqrt(jnp.mean(rows * rows, axis=-1, keepdims=True) + NORM_EPS)


def feed_forward(x, g, wg, wu, wd):
    gate = dot_nn(x, wg)
    up = dot_nn(x, wu)
    grad_hidden = dot_nn(g, wd)
    root = (2.0 / jnp.pi) ** 0.5
    square = gate * gate
    tanh = jnp.tanh(root * gate * (1.0 + 0.044715 * square))
    half = 0.5 * (1.0 + tanh)
    gelu = gate * half
    slope = half + 0.5 * gate * (1.0 - tanh * tanh) * (root * (1.0 + 3 * 0.044715 * square))
    hidden = (gelu * up).astype(BF16)
    grad_gate = (grad_hidden * up * slope).astype(BF16)
    grad_up = (grad_hidden * gelu).astype(BF16)
    return hidden, grad_gate, grad_up


def row_block(n, buf, idx):
    step = buf.shape[0] // n
    return buf.at[pl.ds(pl.multiple_of(idx * step, step), step)]


def lanes_at(start, size):
    return pl.ds(pl.multiple_of(start, 128), size)


def weight_blocks(columns, acts, cols):
    x_cols, g_cols = columns
    return (
        dot_tn(x_cols, acts[1, :, cols]),
        dot_tn(x_cols, acts[2, :, cols]),
        dot_tn(g_cols, acts[0, :, cols]),
    )


def by_columns(x_all, g_all, x_cols, g_cols, sems, use):
    features = x_all.shape[3]
    chunk = x_cols.shape[4]
    count = features // chunk

    def loads(c):
        lanes = lanes_at(c * chunk, chunk)
        return [
            pltpu.make_async_copy(a.at[:, :, :, lanes], b.at[c % 2], sems.at[2 * i + c % 2])
            for i, (a, b) in enumerate(((x_all, x_cols), (g_all, g_cols)))
        ]

    for load in loads(0):
        load.start()

    @pl.loop(0, count)
    def _(c):
        @pl.when(c + 1 < count)
        def _():
            for load in loads(c + 1):
                load.start()

        for load in loads(c):
            load.wait()
        use(pl.multiple_of(c * chunk, chunk), [b[c % 2].reshape(-1, chunk) for b in (x_cols, g_cols)])


def first_kernel(
    n, counts, pumps,
    lens, tok, go, gain_attn, gain_ffn, wq, wkv, wo, wg, wu, wd,
    wg_all, wu_all, wd_all, x_all, g_all, wq_out, wkv_out, wo_out, gains_out,
    query_hbm, keyval_hbm, context_hbm, normed_hbm, middle_hbm, acts_hbm, dwg_hbm, dwu_hbm, dwd_hbm,
    query_out, keyval_out, context_out, normed_out, middle_out, acts_out, dw_out,
    send, recv, local, wq_all, wkv_all, wo_all, gains_all,
    group, kv_parts, branch, branch_c, branch_y, own_normed,
    w_part, x_tile, g_tile, acc_g, acc_u, acc_d,
):
    net = Net(n, send, recv)
    d, t = net.d, net.t
    quarter = wkv_all.shape[1]
    width = wg_all.shape[1]
    cut = acts_out.shape[2]
    rows, features = tok.shape

    def block(buf, idx):
        return row_block(n, buf, idx)

    wkv_own = wkv.at[:, lanes_at(t * quarter, quarter)]
    tokens_g = TensorGather(net, lambda i: group.at[i])
    kv_g = TensorGather(net, lambda i: kv_parts.at[i])
    branch_s = TensorScatter(net, branch, branch_c, branch_y)
    first_w = Spread(net, [wq_all, wkv_all, gains_all], block)
    second_w = Spread(net, [wo_all], block)
    spread_g = WideSpread(net, g_all, late_x=True)
    spread_x = WideSpread(net, x_all)
    deals = [
        Deal(
            net,
            lambda to, w=w, at=at: w.at[:, lanes_at(to * width + at, cut)],
            lambda frm, full=full, at=at: block(full, frm).at[:, pl.ds(at, cut)],
        )
        for at in range(0, width, cut)
        for w, full in ((wg, wg_all), (wu, wu_all), (wd, wd_all))
    ]
    assert net.used <= counts
    flow = Flow(n, [deals[:3], deals[3:]], KEY_1)

    own_gains = block(gains_all, d)
    own_gains[...] = jnp.zeros(own_gains.shape, F32)
    own_gains[0:1, :] = gain_attn[...].astype(F32).reshape(1, -1)
    own_gains[1:2, :] = gain_ffn[...].astype(F32).reshape(1, -1)
    own_copies = [
        (tok, group.at[t]),
        (wq, block(wq_all, d)),
        (wkv_own, block(wkv_all, d)),
        (wo, block(wo_all, d)),
        (go, g_all.at[0, net.z]),
    ] + [
        (w.at[:, lanes_at(d * width, width)], block(full, d))
        for w, full in ((wg, wg_all), (wu, wu_all), (wd, wd_all))
    ]
    own_copies = [
        pltpu.make_async_copy(a, b, local.at[i if i < 5 else 9 + i])
        for i, (a, b) in enumerate(own_copies)
    ]
    for copy in own_copies:
        copy.start()
    net.greet()

    for copy in own_copies[:3]:
        copy.wait()
    tokens_g.begin()
    first_w.begin()
    flow.pump(pumps[0])
    own_copies[3].wait()
    own_copies[4].wait()
    tokens_g.rest()
    second_w.begin()
    spread_g.begin(go)
    flow.pump(pumps[1])

    @pl.loop(1, net.nz)
    def _(h):
        first_w.hop(h)

        @pl.when(h > 1)
        def _():
            second_w.hop(h - 1)

        spread_g.hop(h)

    flow.pump(pumps[2])
    inputs = group[...].reshape(4 * rows, features).astype(F32)
    root = inverse_root(inputs)
    first_w.cross()
    second_w.hop(net.nz - 1)
    spread_g.send_x()
    flow.pump(pumps[3])
    gain = lane_row(gains_all, 0, n)
    normed = (inputs * root * gain).astype(BF16)
    normed_out[...] = normed
    kv_parts[t] = dot_nn(normed, wkv_all[...]).astype(BF16)
    kv_g.begin()
    query_out[...] = dot_nn(normed, wq_all[...]).astype(BF16)
    flow.pump(pumps[4])
    kv_g.rest()
    for i in range(4):
        keyval_out[:, i * quarter : (i + 1) * quarter] = kv_parts[i]
    allowed = allowed_pairs(lens, 4 * rows)
    for h in range(query_out.shape[1] // HD):
        lanes = slice(h * HD, (h + 1) * HD)
        probs = softmax_head(query_out[:, lanes], keyval_out[:, :HD], allowed).astype(BF16)
        context_out[:, lanes] = dot_nn(probs, keyval_out[:, HD:]).astype(BF16)
    flow.pump(pumps[5])
    second_w.cross()
    branch[...] = dot_nt(context_out[...], wo_all[...]).astype(BF16).reshape(branch.shape)
    branch_s.begin()
    flow.pump(pumps[6])
    middle = group[t].astype(F32) + branch_s.rest()
    middle_out[...] = middle
    own_normed[...] = (middle * inverse_root(middle) * lane_row(gains_all, 1, n)).astype(BF16)
    own_x = pltpu.make_async_copy(own_normed, x_all.at[0, net.z], local.at[0])
    own_x.start()
    spread_x.begin(own_normed)
    spread_g.cross()
    flow.pump(pumps[7])
    outs = [
        pltpu.make_async_copy(a, b, local.at[1 + i])
        for i, (a, b) in enumerate(
            (
                (wq_all, wq_out),
                (wkv_all, wkv_out),
                (wo_all, wo_out),
                (gains_all, gains_out),
                (query_out, query_hbm),
                (keyval_out, keyval_hbm),
                (context_out, context_hbm),
                (normed_out, normed_hbm),
                (middle_out, middle_hbm),
            )
        )
    ]
    for copy in outs:
        copy.start()
    own_x.wait()
    spread_x.hops()
    flow.pump(pumps[8])
    spread_x.core(0)
    spread_g.core(0)
    spread_g.core(1)
    spread_x.cross()
    flow.pump(pumps[9])
    spread_x.core(1)
    for x in range(2):
        spread_g.over(x)
        spread_g.core(2 + x)
    flow.pump(pumps[10])
    for slot in range(4):
        spread_g.core_done(slot)

    for i, (copy, deal, full) in enumerate(
        zip(own_copies[5:], deals[:3], (wg_all, wu_all, wd_all))
    ):
        copy.wait()
        deal.done()
        pltpu.make_async_copy(full.at[:, pl.ds(0, cut)], w_part.at[i], local.at[14 + i]).start()
    for acc in (acc_g, acc_u, acc_d):
        acc[...] = jnp.zeros_like(acc)
    for i, full in enumerate((wg_all, wu_all, wd_all)):
        pltpu.make_async_copy(full.at[:, pl.ds(0, cut)], w_part.at[i], local.at[14 + i]).wait()
    flow.pump(pumps[11])
    tile_blocks = x_tile.shape[0]
    tile = tile_blocks * rows

    @pl.loop(0, 8)
    def _(k):
        slot = k % 2 + 4 * ((k // 2) % 2) + 2 * (k // 4)
        for at in range(1, 8):

            @pl.when(k == at)
            def _():
                flow.pump(pumps[11 + at])

        for at, slot_from in ((2, 0), (3, 1), (6, 2), (7, 3)):

            @pl.when(k == at)
            def _():
                spread_x.core_done(slot_from)

        for at, x in ((4, 0), (5, 1)):

            @pl.when(k == at)
            def _():
                spread_x.over(x)
                spread_x.core(2 + x)

        @pl.loop(0, net.nz // tile_blocks)
        def _(sub):
            part = pl.ds(sub * tile_blocks, tile_blocks)
            loads = [
                pltpu.make_async_copy(a.at[slot, part], b, local.at[14 + i])
                for i, (a, b) in enumerate(((x_all, x_tile), (g_all, g_tile)))
            ]
            for load in loads:
                load.start()
            for load in loads:
                load.wait()
            x = x_tile[...].reshape(tile, features)
            g = g_tile[...].reshape(tile, features)
            hidden, grad_gate, grad_up = feed_forward(x, g, w_part[0], w_part[1], w_part[2])
            start = pl.multiple_of((slot * net.nz + sub * tile_blocks) * rows, tile)
            acts_out[0, pl.ds(start, tile), :] = hidden
            acts_out[1, pl.ds(start, tile), :] = grad_gate
            acts_out[2, pl.ds(start, tile), :] = grad_up
            acc_g[...] += dot_tn(x, grad_gate)
            acc_u[...] += dot_tn(x, grad_up)
            acc_d[...] += dot_tn(g, hidden)

    flow.rest()
    more_outs = [pltpu.make_async_copy(acts_out, acts_hbm, local.at[10])]
    for i, (total, place) in enumerate(((acc_g, dwg_hbm), (acc_u, dwu_hbm), (acc_d, dwd_hbm))):
        dw_out[i] = total[...].astype(BF16)
        more_outs.append(pltpu.make_async_copy(dw_out.at[i], place, local.at[11 + i]))
    for copy in more_outs:
        copy.start()
    for deal in deals[3:]:
        deal.done()
    for copy in outs + more_outs:
        copy.wait()
    net.finish()


def second_kernel(
    n, counts, staged, pumps,
    lens, x_all, g_all, acts_first, wg_all, wu_all, wd_all, dwg, dwu, dwd,
    wq_all, wkv_all, wo_all, normed,
    tok, go, gains_all, query, keyval, context, middle,
    block_out, grad_tokens, grad_gains, grad_wq, grad_wkv, grad_wo, grad_wg, grad_wu, grad_wd,
    dx_c, dx_y, dx_x, dx_z, o_c, o_y, o_x, o_z,
    send, recv, local, stage, dw_part,
    acc, branch_rows, gkv, gkv_c, gkv_y, qpart, qpart_c, qpart_y,
    context_all, query_all, key_all, norm_parts, norm_land, branch_parts, branch_land, k_rows,
    gain_parts, gain_land, gain_sum, grad_query, normed_own,
):
    net = Net(n, send, recv)
    d, t = net.d, net.t
    nz = net.nz
    depth, heads = grad_wq.shape
    features, width = wg_all.shape
    cut = acts_first.shape[2]
    two = cut < width
    rows = tok.shape[0]
    quarter = wkv_all.shape[1]
    blocks = 256 // rows
    tile = blocks * rows
    subs = nz // blocks

    def block(buf, idx):
        return row_block(n, buf, idx)

    mem = Staged(stage, local.at[0]) if staged else Direct()
    scatter_dx = WideScatter(net, dx_c, dx_y, dx_x, dx_z, mem, subs)
    scatter_o = WideScatter(net, o_c, o_y, o_x, o_z, mem, subs)
    branch_g = TensorGather(net, lambda i: branch_rows.at[i])
    kv_s = TensorScatter(net, gkv, gkv_c, gkv_y)
    query_s = TensorScatter(net, qpart, qpart_c, qpart_y)
    kv_g = TensorGather(net, lambda i: k_rows.at[i])
    gain_deal = Deal(net, lambda to: gain_parts.at[to], lambda frm: gain_land.at[frm])
    gain_g = TensorGather(net, lambda i: gain_sum.at[i])
    context_s = Spread(net, [context_all], block)
    query_g = Spread(net, [query_all], block)
    key_g = Spread(net, [key_all], block)
    norm_cols = Columns(net, norm_parts, norm_land)
    branch_cols = Columns(net, branch_parts, branch_land)
    outs = (grad_wg, grad_wu, grad_wd)
    deals = [
        Deal(
            net,
            lambda to, p=part: block(p, to),
            lambda frm, o=out: o.at[:, lanes_at(frm * width, cut)],
        )
        for part, out in zip((dwg, dwu, dwd), outs)
    ]
    if two:
        deals += [
            Deal(
                net,
                lambda to, i=i: block(dw_part.at[i], to),
                lambda frm, o=out: o.at[:, lanes_at(frm * width + cut, cut)],
            )
            for i, out in enumerate(outs)
        ]
    flow = Flow(n, [deals[:3], deals[3:]], KEY_2)
    first_half = 3 * (n - 1)
    copies = [
        pltpu.make_async_copy(deal.src(d), deal.dst(d), local.at[1 + i])
        for i, deal in enumerate(deals)
    ]
    for copy in copies[:3]:
        copy.start()
    own_rows = pltpu.make_async_copy(
        normed.at[pl.ds(pl.multiple_of(t * rows, rows), rows)], normed_own, local.at[6]
    )
    own_rows.start()
    block(context_all, d)[...] = context[...]

    def ffn(wg_v, wu_v, wd_v, acts, x_tiles, g_tiles, x_cols, g_cols, one):
        w_loads = [
            pltpu.make_async_copy(a, b, local.at[7 + i])
            for i, (a, b) in enumerate(
                (
                    (wg_all, wg_v), (wu_all, wu_v), (wd_all, wd_v),
                    (acts_first, acts.at[:, :, pl.ds(0, cut)]),
                )
            )
        ]
        for load in w_loads:
            load.start()

        def place(k):
            step = k // subs
            core, y, x, sub = 1 - (step // 2) % 2, 1 - step // 4, 1 - step % 2, k % subs
            start = pl.multiple_of(((4 * core + 2 * y + x) * nz + sub * blocks) * rows, tile)
            return core, y, x, sub, pl.ds(start, tile)

        def loads(k):
            core, y, x, sub, _ = place(k)
            part = pl.ds(sub * blocks, blocks)
            return [
                pltpu.make_async_copy(
                    a.at[4 * core + 2 * y + x, part], b.at[k % 2], local.at[11 + 2 * i + k % 2]
                )
                for i, (a, b) in enumerate(((x_all, x_tiles), (g_all, g_tiles)))
            ]

        def hand_over(scatter, value, k):
            core, y, x, sub, _ = place(k)

            @pl.when(k > 0)
            def _():
                core_before, y_before, x_before, sub_before, _ = place(k - 1)

                @pl.when(core_before == 1)
                def _():
                    scatter.core_sent(2 * y_before + x_before, sub_before)

            @pl.when(core == 1)
            def _():
                one[...] = value.astype(BF16).reshape(one.shape)
                scatter.to_core(one, 2 * y + x, sub)

            @pl.when(core == 0)
            def _():
                scatter.keep(value, 2 * y + x, sub)

        if two:
            for load in loads(0):
                load.start()
        net.greet()
        context_s.begin()
        own_rows.wait()
        norm_cols.begin(normed_own[...])
        flow.pump(pumps[0], first_half)
        for load in w_loads:
            load.wait()
        more = slice(cut, width)

        @pl.loop(0, 8 * subs)
        def _(k):
            core, y, x, sub, here = place(k)
            if two:

                @pl.when(k + 1 < 8 * subs)
                def _():
                    for load in loads(k + 1):
                        load.start()

                for load in loads(k):
                    load.wait()
                done = feed_forward(
                    x_tiles[k % 2].reshape(tile, features),
                    g_tiles[k % 2].reshape(tile, features),
                    wg_v[:, more], wu_v[:, more], wd_v[:, more],
                )
                for i, act in enumerate(done):
                    acts[i, here, more] = act
            dx = dot_nt(acts[1, here, :], wg_v[...]) + dot_nt(acts[2, here, :], wu_v[...])
            hand_over(scatter_dx, dx, k)
            @pl.when((core == 0) & (y == 1))
            def _():
                @pl.loop(0, blocks)
                def _(i):
                    scatter_dx.to_y(x, sub * blocks + blocks - 1 - i)

        @pl.loop(0, 8 * subs)
        def _(k):
            hand_over(scatter_o, dot_nt(acts[0, place(k)[4], :], wd_v[...]), k)

        scatter_dx.over()
        if two:

            def second_gradients(start, columns):
                for i, block in enumerate(weight_blocks(columns, acts, more)):
                    dw_part[i, pl.ds(start, block.shape[0]), :] = block.astype(BF16)

            by_columns(x_all, g_all, x_cols, g_cols, local.at[pl.ds(11, 4)], second_gradients)

    weights = pltpu.VMEM((features, width), BF16)
    tiles = pltpu.VMEM((2, blocks, rows, features), BF16)
    chunks = pltpu.VMEM((2, 8, nz, rows, 256), BF16)
    pl.run_scoped(
        ffn, weights, weights, weights, pltpu.VMEM((3, 8 * nz * rows, width), BF16),
        tiles, tiles, chunks, chunks, pltpu.VMEM((blocks, rows, features), BF16),
    )
    if two:
        for copy in copies[3:]:
            copy.start()
    flow.pump(pumps[1])
    scatter_o.all_to_y(1)
    scatter_dx.lines()
    flow.pump(pumps[2])
    context_s.hop(1)
    scatter_dx.total(acc)

    def attention(wq_v, wo_v, wkv_v):
        attn_loads = [
            pltpu.make_async_copy(a, b, local.at[7 + i])
            for i, (a, b) in enumerate(((wq_all, wq_v), (wo_all, wo_v), (wkv_all, wkv_v)))
        ]
        for load in attn_loads:
            load.start()
        rows_in = middle[...]
        root = inverse_root(rows_in)
        grad_normed = acc[...]
        gain = lane_row(gains_all, 1, n)
        scaled = grad_normed * gain
        inner = jnp.mean(scaled * rows_in, axis=-1, keepdims=True)
        grad_middle = go[...].astype(F32) + root * (scaled - rows_in * (root * root) * inner)
        branch_rows[t] = grad_middle.astype(BF16)
        branch_g.begin()
        grad_tokens[...] = grad_middle
        gain_ffn = jnp.sum(grad_normed * rows_in * root, axis=0, keepdims=True)
        branch_cols.begin(grad_middle.astype(BF16))
        flow.pump(pumps[3])
        for load in attn_loads:
            load.wait()
        branch_g.rest()
        scatter_o.all_to_y(0)
        context_s.hop(2)
        grad_branch = branch_rows[...].reshape(4 * rows, features)
        grad_context = dot_nn(grad_branch, wo_v[...]).astype(BF16)
        pl.loop(3, nz)(context_s.hop)
        scatter_o.over()
        norm_cols.gather()
        flow.pump(pumps[4])

        allowed = allowed_pairs(lens, 4 * rows)
        key, value = keyval[:, :HD], keyval[:, HD:]
        grad_key = jnp.zeros((4 * rows, HD), F32)
        grad_value = jnp.zeros((4 * rows, HD), F32)
        factor = HD ** (-0.5)
        for h in range(heads // HD):
            lanes = slice(h * HD, (h + 1) * HD)
            probs = softmax_head(query[:, lanes], key, allowed)
            grad_head = grad_context[:, lanes]
            grad_probs = dot_nt(grad_head, value)
            inner = jnp.sum(grad_probs * probs, axis=-1, keepdims=True)
            grad_scores = (probs * (grad_probs - inner)).astype(BF16)
            grad_query[:, lanes] = (dot_nn(grad_scores, key) * factor).astype(BF16)
            grad_key += dot_tn(grad_scores, query[:, lanes]) * factor
            grad_value += dot_tn(probs.astype(BF16), grad_head)
        block(query_all, d)[...] = grad_query[...]
        query_g.begin()
        both = jnp.concatenate([grad_key, grad_value], axis=1).astype(BF16)
        for i in range(4):
            gkv[i] = both[:, i * quarter : (i + 1) * quarter]
        kv_s.begin()
        flow.pump(pumps[5])
        term = dot_nt(grad_query[...], wq_v[...])
        grad_kv = kv_s.rest().astype(BF16)
        block(key_all, d)[...] = grad_kv
        key_g.begin()
        term += dot_nt(grad_kv, wkv_v[...])
        qpart[...] = term.astype(BF16).reshape(qpart.shape)
        query_s.begin()
        branch_cols.gather()
        query_g.hop(1)
        key_g.hop(1)
        flow.pump(pumps[6])
        grad_normed = query_s.rest()

        rows_in = tok[...].astype(F32)
        root = inverse_root(rows_in)
        gain = lane_row(gains_all, 0, n)
        scaled = grad_normed * gain
        inner = jnp.mean(scaled * rows_in, axis=-1, keepdims=True)
        grad_tokens[...] += root * (scaled - rows_in * (root * root) * inner)
        gain_attn = jnp.sum(grad_normed * rows_in * root, axis=0, keepdims=True)
        for i in range(n):
            lanes = slice(i * depth, (i + 1) * depth)
            gain_parts[i, 0:1, :] = gain_attn[:, lanes]
            gain_parts[i, 1:2, :] = gain_ffn[:, lanes]
            gain_parts[i, 2:8, :] = jnp.zeros((6, depth), F32)
        gain_deal.begin()
        query_g.hop(2)
        key_g.hop(2)
        scatter_o.line_step(0)
        flow.pump(pumps[7])
        context_s.cross()
        branch_cols.rest()
        branch_cols.times(context_all, grad_wo)

        @pl.loop(3, nz)
        def _(h):
            query_g.hop(h)
            key_g.hop(h)
            scatter_o.line_step(h - 2)

        flow.pump(pumps[8])
        norm_cols.rest()
        key_g.cross()
        norm_cols.times(key_all, k_rows.at[t])
        kv_g.begin()
        gain_land[d] = gain_parts[d]
        gain_deal.done()
        gain_sum[t] = jnp.sum(gain_land[...], axis=0)
        gain_g.begin()
        flow.rest()
        scatter_o.line_step(nz - 2)
        scatter_o.meet(net.z)
        query_g.cross()
        norm_cols.times(query_all, grad_wq)
        gain_g.rest()
        grad_gains[...] = jnp.sum(gain_sum[...], axis=0)
        kv_g.rest()
        for i in range(4):
            grad_wkv[:, i * quarter : (i + 1) * quarter] = k_rows[i]
        scatter_o.total(acc)
        block_out[...] = (middle[...] + acc[...]).astype(BF16)

    assert net.used <= counts
    projection = pltpu.VMEM((features, heads), BF16)
    part = pltpu.VMEM((features, quarter), BF16)
    pl.run_scoped(attention, projection, projection, part)
    for deal in deals:
        deal.done()
    for copy in copies:
        copy.wait()
    net.finish()


def finish_kernel(
    wg, wu, wd, tokens, wq, wkv, wo, block, gains,
    wg_o, wu_o, wd_o, tokens_o, wq_o, wkv_o, wo_o, block_o, gain_attn_o, gain_ffn_o,
):
    for a, b in ((wg, wg_o), (wu, wu_o), (wd, wd_o)):
        b[...] = a[...].astype(F32)

    @pl.when(pl.program_id(0) == 0)
    def _():
        for a, b in ((tokens, tokens_o), (wq, wq_o), (wkv, wkv_o), (wo, wo_o), (block, block_o)):
            b[...] = a[...]
        gain_attn_o[...] = gains[0:1, :]
        gain_ffn_o[...] = gains[1:2, :]


def params(collective_id):
    return pltpu.CompilerParams(
        collective_id=collective_id, has_side_effects=True, vmem_limit_bytes=63 * MIB
    )


KEY_1 = lambda m: -m
KEY_2 = lambda m: (1 - m % 2, m)
PUMPS_1 = (0.119, 0.0, 0.048, 0.048, 0.048, 0.048, 0.048, 0.095, 0.095, 0.095, 0.095, 0.095, 0.167, 0.0, 0.0, 0.0, 0.0, 0.0, 0.0)
PUMPS_2 = (0.476, 0.0, 0.024, 0.238, 0.119, 0.071, 0.071, 0.0, 0.0, 0.0)


def body(
    n, tokens, grad_out, lengths, gain_attn, gain_ffn, w_query, w_keyval, w_out, w_gate, w_up, w_down
):
    nz = n // 2
    rows, features = tokens.shape
    depth, heads = w_query.shape
    quarter = w_keyval.shape[1] // 4
    width = w_gate.shape[1] // n
    group_rows = 4 * rows
    shape = jax.ShapeDtypeStruct
    cut = width // 2 if width // 2 % 128 == 0 else width
    parts = width // cut
    tile_blocks = 256 // rows
    counts = 9 + 4 * 3 * nz + 2 * (5 * nz + 4) + 3 * parts * n
    full = shape((features, width), BF16)
    part = shape((features, cut), BF16)
    wide = shape((8, nz, rows, features), BF16)
    all_rows = 4 * n * rows
    (
        wg_all, wu_all, wd_all, x_all, g_all, wq_all, wkv_all, wo_all, gains_all,
        query, keyval, context, normed, middle, acts, dwg, dwu, dwd,
    ) = pl.pallas_call(
        functools.partial(first_kernel, n, counts, PUMPS_1),
        out_shape=(
            full, full, full, wide, wide,
            shape((features, heads), BF16),
            shape((features, quarter), BF16),
            shape((features, heads), BF16),
            shape((8 * n, depth), F32),
            shape((group_rows, heads), BF16),
            shape((group_rows, 2 * HD), BF16),
            shape((group_rows, heads), BF16),
            shape((group_rows, features), BF16),
            shape((rows, features), F32),
            shape((3, all_rows, cut), BF16),
            part, part, part,
        ),
        in_specs=[SMEM, ANY, ANY, VMEM, VMEM] + [ANY] * 6,
        out_specs=(ANY,) * 18,
        scratch_shapes=[
            pltpu.VMEM((group_rows, heads), BF16),
            pltpu.VMEM((group_rows, 2 * HD), BF16),
            pltpu.VMEM((group_rows, heads), BF16),
            pltpu.VMEM((group_rows, features), BF16),
            pltpu.VMEM((rows, features), F32),
            pltpu.VMEM((3, all_rows, cut), BF16),
            pltpu.VMEM((3, features, cut), BF16),
            pltpu.SemaphoreType.DMA((counts,)),
            pltpu.SemaphoreType.DMA((counts,)),
            pltpu.SemaphoreType.DMA((17,)),
            pltpu.VMEM((features, heads), BF16),
            pltpu.VMEM((features, quarter), BF16),
            pltpu.VMEM((features, heads), BF16),
            pltpu.VMEM((8 * n, depth), F32),
            pltpu.VMEM((4, rows, features), BF16),
            pltpu.VMEM((4, group_rows, quarter), BF16),
            pltpu.VMEM((4, rows, features), BF16),
            pltpu.VMEM((2, rows, features), BF16),
            pltpu.VMEM((rows, features), BF16),
            pltpu.VMEM((rows, features), BF16),
            pltpu.VMEM((3, features, cut), BF16),
            pltpu.VMEM((tile_blocks, rows, features), BF16),
            pltpu.VMEM((tile_blocks, rows, features), BF16),
        ]
        + [pltpu.VMEM((features, cut), F32)] * 3,
        compiler_params=params(0),
        name="forward",
    )(
        lengths, tokens, grad_out, gain_attn, gain_ffn, w_query, w_keyval, w_out, w_gate, w_up, w_down)

    staged = n > 8
    subs = nz // tile_blocks
    counts = 2 * (4 * subs + 5 * nz) + 3 * 3 * nz + 21 + 3 * n + 3 * parts * n
    landing = [
        shape((4, nz, rows, features), BF16),
        shape((2, nz, rows, features), BF16),
        shape((nz, rows, features), BF16),
        shape((nz + 1, rows, features), BF16),
    ] * 2
    out_shape = [
        shape((rows, features), BF16),
        shape((rows, features), F32),
        shape((8, depth), F32),
        shape((depth, heads), F32),
        shape((depth, 4 * quarter), F32),
        shape((depth, heads), F32),
        shape((depth, n * width), BF16),
        shape((depth, n * width), BF16),
        shape((depth, n * width), BF16),
    ]
    out_specs = [VMEM] * 6 + [ANY] * 3
    in_vmem = []
    if staged:
        out_shape += landing
        out_specs += [ANY] * len(landing)
    else:
        in_vmem = [pltpu.VMEM(place.shape, place.dtype) for place in landing]

    results = pl.pallas_call(
        functools.partial(second_kernel, n, counts, staged, PUMPS_2),
        out_shape=tuple(out_shape),
        in_specs=[SMEM] + [ANY] * 13 + [VMEM] * 7,
        out_specs=tuple(out_specs),
        scratch_shapes=in_vmem
        + [
            pltpu.SemaphoreType.DMA((counts,)),
            pltpu.SemaphoreType.DMA((counts,)),
            pltpu.SemaphoreType.DMA((15,)),
            pltpu.VMEM((tile_blocks if staged else 1, rows, features), BF16),
            pltpu.VMEM((3, features, cut if parts > 1 else 128), BF16),
            pltpu.VMEM((rows, features), F32),
            pltpu.VMEM((4, rows, features), BF16),
            pltpu.VMEM((4, group_rows, quarter), BF16),
            pltpu.VMEM((2, group_rows, quarter), BF16),
            pltpu.VMEM((group_rows, quarter), BF16),
            pltpu.VMEM((4, rows, features), BF16),
            pltpu.VMEM((2, rows, features), BF16),
            pltpu.VMEM((rows, features), BF16),
        ]
        + [
            pltpu.VMEM((n * group_rows, heads), BF16),
            pltpu.VMEM((n * group_rows, heads), BF16),
            pltpu.VMEM((n * group_rows, quarter), BF16),
            pltpu.VMEM((n, rows, depth), BF16),
            pltpu.VMEM((4, n, rows, depth), BF16),
            pltpu.VMEM((n, rows, depth), BF16),
            pltpu.VMEM((4, n, rows, depth), BF16),
            pltpu.VMEM((4, depth, quarter), F32),
            pltpu.VMEM((n, 8, depth), F32),
            pltpu.VMEM((n, 8, depth), F32),
            pltpu.VMEM((4, 8, depth), F32),
            pltpu.VMEM((group_rows, heads), BF16),
            pltpu.VMEM((rows, features), BF16),
        ],
        compiler_params=params(1),
        name="backward",
    )(
        lengths, x_all, g_all, acts, wg_all, wu_all, wd_all, dwg, dwu, dwd,
        wq_all, wkv_all, wo_all, normed,
        tokens, grad_out, gains_all, query, keyval, context, middle,
    )
    block_out, grad_tokens, grad_gains, grad_wq, grad_wkv, grad_wo, grad_wg, grad_wu, grad_wd = (
        results[:9]
    )
    chunks = 2
    column_block = pl.BlockSpec((depth, n * width // chunks), lambda i: (0, i))
    small = [
        pl.BlockSpec(a.shape, lambda i: (0, 0)) for a in (grad_tokens, grad_wq, grad_wkv, grad_wo, block_out)
    ]
    gain_spec = pl.BlockSpec((1, depth), lambda i: (0, 0))
    (
        grad_wg, grad_wu, grad_wd, grad_tokens, grad_wq, grad_wkv, grad_wo, block_out,
        grad_gain_attn, grad_gain_ffn,
    ) = pl.pallas_call(
        finish_kernel,
        grid=(chunks,),
        out_shape=tuple(shape((depth, n * width), F32) for _ in range(3))
        + tuple(
            shape(a.shape, a.dtype) for a in (grad_tokens, grad_wq, grad_wkv, grad_wo, block_out)
        )
        + (shape((1, depth), F32),) * 2,
        in_specs=[column_block] * 3 + small + [pl.BlockSpec((8, depth), lambda i: (0, 0))],
        out_specs=[column_block] * 3 + small + [gain_spec] * 2,
        compiler_params=pltpu.CompilerParams(vmem_limit_bytes=63 * MIB),
        name="results",
    )(grad_wg, grad_wu, grad_wd, grad_tokens, grad_wq, grad_wkv, grad_wo, block_out, grad_gains)
    return (
        block_out,
        grad_tokens,
        grad_gain_attn.reshape(depth),
        grad_gain_ffn.reshape(depth),
        grad_wq,
        grad_wkv,
        grad_wo,
        grad_wg,
        grad_wu,
        grad_wd,
    )


def solution(mesh):
    rows = P(("dp", "tensor"), None)
    both = P("dp", "tensor")
    return jax.shard_map(
        functools.partial(body, mesh.shape["dp"]),
        mesh=mesh,
        in_specs=(rows, rows, P("dp", None), P("dp"), P("dp"), both, P("dp", None), both, both, both, both),
        out_specs=(rows, rows, P("dp"), P("dp"), both, P("dp", None), both, both, both, both),
        check_vma=False,
    )
```
